32 devices in a mesh: tm: 8 (over y, x, core), gz: 4 (over z).
Axes of the slice: x: 2, y: 2, z: 4, core: 2. Of those that a mesh axis runs over, the one named last changes fastest.
Arguments:
- state_rhs: float32 [32, 128, 2048], P('tm', 'gz'), may hold values from -6 to 6
- adjoint_rhs: float32 [32, 128, 2048], P('tm', 'gz'), may hold values from -6 to 6
- diffusivity: float32 [128, 2048], P('gz'), may hold values from 0.02 to 2
- velocity: float32 [3, 128, 2048], P(None, 'gz'), may hold values from -4 to 4
Outputs:
- state_out: float32 [32, 128, 2048], P('tm', 'gz')
- adjoint_out: float32 [32, 128, 2048], P('tm', 'gz')
The draws below stay inside these ranges and needn't reach their ends.
All inputs are finite; a program needn't handle non-finite values.
Results may differ from the reference program's by a relative error of at most 0.0003.
Values sent between devices are 32-bit elements; how exact they have to be, the bound alone decides.
No kernel may reach another device: no remote copies, remote signals or barrier semaphores. Data moves between devices by JAX's collectives and lax.ppermute only.
A program may use at most 128 MiB of HBM per device.

```python
import math
import jax
import jax.numpy as jnp
from jax import lax

NY = 64
NXY = 2048
NZ = 128
NT = 32


def block_levels(key, extent, shards, least, high):
    level, own = 1.0, jax.random.fold_in(key, 6)
    for position, blocks in shards:
        heights = jnp.exp(jax.random.uniform(jax.random.fold_in(own, position), (blocks,), jnp.float32, least / len(shards), high / len(shards)))
        level = level * jnp.repeat(heights, extent[position] // blocks).reshape([-1 if axis == position else 1 for axis in range(len(extent))])
    return level


def noise(key, extent, scale, bound, cuts=(), kind=jnp.bfloat16):
    level = block_levels(key, extent, cuts, -0.22, 0.18) if cuts else 1.0
    drawn = jax.random.normal(key, extent, jnp.float32) * scale * level
    return jnp.minimum(jnp.maximum(drawn, -bound), bound).astype(kind)


def setup_inputs(seed: int = 0) -> dict:
    key_of = jax.random.split(jax.random.key(seed), 5)
    return {
        "state_rhs": noise(key_of[0], (NT, NZ, NXY), 1.0, 6.0, ((0, 8), (1, 4)), jnp.float32),
        "adjoint_rhs": noise(key_of[1], (NT, NZ, NXY), 1.0, 6.0, ((0, 8), (1, 4)), jnp.float32),
        "diffusivity": jnp.clip(jnp.exp(math.log(2.0) - 4.6051702 * jax.random.uniform(key_of[2], (NZ, NXY), jnp.float32) ** block_levels(key_of[2], (NZ, NXY), ((0, 4),), -0.2, 0.2)), 0.02, 2.0),
        "velocity": noise(key_of[3], (3, NZ, NXY), 0.8, 4.0, ((1, 4),), jnp.float32),
    }


alpha_wrap = 0.1
beta_couple = 0.5
gamma_couple = 0.5


def ahead_flat(field, stride):
    pad_shape = field.shape[:-1] + (stride,)
    return jnp.concatenate([field[..., stride:], jnp.zeros(pad_shape, field.dtype)], axis=-1)


def behind_flat(field, stride):
    pad_shape = field.shape[:-1] + (stride,)
    return jnp.concatenate([jnp.zeros(pad_shape, field.dtype), field[..., :-stride]], axis=-1)


def neighbour_pairs(field, field_pad, width_y):
    column = jnp.arange(field.shape[-1], dtype=jnp.int32) % width_y
    nothing = jnp.zeros((), field.dtype)
    y_ahead = jnp.where(column == width_y - 1, nothing, ahead_flat(field, 1))
    y_behind = jnp.where(column == 0, nothing, behind_flat(field, 1))
    return [(field_pad[..., 2:, :], field_pad[..., :-2, :]),
            (ahead_flat(field, width_y), behind_flat(field, width_y)),
            (y_ahead, y_behind)]


def face_weights(kappa, kappa_pad, width_y):
    pairs = neighbour_pairs(kappa, kappa_pad, width_y)
    weights = []
    diagonal = jnp.zeros_like(kappa)
    for ahead, behind in pairs:
        face_ahead = jnp.where(ahead > 0.0, 0.5 * (kappa + ahead), kappa)
        face_behind = jnp.where(behind > 0.0, 0.5 * (kappa + behind), kappa)
        weights.append((face_ahead, face_behind))
        diagonal = diagonal + face_ahead + face_behind
    return weights, diagonal


def coupling(field, field_pad, weights, velocity, width_y):
    sign = jnp.array([1.0, -1.0, 1.0, -1.0], field.dtype).reshape((4,) + (1,) * (field.ndim - 1))
    pairs = neighbour_pairs(field, field_pad, width_y)
    speeds = [velocity[2], velocity[0], velocity[1]]
    total = jnp.zeros_like(field)
    for index in range(3):
        ahead, behind = pairs[index]
        face_ahead, face_behind = weights[index]
        total = total + face_ahead * ahead + face_behind * behind - sign * (0.5 * speeds[index]) * (ahead - behind)
    return total


def apply_inverse(stacked, lam_real, lam_imag, diagonal):
    shifted = lam_real + diagonal
    determinant = shifted * shifted + lam_imag * lam_imag + beta_couple * gamma_couple
    state_real, adjoint_real, state_imag, adjoint_imag = stacked[0], stacked[1], stacked[2], stacked[3]
    out_state_real = (shifted * state_real + lam_imag * state_imag + beta_couple * adjoint_real) / determinant
    out_state_imag = (shifted * state_imag - lam_imag * state_real + beta_couple * adjoint_imag) / determinant
    out_adjoint_real = (shifted * adjoint_real - lam_imag * adjoint_imag - gamma_couple * state_real) / determinant
    out_adjoint_imag = (shifted * adjoint_imag + lam_imag * adjoint_real - gamma_couple * state_imag) / determinant
    return jnp.stack([out_state_real, out_adjoint_real, out_state_imag, out_adjoint_imag])


def reference(state_rhs, adjoint_rhs, diffusivity, velocity):
    moments = jnp.arange(NT, dtype=jnp.float32)
    damping = jnp.power(jnp.asarray(alpha_wrap, jnp.float32), moments / NT)
    fields = jnp.stack([state_rhs, adjoint_rhs]) * damping[None, :, None, None]
    spectrum = jnp.fft.fft(fields, axis=1)
    spec_real = jnp.moveaxis(jnp.real(spectrum), 1, 0)
    spec_imag = jnp.moveaxis(jnp.imag(spectrum), 1, 0)
    angle = moments * (2.0 * math.pi / NT)
    ratio = alpha_wrap ** (1.0 / NT)
    lam_real = 1.0 - ratio * jnp.cos(angle)
    lam_imag = ratio * jnp.sin(angle)
    kappa_pad = jnp.pad(diffusivity, ((1, 1), (0, 0)))
    weights, diagonal = face_weights(diffusivity, kappa_pad, NY)

    def solve_one(item):
        part_real, part_imag, one_real, one_imag = item
        stacked = jnp.concatenate([part_real, part_imag])
        first = apply_inverse(stacked, one_real, one_imag, diagonal)
        first_pad = jnp.pad(first, ((0, 0), (1, 1), (0, 0)))
        return apply_inverse(stacked + coupling(first, first_pad, weights, velocity, NY), one_real, one_imag, diagonal)

    solved = lax.map(solve_one, (spec_real, spec_imag, lam_real, lam_imag))
    combined = solved[:, :2] + 1j * solved[:, 2:]
    back = jnp.real(jnp.fft.ifft(combined, axis=0))
    undo = jnp.power(jnp.asarray(alpha_wrap, jnp.float32), -moments / NT)
    result = back * undo[:, None, None, None]
    return result[:, 0], result[:, 1]
```

```python
import functools
import math

import jax
import jax.numpy as jnp
from jax import lax
from jax.experimental import pallas as pl
from jax.experimental.pallas import tpu as pltpu
from jax.sharding import PartitionSpec as P

NY = 64
LANES = 128

alpha_wrap = 0.1
beta_couple = 0.5
gamma_couple = 0.5


def this_core():
    return lax.rem(lax.axis_index("tm"), 2)


def this_chip():
    return lax.div(lax.axis_index("tm"), 2)


def lane_block(start):
    return pl.ds(pl.multiple_of(start, LANES), LANES)


def power(value, count):
    result = None
    while count:
        if count & 1:
            result = value if result is None else result * value
        count >>= 1
        if count:
            value = value * value
    return result


def step_scale(ratio, steps, chips, sign):
    chip = this_chip()
    base = jnp.float32(1.0)
    bit = 0
    while 1 << bit < chips:
        factor = ratio ** (sign * steps * (1 << bit))
        base = base * jnp.where(lax.rem(lax.div(chip, 1 << bit), 2) == 1, factor, 1.0)
        bit += 1
    return [base * (ratio ** (sign * step)) for step in range(steps)]


def side_values(field, left, right, before, after):
    rows = field.shape[0]
    lane = lax.broadcasted_iota(jnp.int32, field.shape, 1)
    row = lax.broadcasted_iota(jnp.int32, field.shape, 0)
    z_ahead = jnp.where(row == rows - 1, after, pltpu.roll(field, rows - 1, 0))
    z_behind = jnp.where(row == 0, before, pltpu.roll(field, 1, 0))
    turned = pltpu.roll(field, NY, 1)
    x_ahead = jnp.where(lane < NY, turned, pltpu.roll(right, NY, 1))
    x_behind = jnp.where(lane < NY, pltpu.roll(left, NY, 1), turned)
    y_ahead = pltpu.roll(field, LANES - 1, 1)
    y_behind = pltpu.roll(field, 1, 1)
    return ((z_ahead, z_behind), (x_ahead, x_behind), (y_ahead, y_behind))


def faces(kappa_ref, outer_ref, group, half):
    core = this_core()
    groups = kappa_ref.shape[1] // LANES
    own = pl.ds(pl.multiple_of(core * half, 8), half)
    here = lane_block(group * LANES)
    kappa = kappa_ref[own, here]
    left = kappa_ref[own, lane_block(jnp.maximum(group - 1, 0) * LANES)]
    right = kappa_ref[own, lane_block(jnp.minimum(group + 1, groups - 1) * LANES)]
    outer = outer_ref[0:1, here]
    before = jnp.where(core == 0, outer, kappa_ref[half - 1 : half, here])
    after = jnp.where(core == 0, kappa_ref[half : half + 1, here], outer)
    pairs = side_values(kappa, left, right, before, after)
    lane = lax.broadcasted_iota(jnp.int32, kappa.shape, 1)
    column = lax.rem(lane, NY)
    inside = (
        (pairs[0][0] > 0.0, pairs[0][1] > 0.0),
        (
            jnp.logical_or(lane < NY, group < groups - 1),
            jnp.logical_or(lane >= NY, group > 0),
        ),
        (column < NY - 1, column > 0),
    )
    weights = [
        [jnp.where(ok, 0.5 * (kappa + value), kappa) for ok, value in zip(oks, values)]
        for oks, values in zip(inside, pairs)
    ]
    return weights, inside


def cell_factors(diagonal, ratio):
    shifted = 1.0 + diagonal
    lifted = shifted * shifted - (ratio * ratio + beta_couple * gamma_couple)
    mix = shifted / (lifted + jnp.sqrt(lifted * lifted + shifted * shifted))
    inverse = 1.0 / (shifted + 0.5 * mix)
    return ratio * inverse, inverse, mix * inverse, 1.0 / shifted


def ordered(own, other, step, steps_local):
    mine = this_core() == step // steps_local
    index = step % steps_local
    return jnp.where(mine, own(index), other(index))


def local_ends(values, decay, inverse, mixed, upright, steps):
    back = None
    last = None
    weight = None
    for step in reversed(range(steps)):
        state, adjoint = values(step)
        drive = inverse * adjoint - mixed * state
        back = drive if back is None else decay * back + drive
        term = state + 0.5 * back
        last = term if last is None else last + weight * term
        weight = decay if weight is None else weight * decay
    return back, last * upright


def solve_steps(values, decay, inverse, mixed, upright, ratio, back_in, state_in, steps, put):
    backs = [None] * steps
    back = back_in
    for step in reversed(range(steps)):
        state, adjoint = values(step)
        back = decay * back + (inverse * adjoint - mixed * state)
        backs[step] = back
    gain = ratio * mixed
    half_up = 0.5 * upright
    previous = state_in
    for step in range(steps):
        state, _ = values(step)
        current = decay * previous + (upright * state + half_up * backs[step])
        put(step, current, backs[step] - gain * previous)
        previous = current


def first_kernel(ratio, steps_local, chips, own_s, own_a, other_s, other_a, kappa_ref, outer_ref, factor_ref, near_ref, far_ref):
    steps = 2 * steps_local
    half = own_s.shape[1]
    tile = half // 2
    groups = own_s.shape[2] // LANES
    scales = step_scale(ratio, steps, chips, 1)

    def one(index, carry):
        here = lane_block(index * LANES)
        weights, _ = faces(kappa_ref, outer_ref, pl.program_id(0) * groups + index, half)
        diagonal = weights[0][0] + weights[0][1]
        diagonal = diagonal + weights[1][0] + weights[1][1]
        diagonal = diagonal + weights[2][0] + weights[2][1]
        decay, inverse, mixed, upright = cell_factors(diagonal, ratio)
        for slot, value in enumerate((decay, inverse, mixed, upright)):
            factor_ref[slot, :, here] = value

        def values(step):
            return (
                ordered(lambda i: own_s[i, :, here], lambda i: other_s[i, :, here], step, steps_local) * scales[step],
                ordered(lambda i: own_a[i, :, here], lambda i: other_a[i, :, here], step, steps_local) * scales[step],
            )

        back, last = local_ends(values, decay, inverse, mixed, upright, steps)
        near_ref[0, :, here] = back[:tile]
        near_ref[1, :, here] = last[:tile]
        far_ref[0, :, here] = back[tile:]
        far_ref[1, :, here] = last[tile:]
        return carry

    lax.fori_loop(0, groups, one, 0)


def ring_factors(factors, steps, chips):
    decay, _, _, upright = factors
    block = power(decay, steps)
    square = decay * decay
    response = (0.5 * upright) * decay * (1.0 - block * block) / (1.0 - square)
    closing = 1.0 / (1.0 - power(block, chips))
    return block, response, closing


def contribution(ends, offset, block, response, closing):
    back, last = ends
    square = block * block
    if offset == 0:
        up, down, cross = square * block, square * block, 1.0 + square + square * square * (1.0 + square)
    elif offset == 1:
        up, down, cross = None, square, block * (1.0 + square) * (1.0 + square)
    elif offset == 2:
        up, down, cross = block, block, 2.0 * square * (1.0 + square)
    else:
        up, down, cross = square, None, block * (1.0 + square) * (1.0 + square)
    entering_back = back if up is None else up * back
    entering_state = last if down is None else down * last
    entering_state = entering_state + (cross * response * closing) * back
    return closing * entering_back, closing * entering_state


def either(flag, one, other):
    return tuple(jnp.where(flag, a, b) for a, b in zip(one, other))


def relay_kernel(steps, factor_ref, near_ref, near_in, far_ref, far_in, near_out, far_out):
    tile, cells = near_ref.shape[1:]
    odd = lax.rem(this_chip(), 2) == 1

    def one(index, carry):
        here = lane_block(index * LANES)
        for rows, mine, theirs, out, first in (
            (slice(0, tile), near_ref, near_in, near_out, True),
            (slice(tile, 2 * tile), far_ref, far_in, far_out, False),
        ):
            factors = [factor_ref[slot, rows, here] for slot in range(4)]
            ring = ring_factors(factors, steps, 4)
            a = (mine[0, :, here], mine[1, :, here])
            b = (theirs[0, :, here], theirs[1, :, here])
            if first:
                one_part = contribution(a, 2, *ring)
                other_part = either(odd, contribution(b, 1, *ring), contribution(b, 3, *ring))
            else:
                one_part = either(odd, contribution(a, 1, *ring), contribution(a, 3, *ring))
                other_part = either(odd, contribution(b, 3, *ring), contribution(b, 1, *ring))
            out[0, :, here] = one_part[0] + other_part[0]
            out[1, :, here] = one_part[1] + other_part[1]
        return carry

    lax.fori_loop(0, cells // LANES, one, 0)


def entering(factors, near, near_in, near_tail, far, far_in, far_tail, here, tile, steps):
    odd = lax.rem(this_chip(), 2) == 1
    backs, states = [], []
    for rows, mine, theirs, tail, first in (
        (slice(0, tile), near, near_in, near_tail, True),
        (slice(tile, 2 * tile), far, far_in, far_tail, False),
    ):
        ring = ring_factors([f[rows] for f in factors], steps, 4)
        a = (mine[0, :, here], mine[1, :, here])
        b = (theirs[0, :, here], theirs[1, :, here])
        own = contribution(a, 0, *ring)
        if first:
            near_by = either(odd, contribution(b, 3, *ring), contribution(b, 1, *ring))
        else:
            near_by = contribution(b, 2, *ring)
        backs.append(own[0] + near_by[0] + tail[0, :, here])
        states.append(own[1] + near_by[1] + tail[1, :, here])
    return jnp.concatenate(backs, axis=0), jnp.concatenate(states, axis=0)


def sweep_kernel(ratio, steps_local, chips, own_s, own_a, other_s, other_a, factor_ref, *rest):
    *ends, first_ref, edge_ref, inner_ref = rest
    steps = 2 * steps_local
    half = own_s.shape[1]
    groups = own_s.shape[2] // LANES
    scales = step_scale(ratio, steps, chips, 1)
    core = this_core()

    def one(index, carry):
        here = lane_block(index * LANES)
        factors = [factor_ref[slot, :, here] for slot in range(4)]

        def values(step):
            return (
                ordered(lambda i: own_s[i, :, here], lambda i: other_s[i, :, here], step, steps_local) * scales[step],
                ordered(lambda i: own_a[i, :, here], lambda i: other_a[i, :, here], step, steps_local) * scales[step],
            )

        back_in, state_in = enter_values(ends, factors, here, half, steps)

        def put(step, state, adjoint):
            for field, value in enumerate((state, adjoint)):
                slot = 2 * step + field
                first_ref[slot, :, here] = value
                head, tail = value[0:1], value[half - 1 : half]
                edge_ref[slot : slot + 1, here] = jnp.where(core == 0, head, tail)
                inner_ref[slot : slot + 1, here] = jnp.where(core == 0, tail, head)

        solve_steps(values, *factors, ratio, back_in, state_in, steps, put)
        return carry

    lax.fori_loop(0, groups, one, 0)


def enter_values(ends, factors, here, half, steps):
    if len(ends) == 1:
        return ends[0][0, :, here], ends[0][1, :, here]
    return entering(factors, *ends, here, half // 2, steps)


def coupling_kernel(ratio, steps, first_ref, outer_ref, inner_ref, kappa_ref, outer_kappa, velocity_ref, factor_ref, coupled_ref, near_ref, far_ref):
    half = first_ref.shape[1]
    tile = half // 2
    groups = coupled_ref.shape[2] // LANES
    total = first_ref.shape[2] // LANES
    core = this_core()

    def one(index, carry):
        here = lane_block(index * LANES)
        group = pl.program_id(0) * groups + index
        there = lane_block(group * LANES)
        left = lane_block(jnp.maximum(group - 1, 0) * LANES)
        right = lane_block(jnp.minimum(group + 1, total - 1) * LANES)
        weights, inside = faces(kappa_ref, outer_kappa, group, half)
        own = pl.ds(pl.multiple_of(core * half, 8), half)
        tables = ([], [])
        for direction, component in enumerate((2, 0, 1)):
            drift = 0.5 * velocity_ref[component, :, here]
            ahead, behind = weights[direction]
            ok_ahead, ok_behind = inside[direction]
            for field, sign in enumerate((1.0, -1.0)):
                tables[field].append(
                    (
                        jnp.where(ok_ahead, ahead - sign * drift, 0.0),
                        jnp.where(ok_behind, behind + sign * drift, 0.0),
                    )
                )
        decay, inverse, mixed, upright = [factor_ref[slot, :, here] for slot in range(4)]

        def values(step):
            results = []
            for field in range(2):
                slot = 2 * step + field
                outer = outer_ref[slot : slot + 1, there]
                inner = inner_ref[slot : slot + 1, there]
                before = jnp.where(core == 0, outer, inner)
                after = jnp.where(core == 0, inner, outer)
                pairs = side_values(first_ref[slot, :, there], first_ref[slot, :, left], first_ref[slot, :, right], before, after)
                result = None
                for (ahead, behind), (c_ahead, c_behind) in zip(pairs, tables[field]):
                    term = c_ahead * ahead + c_behind * behind
                    result = term if result is None else result + term
                coupled_ref[slot, :, here] = result
                results.append(result)
            return results

        back, last = local_ends(values, decay, inverse, mixed, upright, steps)
        near_ref[0, :, here] = back[:tile]
        near_ref[1, :, here] = last[:tile]
        far_ref[0, :, here] = back[tile:]
        far_ref[1, :, here] = last[tile:]
        return carry

    lax.fori_loop(0, groups, one, 0)


def last_kernel(ratio, steps_local, chips, coupled_ref, first_ref, factor_ref, *rest):
    *ends, keep_ref, send_ref = rest
    steps = 2 * steps_local
    half = first_ref.shape[1]
    groups = first_ref.shape[2] // LANES
    scales = step_scale(ratio, steps, chips, -1)
    core = this_core()

    def one(index, carry):
        here = lane_block(index * LANES)
        factors = [factor_ref[slot, :, here] for slot in range(4)]

        def values(step):
            return coupled_ref[2 * step, :, here], coupled_ref[2 * step + 1, :, here]

        back_in, state_in = enter_values(ends, factors, here, half, steps)
        pending = {}

        def put(step, state, adjoint):
            for field, value in enumerate((state, adjoint)):
                done = (first_ref[2 * step + field, :, here] + value) * scales[step]
                if step < steps_local:
                    pending[step, field] = done
                else:
                    early = pending[step - steps_local, field]
                    slot = step - steps_local
                    keep_ref[field, slot, :, here] = jnp.where(core == 0, early, done)
                    send_ref[field, slot, :, here] = jnp.where(core == 0, done, early)

        solve_steps(values, *factors, ratio, back_in, state_in, steps, put)
        return carry

    lax.fori_loop(0, groups, one, 0)


def body(state_rhs, adjoint_rhs, diffusivity, velocity):
    steps_local, depth, cells = state_rhs.shape
    ranks = lax.axis_size("tm")
    slabs = lax.axis_size("gz")
    chips = ranks // 2
    total = steps_local * ranks
    steps = 2 * steps_local
    half = depth // 2
    tile = half // 2
    ratio = alpha_wrap ** (1.0 / total)
    core = this_core()
    f32 = jnp.float32

    def partner(value, mask):
        return lax.ppermute(value, "tm", [(i, i ^ mask) for i in range(ranks)])

    outward = []
    for t in range(ranks):
        for g in range(slabs):
            to = g - 1 if t % 2 == 0 else g + 1
            if 0 <= to < slabs:
                outward.append((t * slabs + g, (t ^ 1) * slabs + to))

    def across(value):
        return lax.ppermute(value, ("tm", "gz"), outward)

    other_s = partner(state_rhs, 1)
    other_a = partner(adjoint_rhs, 1)
    outer_kappa = across(jnp.where(core == 0, diffusivity[:1], diffusivity[depth - 1 :]))

    width = 512
    blocks = cells // width
    raw = pl.BlockSpec((steps_local, half, width), lambda i: (0, this_core(), i))
    whole = lambda *shape: pl.BlockSpec(shape, lambda i: (0,) * len(shape))
    strip = lambda *shape: pl.BlockSpec(shape + (width,), lambda i: (0,) * len(shape) + (i,))
    params = pltpu.CompilerParams(vmem_limit_bytes=48 * 1024 * 1024)
    shape = lambda *s: jax.ShapeDtypeStruct(s, f32)
    ends_shape = [shape(2, tile, cells)] * 2
    ends_spec = [strip(2, tile)] * 2

    factors, near, far = pl.pallas_call(
        functools.partial(first_kernel, ratio, steps_local, chips),
        grid=(blocks,),
        in_specs=[raw] * 4 + [whole(depth, cells), whole(1, cells)],
        out_specs=[strip(4, half)] + ends_spec,
        out_shape=[shape(4, half, cells)] + ends_shape,
        compiler_params=params,
        name="ends_of_first",
    )(state_rhs, adjoint_rhs, other_s, other_a, diffusivity, outer_kappa)

    def exchange(near, far):
        if chips != 4:
            gathered = lax.all_gather(jnp.concatenate([near, far], axis=1), "tm")
            gathered = lax.dynamic_index_in_dim(
                gathered.reshape((chips, 2) + gathered.shape[1:]), core, 1, keepdims=False
            )
            block, response, closing = ring_factors([factors[i] for i in range(4)], steps, chips)
            at = lambda array, index: lax.dynamic_index_in_dim(array, lax.rem(index + 2 * chips, chips), 0, keepdims=False)
            chip = this_chip()

            def entering_back(where):
                value = jnp.zeros((half, cells), f32)
                for offset in reversed(range(chips)):
                    value = block * value + at(gathered[:, 0], where + 1 + offset)
                return value * closing

            value = jnp.zeros((half, cells), f32)
            for offset in reversed(range(chips)):
                source = chip - 1 - offset
                value = block * value + at(gathered[:, 1], source) + response * entering_back(source)
            return [jnp.stack([entering_back(chip), value * closing])]
        near_in, far_in = partner(near, 2), partner(far, 4)
        near_out, far_out = pl.pallas_call(
            functools.partial(relay_kernel, steps),
            out_shape=ends_shape,
            compiler_params=params,
            name="relay",
        )(factors, near, near_in, far, far_in)
        return [near, near_in, partner(near_out, 4), far, far_in, partner(far_out, 2)]

    def end_specs(ends):
        return [strip(*end.shape[:-1]) for end in ends]

    ends = exchange(near, far)
    first, edge, inner_edge = pl.pallas_call(
        functools.partial(sweep_kernel, ratio, steps_local, chips),
        grid=(blocks,),
        in_specs=[raw] * 4 + [strip(4, half)] + end_specs(ends),
        out_specs=[strip(2 * steps, half), strip(2 * steps), strip(2 * steps)],
        out_shape=[shape(2 * steps, half, cells), shape(2 * steps, cells), shape(2 * steps, cells)],
        compiler_params=params,
        name="first_sweep",
    )(state_rhs, adjoint_rhs, other_s, other_a, factors, *ends)

    outer = across(edge)
    inner = partner(inner_edge, 1)
    coupled, near, far = pl.pallas_call(
        functools.partial(coupling_kernel, ratio, steps),
        grid=(blocks,),
        in_specs=[
            whole(2 * steps, half, cells),
            whole(2 * steps, cells),
            whole(2 * steps, cells),
            whole(depth, cells),
            whole(1, cells),
            pl.BlockSpec((3, half, width), lambda i: (0, this_core(), i)),
            strip(4, half),
        ],
        out_specs=[strip(2 * steps, half)] + ends_spec,
        out_shape=[shape(2 * steps, half, cells)] + ends_shape,
        compiler_params=params,
        name="couplings",
    )(first, outer, inner, diffusivity, outer_kappa, velocity, factors)

    ends = exchange(near, far)
    keep, send = pl.pallas_call(
        functools.partial(last_kernel, ratio, steps_local, chips),
        grid=(blocks,),
        in_specs=[strip(2 * steps, half)] * 2 + [strip(4, half)] + end_specs(ends),
        out_specs=[strip(2, steps_local, half)] * 2,
        out_shape=[shape(2, steps_local, half, cells)] * 2,
        compiler_params=params,
        name="second_sweep",
    )(coupled, first, factors, *ends)

    received = partner(send, 1)
    upper = jnp.where(core == 0, keep, received)
    lower = jnp.where(core == 0, received, keep)
    result = jnp.concatenate([upper, lower], axis=2)
    return result[0], result[1]


def solution(mesh):
    placed = (P("tm", "gz", None), P("tm", "gz", None), P("gz", None), P(None, "gz", None))
    return jax.shard_map(
        body,
        mesh=mesh,
        in_specs=placed,
        out_specs=(P("tm", "gz", None), P("tm", "gz", None)),
        check_vma=False,
    )
```

```python
import functools
import math

import jax
import jax.numpy as jnp
from jax import lax
from jax.experimental import pallas as pl
from jax.experimental.pallas import tpu as pltpu
from jax.sharding import PartitionSpec as P

NY = 64
LANES = 128

alpha_wrap = 0.1
beta_couple = 0.5
gamma_couple = 0.5


def this_core():
    return lax.rem(lax.axis_index("tm"), 2)


def this_chip():
    return lax.div(lax.axis_index("tm"), 2)


def lane_block(start):
    return pl.ds(pl.multiple_of(start, LANES), LANES)


def power(value, count):
    result = None
    while count:
        if count & 1:
            result = value if result is None else result * value
        count >>= 1
        if count:
            value = value * value
    return result


def step_scale(ratio, steps, chips, sign):
    chip = this_chip()
    base = jnp.float32(1.0)
    bit = 0
    while 1 << bit < chips:
        factor = ratio ** (sign * steps * (1 << bit))
        base = base * jnp.where(lax.rem(lax.div(chip, 1 << bit), 2) == 1, factor, 1.0)
        bit += 1
    return [base * (ratio ** (sign * step)) for step in range(steps)]


def side_values(field, left, right, before, after):
    rows = field.shape[0]
    lane = lax.broadcasted_iota(jnp.int32, field.shape, 1)
    row = lax.broadcasted_iota(jnp.int32, field.shape, 0)
    z_ahead = jnp.where(row == rows - 1, after, pltpu.roll(field, rows - 1, 0))
    z_behind = jnp.where(row == 0, before, pltpu.roll(field, 1, 0))
    turned = pltpu.roll(field, NY, 1)
    x_ahead = jnp.where(lane < NY, turned, pltpu.roll(right, NY, 1))
    x_behind = jnp.where(lane < NY, pltpu.roll(left, NY, 1), turned)
    y_ahead = pltpu.roll(field, LANES - 1, 1)
    y_behind = pltpu.roll(field, 1, 1)
    return ((z_ahead, z_behind), (x_ahead, x_behind), (y_ahead, y_behind))


def faces(kappa_ref, outer, group, half):
    core = this_core()
    groups = kappa_ref.shape[1] // LANES
    own = pl.ds(pl.multiple_of(core * half, 8), half)
    here = lane_block(group * LANES)
    kappa = kappa_ref[own, here]
    left = kappa_ref[own, lane_block(jnp.maximum(group - 1, 0) * LANES)]
    right = kappa_ref[own, lane_block(jnp.minimum(group + 1, groups - 1) * LANES)]
    before = jnp.where(core == 0, outer, kappa_ref[half - 1 : half, here])
    after = jnp.where(core == 0, kappa_ref[half : half + 1, here], outer)
    pairs = side_values(kappa, left, right, before, after)
    lane = lax.broadcasted_iota(jnp.int32, kappa.shape, 1)
    column = lax.rem(lane, NY)
    inside = (
        (pairs[0][0] > 0.0, pairs[0][1] > 0.0),
        (
            jnp.logical_or(lane < NY, group < groups - 1),
            jnp.logical_or(lane >= NY, group > 0),
        ),
        (column < NY - 1, column > 0),
    )
    weights = [
        [jnp.where(ok, 0.5 * (kappa + value), kappa) for ok, value in zip(oks, values)]
        for oks, values in zip(inside, pairs)
    ]
    return weights, inside


def total_weight(weights):
    diagonal = weights[0][0] + weights[0][1]
    diagonal = diagonal + weights[1][0] + weights[1][1]
    return diagonal + weights[2][0] + weights[2][1]


def layer_diagonal(kappa, ahead, behind):
    rows = kappa.shape[0]
    lane = lax.broadcasted_iota(jnp.int32, kappa.shape, 1)
    row = lax.broadcasted_iota(jnp.int32, kappa.shape, 0)
    column = lax.rem(lane, NY)
    turned = pltpu.roll(kappa, NY, 1)
    x_ahead = jnp.where(lane < NY, turned, pltpu.roll(turned, rows - 1, 0))
    x_behind = jnp.where(lane < NY, pltpu.roll(turned, 1, 0), turned)
    pairs = (
        (ahead, ahead > 0.0),
        (behind, behind > 0.0),
        (x_ahead, jnp.logical_or(lane < NY, row < rows - 1)),
        (x_behind, jnp.logical_or(lane >= NY, row > 0)),
        (pltpu.roll(kappa, LANES - 1, 1), column < NY - 1),
        (pltpu.roll(kappa, 1, 1), column > 0),
    )
    total = None
    for value, ok in pairs:
        weight = jnp.where(ok, 0.5 * (kappa + value), kappa)
        total = weight if total is None else total + weight
    return total


def cell_factors(diagonal, ratio):
    shifted = 1.0 + diagonal
    lifted = shifted * shifted - (ratio * ratio + beta_couple * gamma_couple)
    mix = shifted / (lifted + jnp.sqrt(lifted * lifted + shifted * shifted))
    inverse = 1.0 / (shifted + 0.5 * mix)
    return ratio * inverse, inverse, mix * inverse, 1.0 / shifted


def local_ends(values, decay, inverse, mixed, upright, steps):
    back = None
    last = None
    weight = None
    for step in reversed(range(steps)):
        state, adjoint = values(step)
        drive = inverse * adjoint - mixed * state
        back = drive if back is None else decay * back + drive
        term = state + 0.5 * back
        last = term if last is None else last + weight * term
        weight = decay if weight is None else weight * decay
    return back, last * upright


def solve_steps(values, decay, inverse, mixed, upright, ratio, back_in, state_in, steps, put):
    backs = [None] * steps
    back = back_in
    for step in reversed(range(steps)):
        state, adjoint = values(step)
        drive = inverse * adjoint - mixed * state
        back = drive if back is None else decay * back + drive
        backs[step] = back
    gain = ratio * mixed
    half_up = 0.5 * upright
    previous = state_in
    for step in range(steps):
        state, _ = values(step)
        current = upright * state + half_up * backs[step]
        adjoint = backs[step]
        if previous is not None:
            current = current + decay * previous
            adjoint = adjoint - gain * previous
        put(step, current, adjoint)
        previous = current
    return backs[0], previous


def pack_kernel(state, adjoint, kappa, keep, send, slab, outer_cross, outer_straight, inner_keep, inner_send, layers, sems):
    steps_local = state.shape[0]
    half = keep.shape[2]
    core = this_core()
    mine = pl.ds(pl.multiple_of(core * half, 8), half)
    others = pl.ds(pl.multiple_of((1 - core) * half, 8), half)
    copies = [pltpu.make_async_copy(kappa, slab, sems.at[4])]
    for field, source in enumerate((state, adjoint)):
        copies.append(pltpu.make_async_copy(source.at[:, mine, :], keep.at[field], sems.at[2 * field]))
        copies.append(pltpu.make_async_copy(source.at[:, others, :], send.at[field], sems.at[2 * field + 1]))
    for copy in copies:
        copy.start()

    def lay(source, rows, target):
        for group in range(target.shape[0]):
            lanes = slice(group * LANES, (group + 1) * LANES)
            one, other = [source[row : row + 1, lanes] for row in rows]
            target[group : group + 1, :] = jnp.where(core == 0, one, other)

    copies[0].wait()
    last = 2 * half - 1
    lay(slab, (0, last), outer_cross.at[2 * steps_local])
    lay(slab, (1, last - 1), outer_cross.at[2 * steps_local + 1])
    for slot, row in enumerate((0, half - 1, half, half + 1)):
        lay(slab, (row, last - row), layers.at[slot])
    for copy in copies[1:]:
        copy.wait()
    near, far = (0, half - 1), (half - 1, 0)
    for index in range(steps_local):
        for field in range(2):
            slot = 2 * index + field
            lay(keep.at[field, index], near, outer_cross.at[slot])
            lay(send.at[field, index], far, outer_straight.at[slot])
            lay(send.at[field, index], near, inner_keep.at[slot])
            lay(keep.at[field, index], far, inner_send.at[slot])


def ends_kernel(ratio, chips, keep, other, slab, cross, straight, inner_keep, inner_other, layers, raw_ref, factor_ref, near_ref, far_ref):
    steps_local, half, cells = keep.shape[1:]
    steps = 2 * steps_local
    tile = half // 2
    groups = cells // LANES
    core = this_core()
    scales = step_scale(ratio, steps, chips, 1)

    def order(position, index):
        sub = core if position == 0 else 1 - core
        return sub * steps + 2 * index, jnp.where(sub == 0, scales[index], scales[steps_local + index])

    def set_factors(diagonal, here):
        for slot, value in enumerate(cell_factors(diagonal, ratio)):
            factor_ref[slot, :, here] = value

    def prepare(group, carry):
        here = lane_block(group * LANES)
        weights, _ = faces(slab, cross[steps, pl.ds(group, 1), :], group, half)
        set_factors(total_weight(weights), here)
        for position, source in enumerate((keep, other)):
            for index in range(steps_local):
                slot, scale = order(position, index)
                for field in range(2):
                    raw_ref[slot + field, :, here] = source[field, index, :, here] * scale
        return carry

    lax.fori_loop(0, groups, prepare, 0)
    outer, inner = slice(cells, cells + LANES), slice(cells + LANES, cells + 2 * LANES)
    set_factors(layer_diagonal(cross[steps], layers[0], cross[steps + 1]), outer)
    set_factors(layer_diagonal(layers[2], layers[1], layers[3]), inner)
    for sources, here in (((straight, cross), outer), ((inner_keep, inner_other), inner)):
        for position, source in enumerate(sources):
            for index in range(steps_local):
                slot, scale = order(position, index)
                for field in range(2):
                    raw_ref[slot + field, :, here] = source[2 * index + field] * scale

    def one(group, carry):
        here = lane_block(group * LANES)
        factors = [factor_ref[slot, :, here] for slot in range(4)]
        values = lambda step: (raw_ref[2 * step, :, here], raw_ref[2 * step + 1, :, here])
        put_ends(local_ends(values, *factors, steps), near_ref, far_ref, here, tile)
        return carry

    lax.fori_loop(0, groups + 2, one, 0)


def put_ends(ends, near_ref, far_ref, here, tile):
    for slot, value in enumerate(ends):
        near_ref[slot, :, here] = value[:tile]
        far_ref[slot, :, here] = value[tile:]


def power_sum(value, count):
    total = None
    for _ in range(count):
        total = 1.0 if total is None else 1.0 + value * total
    return total


def response_of(decay, upright, steps):
    return (0.5 * upright) * decay * power_sum(decay * decay, steps)


def ring_factors(factors, steps, chips):
    decay, _, _, upright = factors
    block = power(decay, steps)
    return block, response_of(decay, upright, steps), 1.0 / (1.0 - power(block, chips))


def contribution(ends, offset, block, response, closing):
    back, last = ends
    square = block * block
    if offset == 0:
        up, down, cross = square * block, square * block, 1.0 + square + square * square * (1.0 + square)
    elif offset == 1:
        up, down, cross = None, square, block * (1.0 + square) * (1.0 + square)
    elif offset == 2:
        up, down, cross = block, block, 2.0 * square * (1.0 + square)
    else:
        up, down, cross = square, None, block * (1.0 + square) * (1.0 + square)
    entering_back = back if up is None else up * back
    entering_state = last if down is None else down * last
    entering_state = entering_state + (cross * response * closing) * back
    return closing * entering_back, closing * entering_state


def either(flag, one, other):
    return tuple(jnp.where(flag, a, b) for a, b in zip(one, other))


def relay_kernel(steps, factor_ref, near_ref, near_in, far_ref, far_in, near_out, far_out):
    tile, cells = near_ref.shape[1:]
    odd = lax.rem(this_chip(), 2) == 1

    def one(index, carry):
        here = lane_block(index * LANES)
        for rows, mine, theirs, out, first in (
            (slice(0, tile), near_ref, near_in, near_out, True),
            (slice(tile, 2 * tile), far_ref, far_in, far_out, False),
        ):
            factors = [factor_ref[slot, rows, here] for slot in range(4)]
            ring = ring_factors(factors, steps, 4)
            a = (mine[0, :, here], mine[1, :, here])
            b = (theirs[0, :, here], theirs[1, :, here])
            if first:
                one_part = contribution(a, 2, *ring)
                other_part = either(odd, contribution(b, 1, *ring), contribution(b, 3, *ring))
            else:
                one_part = either(odd, contribution(a, 1, *ring), contribution(a, 3, *ring))
                other_part = either(odd, contribution(b, 3, *ring), contribution(b, 1, *ring))
            out[0, :, here] = one_part[0] + other_part[0]
            out[1, :, here] = one_part[1] + other_part[1]
        return carry

    lax.fori_loop(0, cells // LANES, one, 0)


def entering(factors, near, near_in, near_tail, far, far_in, far_tail, here, tile, steps):
    odd = lax.rem(this_chip(), 2) == 1
    backs, states = [], []
    for rows, mine, theirs, tail, first in (
        (slice(0, tile), near, near_in, near_tail, True),
        (slice(tile, 2 * tile), far, far_in, far_tail, False),
    ):
        ring = ring_factors([f[rows] for f in factors], steps, 4)
        a = (mine[0, :, here], mine[1, :, here])
        b = (theirs[0, :, here], theirs[1, :, here])
        own = contribution(a, 0, *ring)
        if first:
            near_by = either(odd, contribution(b, 3, *ring), contribution(b, 1, *ring))
        else:
            near_by = contribution(b, 2, *ring)
        backs.append(own[0] + near_by[0] + tail[0, :, here])
        states.append(own[1] + near_by[1] + tail[1, :, here])
    return jnp.concatenate(backs, axis=0), jnp.concatenate(states, axis=0)


def enter_values(ends, factors, here, half, steps):
    if len(ends) == 1:
        return ends[0][0, :, here], ends[0][1, :, here]
    return entering(factors, *ends, here, half // 2, steps)


def couplings_kernel(ratio, steps, raw_ref, factor_ref, slab, cross, velocity_ref, *rest):
    *ends, first_ref, coupled_ref, near_ref, far_ref, layers = rest
    half = raw_ref.shape[1]
    tile = half // 2
    cells = slab.shape[1]
    groups = cells // LANES
    core = this_core()

    def sweep(side, group, carry):
        here = lane_block(group * LANES)
        factors = [factor_ref[slot, :, here] for slot in range(4)]
        values = lambda step: (raw_ref[2 * step, :, here], raw_ref[2 * step + 1, :, here])

        def put(step, state, adjoint):
            if side is None:
                first_ref[2 * step, :, here] = state
                first_ref[2 * step + 1, :, here] = adjoint
            else:
                layers[side, 2 * step] = state
                layers[side, 2 * step + 1] = adjoint

        solve_steps(values, *factors, ratio, *enter_values(ends, factors, here, half, steps), steps, put)
        return carry

    lax.fori_loop(0, groups, functools.partial(sweep, None), 0)
    for side in range(2):
        sweep(side, groups + side, 0)

    def one(group, carry):
        here = lane_block(group * LANES)
        left = lane_block(jnp.maximum(group - 1, 0) * LANES)
        right = lane_block(jnp.minimum(group + 1, groups - 1) * LANES)
        row = pl.ds(group, 1)
        own = pl.ds(pl.multiple_of(core * half, 8), half)
        weights, inside = faces(slab, cross[steps, row, :], group, half)
        tables = ([], [])
        for direction, component in enumerate((2, 0, 1)):
            drift = 0.5 * velocity_ref[component, own, here]
            ahead, behind = weights[direction]
            ok_ahead, ok_behind = inside[direction]
            for field, sign in enumerate((1.0, -1.0)):
                tables[field].append(
                    (
                        jnp.where(ok_ahead, ahead - sign * drift, 0.0),
                        jnp.where(ok_behind, behind + sign * drift, 0.0),
                    )
                )
        factors = [factor_ref[slot, :, here] for slot in range(4)]

        def values(step):
            results = []
            for field in range(2):
                slot = 2 * step + field
                outer = layers[0, slot, row, :]
                inner = layers[1, slot, row, :]
                before = jnp.where(core == 0, outer, inner)
                after = jnp.where(core == 0, inner, outer)
                pairs = side_values(first_ref[slot, :, here], first_ref[slot, :, left], first_ref[slot, :, right], before, after)
                result = None
                for (ahead, behind), (c_ahead, c_behind) in zip(pairs, tables[field]):
                    term = c_ahead * ahead + c_behind * behind
                    result = term if result is None else result + term
                coupled_ref[slot, :, here] = result
                results.append(result)
            return results

        put_ends(local_ends(values, *factors, steps), near_ref, far_ref, here, tile)
        return carry

    lax.fori_loop(0, groups, one, 0)


def parts_kernel(ratio, steps_local, coupled_ref, first_ref, factor_ref, keep, send, middle_ref):
    groups = coupled_ref.shape[2] // LANES
    core = this_core()

    def one(group, carry):
        here = lane_block(group * LANES)
        factors = [factor_ref[slot, :, here] for slot in range(4)]
        results = {}
        for sub in range(2):
            offset = 2 * steps_local * sub

            def values(step):
                return coupled_ref[offset + 2 * step, :, here], coupled_ref[offset + 2 * step + 1, :, here]

            def put(step, state, adjoint):
                results[sub, step] = (state, adjoint)

            back, last = solve_steps(values, *factors, ratio, None, None, steps_local, put)
            if sub == 1:
                middle_ref[0, :, here] = back
            else:
                middle_ref[1, :, here] = last
        for step in range(steps_local):
            for field in range(2):
                early, late = [
                    first_ref[2 * steps_local * sub + 2 * step + field, :, here] + results[sub, step][field]
                    for sub in range(2)
                ]
                keep[field, step, :, here] = jnp.where(core == 0, early, late)
                send[field, step, :, here] = jnp.where(core == 0, late, early)
        return carry

    lax.fori_loop(0, groups, one, 0)


def carry_kernel(steps_local, factor_ref, middle_ref, *rest):
    *ends, keep, send = rest
    half, cells = middle_ref.shape[1:]
    core = this_core()

    def one(group, carry):
        here = lane_block(group * LANES)
        factors = [factor_ref[slot, :, here] for slot in range(4)]
        decay, _, _, upright = factors
        back, state = enter_values(ends, factors, here, half, 2 * steps_local)
        block = power(decay, steps_local)
        early_back = middle_ref[0, :, here] + block * back
        late_state = middle_ref[1, :, here] + block * state + response_of(decay, upright, steps_local) * early_back
        for slot, (early, late) in enumerate(((early_back, back), (state, late_state))):
            keep[slot, :, here] = jnp.where(core == 0, early, late)
            send[slot, :, here] = jnp.where(core == 0, late, early)
        return carry

    lax.fori_loop(0, cells // LANES, one, 0)


def finish_kernel(ratio, chips, keep, other, keep_in, other_in, factor_ref, other_factor, state_out, adjoint_out, result, sems):
    steps_local, half, cells = keep.shape[1:]
    core = this_core()
    whole = step_scale(ratio, 2 * steps_local, chips, -1)
    scales = [jnp.where(core == 0, whole[step], whole[steps_local + step]) for step in range(steps_local)]
    copies = []
    for part, (parts, entered, table) in enumerate(((keep, keep_in, factor_ref), (other, other_in, other_factor))):

        def one(group, carry):
            here = lane_block(group * LANES)
            decay, _, mixed, upright = [table[slot, :, here] for slot in range(4)]
            backs = [entered[0, :, here]]
            for _ in range(steps_local):
                backs.append(decay * backs[-1])
            backs = backs[:0:-1]
            gain = ratio * mixed
            half_up = 0.5 * upright
            previous = entered[1, :, here]
            for step in range(steps_local):
                current = decay * previous + half_up * backs[step]
                result[part, 0, step, :, here] = (parts[0, step, :, here] + current) * scales[step]
                result[part, 1, step, :, here] = (parts[1, step, :, here] + (backs[step] - gain * previous)) * scales[step]
                previous = current
            return carry

        lax.fori_loop(0, cells // LANES, one, 0)
        rows = pl.ds(pl.multiple_of((core if part == 0 else 1 - core) * half, 8), half)
        for field, out in enumerate((state_out, adjoint_out)):
            copies.append(pltpu.make_async_copy(result.at[part, field], out.at[:, rows, :], sems.at[part, field]))
            copies[-1].start()
    for copy in copies:
        copy.wait()


def body(state_rhs, adjoint_rhs, diffusivity, velocity):
    steps_local, depth, cells = state_rhs.shape
    ranks = lax.axis_size("tm")
    slabs = lax.axis_size("gz")
    chips = ranks // 2
    total = steps_local * ranks
    steps = 2 * steps_local
    half = depth // 2
    tile = half // 2
    groups = cells // LANES
    wide = cells + 2 * LANES
    ratio = alpha_wrap ** (1.0 / total)
    core = this_core()
    f32 = jnp.float32
    anywhere = pl.BlockSpec(memory_space=pl.ANY)

    def partner(value, mask):
        return lax.ppermute(value, "tm", [(i, i ^ mask) for i in range(ranks)])

    def outward(value, flip):
        pairs = []
        for t in range(ranks):
            for g in range(slabs):
                down = (t + flip) % 2 == 1
                to = g - 1 if down else g + 1
                if 0 <= to < slabs:
                    pairs.append((t * slabs + g, (t ^ flip) * slabs + to))
        return lax.ppermute(value, ("tm", "gz"), pairs)

    def call(kernel, name, out_shape, *args, **kwargs):
        shapes = [jax.ShapeDtypeStruct(s, f32) for s in out_shape]
        return pl.pallas_call(
            kernel,
            out_shape=shapes,
            compiler_params=pltpu.CompilerParams(vmem_limit_bytes=32 * 1024 * 1024),
            name=name,
            **kwargs,
        )(*args)

    layer = (groups, LANES)
    halves = (2, steps_local, half, cells)
    keep, send, slab, cross, straight, inner_keep, inner_send, layers = call(
        pack_kernel,
        "halves_and_layers",
        [halves, halves, (depth, cells), (steps + 2,) + layer, (steps,) + layer, (steps,) + layer, (steps,) + layer, (4,) + layer],
        state_rhs,
        adjoint_rhs,
        diffusivity,
        in_specs=[anywhere] * 3,
        scratch_shapes=[pltpu.SemaphoreType.DMA((5,))],
    )
    other = partner(send, 1)
    inner_other = partner(inner_send, 1)
    cross = outward(cross, 1)
    straight = outward(straight, 0)
    ends_shape = [(2, tile, wide)] * 2
    raw, factors, near, far = call(
        functools.partial(ends_kernel, ratio, chips),
        "ends_of_first",
        [(2 * steps, half, wide), (4, half, wide)] + ends_shape,
        keep,
        other,
        slab,
        cross,
        straight,
        inner_keep,
        inner_other,
        layers,
    )

    def exchange(near, far):
        width = near.shape[2]
        if chips != 4:
            gathered = lax.all_gather(jnp.concatenate([near, far], axis=1), "tm")
            gathered = lax.dynamic_index_in_dim(
                gathered.reshape((chips, 2) + gathered.shape[1:]), core, 1, keepdims=False
            )
            block, response, closing = ring_factors([factors[i, :, :width] for i in range(4)], steps, chips)
            at = lambda array, index: lax.dynamic_index_in_dim(array, lax.rem(index + 2 * chips, chips), 0, keepdims=False)
            chip = this_chip()

            def entering_back(where):
                value = jnp.zeros((half, width), f32)
                for offset in reversed(range(chips)):
                    value = block * value + at(gathered[:, 0], where + 1 + offset)
                return value * closing

            value = jnp.zeros((half, width), f32)
            for offset in reversed(range(chips)):
                source = chip - 1 - offset
                value = block * value + at(gathered[:, 1], source) + response * entering_back(source)
            return [jnp.stack([entering_back(chip), value * closing])]
        near_in, far_in = partner(near, 2), partner(far, 4)
        near_out, far_out = call(
            functools.partial(relay_kernel, steps), "relay", [near.shape] * 2, factors, near, near_in, far, far_in
        )
        return [near, near_in, partner(near_out, 4), far, far_in, partner(far_out, 2)]

    ends = exchange(near, far)
    other_factors = partner(factors, 1)
    first, coupled, near, far = call(
        functools.partial(couplings_kernel, ratio, steps),
        "first_sweep_and_couplings",
        [(2 * steps, half, cells)] * 2 + [(2, tile, cells)] * 2,
        raw,
        factors,
        slab,
        cross,
        velocity,
        *ends,
        scratch_shapes=[pltpu.VMEM((2, 2 * steps) + layer, f32)],
    )
    ends = exchange(near, far)
    keep, send, middle = call(
        functools.partial(parts_kernel, ratio, steps_local),
        "own_steps",
        [halves, halves, (2, half, cells)],
        coupled,
        first,
        factors,
    )
    other = partner(send, 1)
    keep_in, send_in = call(
        functools.partial(carry_kernel, steps_local), "entering", [(2, half, cells)] * 2, factors, middle, *ends
    )
    other_in = partner(send_in, 1)
    return call(
        functools.partial(finish_kernel, ratio, chips),
        "finish",
        [(steps_local, depth, cells)] * 2,
        keep,
        other,
        keep_in,
        other_in,
        factors,
        other_factors,
        out_specs=[anywhere] * 2,
        scratch_shapes=[pltpu.VMEM((2,) + halves, f32), pltpu.SemaphoreType.DMA((2, 2))],
    )


def solution(mesh):
    placed = (P("tm", "gz", None), P("tm", "gz", None), P("gz", None), P(None, "gz", None))
    return jax.shard_map(
        body,
        mesh=mesh,
        in_specs=placed,
        out_specs=(P("tm", "gz", None), P("tm", "gz", None)),
        check_vma=False,
    )
```

```python
import functools
import math

import jax
import jax.numpy as jnp
from jax import lax
from jax.experimental import pallas as pl
from jax.experimental.pallas import tpu as pltpu
from jax.sharding import PartitionSpec as P

NY = 64
LANES = 128

alpha_wrap = 0.1
beta_couple = 0.5
gamma_couple = 0.5


def this_core():
    return lax.rem(lax.axis_index("tm"), 2)


def this_chip():
    return lax.div(lax.axis_index("tm"), 2)


def lane_block(start, width=LANES):
    return pl.ds(pl.multiple_of(start, LANES), width)


def each_block(cells, width, work):
    def one(index, carry):
        work(lane_block(index * width, width))
        return carry

    lax.fori_loop(0, cells // width, one, 0)
    if cells % width:
        work(slice(cells - cells % width, cells))


def power(value, count):
    result = None
    while count:
        if count & 1:
            result = value if result is None else result * value
        count >>= 1
        if count:
            value = value * value
    return result


def step_scale(ratio, steps, chips, sign):
    chip = this_chip()
    base = jnp.float32(1.0)
    bit = 0
    while 1 << bit < chips:
        factor = ratio ** (sign * steps * (1 << bit))
        base = base * jnp.where(lax.rem(lax.div(chip, 1 << bit), 2) == 1, factor, 1.0)
        bit += 1
    return [base * (ratio ** (sign * step)) for step in range(steps)]


OUTER, INNER = 0, 1
UNROLL_ENDS = 4
UNROLL_COUPLINGS = 2


def tile_rows(side, half, depth):
    core = this_core()
    tile = half // 2
    return core * (depth - tile) if side == OUTER else tile + core * tile


def faces(side, slab, outer, group, half):
    core = this_core()
    depth, cells = slab.shape
    tile = half // 2
    groups = cells // LANES
    own = pl.ds(pl.multiple_of(tile_rows(side, half, depth), 8), tile)
    here = lane_block(group * LANES)
    kappa = slab[own, here]
    left = slab[own, lane_block(jnp.maximum(group - 1, 0) * LANES)]
    right = slab[own, lane_block(jnp.minimum(group + 1, groups - 1) * LANES)]
    mirrored = lambda row: jnp.where(core == 0, slab[row : row + 1, here], slab[depth - 1 - row : depth - row, here])
    outward = outer if side == OUTER else mirrored(tile - 1)
    inward = mirrored(tile if side == OUTER else half)
    first, last = edge_rows(kappa.shape)
    shift, back = z_shifts(tile)
    lane = lax.broadcasted_iota(jnp.int32, kappa.shape, 1)
    column = lax.rem(lane, NY)
    low = lane < NY
    turned = pltpu.roll(kappa, NY, 1)
    outward = jnp.where(first, outward, pltpu.roll(kappa, shift, 0))
    inward = jnp.where(last, inward, pltpu.roll(kappa, back, 0))
    pairs = (
        ((outward, outward > 0.0), (inward, inward > 0.0)),
        (
            (jnp.where(low, turned, pltpu.roll(right, NY, 1)), jnp.logical_or(low, group < groups - 1)),
            (jnp.where(low, pltpu.roll(left, NY, 1), turned), jnp.logical_or(lane >= NY, group > 0)),
        ),
        ((pltpu.roll(kappa, LANES - 1, 1), column < NY - 1), (pltpu.roll(kappa, 1, 1), column > 0)),
    )
    return [[(jnp.where(ok, 0.5 * (kappa + value), kappa), ok) for value, ok in pair] for pair in pairs]


def edge_rows(shape):
    core = this_core()
    row = lax.broadcasted_iota(jnp.int32, shape, 0)
    last = shape[0] - 1
    return row == core * last, row == (1 - core) * last


def z_shifts(tile):
    core = this_core()
    return 1 + core * (tile - 2), tile - 1 - core * (tile - 2)


def total_weight(weights):
    total = None
    for pair in weights:
        for weight, _ in pair:
            total = weight if total is None else total + weight
    return total


def layer_diagonal(kappa, ahead, behind):
    rows = kappa.shape[0]
    lane = lax.broadcasted_iota(jnp.int32, kappa.shape, 1)
    row = lax.broadcasted_iota(jnp.int32, kappa.shape, 0)
    column = lax.rem(lane, NY)
    turned = pltpu.roll(kappa, NY, 1)
    x_ahead = jnp.where(lane < NY, turned, pltpu.roll(turned, rows - 1, 0))
    x_behind = jnp.where(lane < NY, pltpu.roll(turned, 1, 0), turned)
    pairs = (
        (ahead, ahead > 0.0),
        (behind, behind > 0.0),
        (x_ahead, jnp.logical_or(lane < NY, row < rows - 1)),
        (x_behind, jnp.logical_or(lane >= NY, row > 0)),
        (pltpu.roll(kappa, LANES - 1, 1), column < NY - 1),
        (pltpu.roll(kappa, 1, 1), column > 0),
    )
    total = None
    for value, ok in pairs:
        weight = jnp.where(ok, 0.5 * (kappa + value), kappa)
        total = weight if total is None else total + weight
    return total


def cell_factors(diagonal, ratio):
    shifted = 1.0 + diagonal
    lifted = shifted * shifted - (ratio * ratio + beta_couple * gamma_couple)
    mix = shifted / (lifted + jnp.sqrt(lifted * lifted + shifted * shifted))
    inverse = 1.0 / (shifted + 0.5 * mix)
    return ratio * inverse, inverse, mix * inverse, 1.0 / shifted


def local_ends(values, decay, inverse, mixed, upright, steps):
    back = None
    last = None
    weight = None
    for step in reversed(range(steps)):
        state, adjoint = values(step)
        drive = inverse * adjoint - mixed * state
        back = drive if back is None else decay * back + drive
        term = state + 0.5 * back
        last = term if last is None else last + weight * term
        weight = decay if weight is None else weight * decay
    return back, last * upright


def solve_steps(values, decay, inverse, mixed, upright, ratio, back_in, state_in, steps, put):
    backs = [None] * steps
    back = back_in
    for step in reversed(range(steps)):
        state, adjoint = values(step)
        drive = inverse * adjoint - mixed * state
        back = drive if back is None else decay * back + drive
        backs[step] = back
    gain = ratio * mixed
    half_up = 0.5 * upright
    previous = state_in
    for step in range(steps):
        state, _ = values(step)
        current = upright * state + half_up * backs[step]
        adjoint = backs[step]
        if previous is not None:
            current = current + decay * previous
            adjoint = adjoint - gain * previous
        put(step, current, adjoint)
        previous = current
    return backs[0], previous


def pack_kernel(state, adjoint, kappa, keep, send, slab, outer_cross, outer_straight, inner_keep, inner_send, layers, sems):
    steps_local = state.shape[0]
    half = keep.shape[2]
    core = this_core()
    mine = pl.ds(pl.multiple_of(core * half, 8), half)
    others = pl.ds(pl.multiple_of((1 - core) * half, 8), half)
    copies = [pltpu.make_async_copy(kappa, slab, sems.at[4])]
    for field, source in enumerate((state, adjoint)):
        copies.append(pltpu.make_async_copy(source.at[:, mine, :], keep.at[field], sems.at[2 * field]))
        copies.append(pltpu.make_async_copy(source.at[:, others, :], send.at[field], sems.at[2 * field + 1]))
    for copy in copies:
        copy.start()

    def lay(source, rows, target):
        for group in range(target.shape[0]):
            lanes = slice(group * LANES, (group + 1) * LANES)
            one, other = [source[row : row + 1, lanes] for row in rows]
            target[group : group + 1, :] = jnp.where(core == 0, one, other)

    copies[0].wait()
    last = 2 * half - 1
    lay(slab, (0, last), outer_cross.at[2 * steps_local])
    lay(slab, (1, last - 1), outer_cross.at[2 * steps_local + 1])
    for slot, row in enumerate((0, half - 1, half, half + 1)):
        lay(slab, (row, last - row), layers.at[slot])
    for copy in copies[1:]:
        copy.wait()
    near, far = (0, half - 1), (half - 1, 0)
    for index in range(steps_local):
        for field in range(2):
            slot = 2 * index + field
            lay(keep.at[field, index], near, outer_cross.at[slot])
            lay(send.at[field, index], far, outer_straight.at[slot])
            lay(send.at[field, index], near, inner_keep.at[slot])
            lay(keep.at[field, index], far, inner_send.at[slot])


def ends_kernel(side, ratio, chips, keep, other, slab, near_cut, near_cut_other, layers, *rest):
    kappa_cut = rest[0] if side == OUTER else None
    raw_ref, factor_ref, ends_ref = rest[-3:]
    steps_local, half, cells = keep.shape[1:]
    steps = 2 * steps_local
    tile = half // 2
    groups = cells // LANES
    core = this_core()
    scales = step_scale(ratio, steps, chips, 1)
    own = pl.ds(pl.multiple_of((core if side == OUTER else 1 - core) * tile, 8), tile)
    places = []
    for position in range(2):
        sub = core if position == 0 else 1 - core
        for index in range(steps_local):
            scale = jnp.where(sub == 0, scales[index], scales[steps_local + index])
            places.append((position, index, sub * steps + 2 * index, scale))

    def work(diagonal, loads, stores):
        factors = cell_factors(diagonal, ratio)
        for slot, value in enumerate(factors):
            stores(factor_ref, slot, value)
        for position, index, slot, scale in places:
            for field in range(2):
                stores(raw_ref, slot + field, loads(position, index, field) * scale)

    def put_ends(here):
        factors = [factor_ref[slot, :, here] for slot in range(4)]
        values = lambda step: (raw_ref[2 * step, :, here], raw_ref[2 * step + 1, :, here])
        for slot, value in enumerate(local_ends(values, *factors, steps)):
            ends_ref[slot, :, here] = value

    def one(group, carry):
        here = lane_block(group * LANES)
        beyond = kappa_cut[steps, pl.ds(group, 1), :] if side == OUTER else None
        diagonal = total_weight(faces(side, slab, beyond, group, half))

        def stores(ref, slot, value):
            ref[slot, :, here] = value

        work(diagonal, lambda position, index, field: (keep, other)[position][field, index, own, here], stores)
        put_ends(here)
        return carry

    lax.fori_loop(0, groups, one, 0, unroll=UNROLL_ENDS)

    def stores_cut(ref, slot, value):
        for part in range(2):
            lanes = slice(cells + part * LANES, cells + (part + 1) * LANES)
            ref[slot, :, lanes] = value[part * tile : (part + 1) * tile]

    if side == OUTER:
        diagonal = layer_diagonal(kappa_cut[steps], layers[0], kappa_cut[steps + 1])
    else:
        diagonal = layer_diagonal(layers[2], layers[1], layers[3])
    sources = (near_cut, near_cut_other)
    work(diagonal, lambda position, index, field: sources[position][2 * index + field], stores_cut)
    for part in range(2):
        put_ends(slice(cells + part * LANES, cells + (part + 1) * LANES))


def power_sum(value, count):
    total = None
    for _ in range(count):
        total = 1.0 if total is None else 1.0 + value * total
    return total


def response_of(decay, upright, steps):
    return (0.5 * upright) * decay * power_sum(decay * decay, steps)


def ring_factors(factors, steps, chips):
    decay, _, _, upright = factors
    block = power(decay, steps)
    return block, response_of(decay, upright, steps), 1.0 / (1.0 - power(block, chips))


def contribution(ends, offset, block, response, closing):
    back, last = ends
    square = block * block
    if offset == 0:
        up, down, cross = square * block, square * block, 1.0 + square + square * square * (1.0 + square)
    elif offset == 1:
        up, down, cross = None, square, block * (1.0 + square) * (1.0 + square)
    elif offset == 2:
        up, down, cross = block, block, 2.0 * square * (1.0 + square)
    else:
        up, down, cross = square, None, block * (1.0 + square) * (1.0 + square)
    entering_back = back if up is None else up * back
    entering_state = last if down is None else down * last
    entering_state = entering_state + (cross * response * closing) * back
    return closing * entering_back, closing * entering_state


def either(flag, one, other):
    return tuple(jnp.where(flag, a, b) for a, b in zip(one, other))


def relay_kernel(side, steps, factor_ref, mine, theirs, out):
    odd = lax.rem(this_chip(), 2) == 1

    def one(here):
        ring = ring_factors([factor_ref[slot, :, here] for slot in range(4)], steps, 4)
        a = (mine[0, :, here], mine[1, :, here])
        b = (theirs[0, :, here], theirs[1, :, here])
        if side == OUTER:
            one_part = contribution(a, 2, *ring)
            other_part = either(odd, contribution(b, 1, *ring), contribution(b, 3, *ring))
        else:
            one_part = either(odd, contribution(a, 1, *ring), contribution(a, 3, *ring))
            other_part = either(odd, contribution(b, 3, *ring), contribution(b, 1, *ring))
        out[0, :, here] = one_part[0] + other_part[0]
        out[1, :, here] = one_part[1] + other_part[1]

    each_block(mine.shape[2], 4 * LANES, one)


def entering(side, factors, ends, here, steps):
    if len(ends) == 1:
        return ends[0][0, :, here], ends[0][1, :, here]
    odd = lax.rem(this_chip(), 2) == 1
    mine, theirs, tail = ends
    ring = ring_factors(factors, steps, 4)
    own = contribution((mine[0, :, here], mine[1, :, here]), 0, *ring)
    b = (theirs[0, :, here], theirs[1, :, here])
    if side == OUTER:
        near_by = either(odd, contribution(b, 3, *ring), contribution(b, 1, *ring))
    else:
        near_by = contribution(b, 2, *ring)
    return own[0] + near_by[0] + tail[0, :, here], own[1] + near_by[1] + tail[1, :, here]


def sweep_kernel(side, ratio, raw_ref, factor_ref, *rest):
    *ends, first_ref, turned_ref, layer_ref = rest
    tile = raw_ref.shape[1]
    steps = raw_ref.shape[0] // 2
    cells = first_ref.shape[2]

    def sweep(put, here):
        factors = [factor_ref[slot, :, here] for slot in range(4)]
        values = lambda step: (raw_ref[2 * step, :, here], raw_ref[2 * step + 1, :, here])
        solve_steps(values, *factors, ratio, *entering(side, factors, ends, here, steps), steps, put)

    def own(here):
        def put(step, state, adjoint):
            for field, value in enumerate((state, adjoint)):
                slot = 2 * step + field
                first_ref[slot, :, here] = value
                turned_ref[slot, :, here] = turned(value)

        sweep(put, here)

    each_block(cells, 2 * LANES, own)

    def put_layer(step, state, adjoint):
        for field, value in enumerate((state, adjoint)):
            for part in range(2):
                layer_ref[2 * step + field, part * tile : (part + 1) * tile, :] = value[:, part * LANES : (part + 1) * LANES]

    sweep(put_layer, slice(cells, cells + 2 * LANES))


def turned(value):
    parts = [pltpu.roll(value[:, i : i + LANES], NY, 1) for i in range(0, value.shape[1], LANES)]
    return parts[0] if len(parts) == 1 else jnp.concatenate(parts, axis=1)


def couplings_kernel(side, first_ref, turned_ref, next_ref, layer_ref, slab, velocity_ref, factor_ref, *rest):
    coupled_ref, ends_ref = rest[-2:]
    slots, tile, cells = first_ref.shape
    steps = slots // 2
    depth = slab.shape[0]
    half = 2 * tile
    groups = cells // LANES
    core = this_core()
    own = pl.ds(pl.multiple_of(tile_rows(side, half, depth), 8), tile)
    out_shift, in_shift = z_shifts(tile)

    def one(group, carry):
        here = lane_block(group * LANES)
        left = lane_block(jnp.maximum(group - 1, 0) * LANES)
        right = lane_block(jnp.minimum(group + 1, groups - 1) * LANES)
        row = pl.ds(group, 1)
        beyond = rest[0][steps, row, :] if side == OUTER else None
        weights = faces(side, slab, beyond, group, half)
        lane = lax.broadcasted_iota(jnp.int32, (tile, LANES), 1)
        low = lane < NY
        first, last = edge_rows((tile, LANES))
        drifts = [0.5 * velocity_ref[component, own, here] for component in (2, 0, 1)]
        drifts[0] = jnp.where(core == 0, -drifts[0], drifts[0])
        tables = []
        for sign in (1.0, -1.0):
            one_way, other_way = [], []
            for ((ahead, ok_ahead), (behind, ok_behind)), drift in zip(weights, drifts):
                one_way.append(jnp.where(ok_ahead, ahead - sign * drift, 0.0))
                other_way.append(jnp.where(ok_behind, behind + sign * drift, 0.0))
            x_same = jnp.where(low, one_way[1], other_way[1])
            x_next = jnp.where(low, other_way[1], one_way[1])
            tables.append((one_way[0], other_way[0], x_same, x_next, one_way[2], other_way[2]))
        factors = [factor_ref[slot, :, here] for slot in range(4)]

        def values(step):
            results = []
            for field in range(2):
                slot = 2 * step + field
                c_out, c_in, x_same, x_next, c_ahead, c_behind = tables[field]
                value = first_ref[slot, :, here]
                following = next_ref[slot, :, here]
                cut = layer_ref[slot, row, :]
                if side == OUTER:
                    outward = jnp.where(first, cut, pltpu.roll(value, out_shift, 0))
                    inward = pltpu.roll(jnp.where(first, following, value), in_shift, 0)
                else:
                    outward = pltpu.roll(jnp.where(last, following, value), out_shift, 0)
                    inward = jnp.where(last, cut, pltpu.roll(value, in_shift, 0))
                result = c_out * outward + c_in * inward
                beside = jnp.where(low, turned_ref[slot, :, left], turned_ref[slot, :, right])
                result = result + (x_same * turned_ref[slot, :, here] + x_next * beside)
                result = result + (c_ahead * pltpu.roll(value, LANES - 1, 1) + c_behind * pltpu.roll(value, 1, 1))
                coupled_ref[slot, :, here] = result
                results.append(result)
            return results

        for slot, value in enumerate(local_ends(values, *factors, steps)):
            ends_ref[slot, :, here] = value
        return carry

    lax.fori_loop(0, groups, one, 0, unroll=UNROLL_COUPLINGS)


def parts_kernel(ratio, outer, outer_first, outer_factors, inner, inner_first, inner_factors, keep, send, middle):
    steps_local = keep.shape[1]
    tile, cells = outer.shape[1:]
    core = this_core()
    for side, (coupled_ref, first_ref, factor_ref) in enumerate(
        ((outer, outer_first, outer_factors), (inner, inner_first, inner_factors))
    ):
        rows = slice(side * tile, (side + 1) * tile)

        def one(here):
            factors = [factor_ref[slot, :, here] for slot in range(4)]
            results = {}
            for sub in range(2):
                offset = 2 * steps_local * sub

                def values(step):
                    return coupled_ref[offset + 2 * step, :, here], coupled_ref[offset + 2 * step + 1, :, here]

                def put(step, state, adjoint):
                    results[sub, step] = (state, adjoint)

                back, last = solve_steps(values, *factors, ratio, None, None, steps_local, put)
                middle[1 - sub, rows, here] = last if sub == 0 else back
            for step in range(steps_local):
                for field in range(2):
                    early, late = [
                        first_ref[2 * steps_local * sub + 2 * step + field, :, here] + results[sub, step][field]
                        for sub in range(2)
                    ]
                    keep[field, step, rows, here] = jnp.where(core == 0, early, late)
                    send[field, step, rows, here] = jnp.where(core == 0, late, early)

        each_block(cells, 2 * LANES, one)


def carry_kernel(side, steps_local, factor_ref, middle, *rest):
    *ends, keep, send = rest
    tile, cells = keep.shape[1:]
    rows = slice(side * tile, (side + 1) * tile)
    core = this_core()

    def one(here):
        factors = [factor_ref[slot, :, here] for slot in range(4)]
        decay, _, _, upright = factors
        back, state = entering(side, factors, ends, here, 2 * steps_local)
        block = power(decay, steps_local)
        early_back = middle[0, rows, here] + block * back
        late_state = middle[1, rows, here] + block * state + response_of(decay, upright, steps_local) * early_back
        for slot, (early, late) in enumerate(((early_back, back), (state, late_state))):
            keep[slot, :, here] = jnp.where(core == 0, early, late)
            send[slot, :, here] = jnp.where(core == 0, late, early)

    each_block(cells, 4 * LANES, one)


def finish_kernel(side, ratio, chips, keep, other, keep_in, other_in, factor_ref, other_factor, *rest):
    state_out, adjoint_out, result, sems = rest[-4:]
    steps_local = keep.shape[1]
    tile, cells = keep_in.shape[1:]
    half = 2 * tile
    depth = state_out.shape[1]
    core = this_core()
    whole = step_scale(ratio, 2 * steps_local, chips, -1)
    scales = [jnp.where(core == 0, whole[step], whole[steps_local + step]) for step in range(steps_local)]
    held = slice(side * tile, (side + 1) * tile)
    start = tile_rows(side, half, depth)
    copies = []
    for part, (parts, entered, table) in enumerate(((keep, keep_in, factor_ref), (other, other_in, other_factor))):

        def one(here):
            decay, _, mixed, upright = [table[slot, :, here] for slot in range(4)]
            backs = [entered[0, :, here]]
            for _ in range(steps_local):
                backs.append(decay * backs[-1])
            backs = backs[:0:-1]
            gain = ratio * mixed
            half_up = 0.5 * upright
            previous = entered[1, :, here]
            for step in range(steps_local):
                current = decay * previous + half_up * backs[step]
                adjoint = backs[step] - gain * previous
                result[part, 0, step, :, here] = (parts[0, step, held, here] + current) * scales[step]
                result[part, 1, step, :, here] = (parts[1, step, held, here] + adjoint) * scales[step]
                previous = current

        each_block(cells, 4 * LANES, one)
        rows = pl.ds(pl.multiple_of(start if part == 0 else depth - tile - start, 8), tile)
        for field, out in enumerate((state_out, adjoint_out)):
            copies.append(pltpu.make_async_copy(result.at[part, field], out.at[:, rows, :], sems.at[part, field]))
            copies[-1].start()
    for copy in copies:
        copy.wait()


def either(flag, one, other):
    return tuple(jnp.where(flag, a, b) for a, b in zip(one, other))


def body(state_rhs, adjoint_rhs, diffusivity, velocity):
    steps_local, depth, cells = state_rhs.shape
    ranks = lax.axis_size("tm")
    slabs = lax.axis_size("gz")
    chips = ranks // 2
    total = steps_local * ranks
    steps = 2 * steps_local
    half = depth // 2
    tile = half // 2
    groups = cells // LANES
    wide = cells + 2 * LANES
    ratio = alpha_wrap ** (1.0 / total)
    core = this_core()
    f32 = jnp.float32
    anywhere = pl.BlockSpec(memory_space=pl.ANY)

    def partner(value, mask):
        return lax.ppermute(value, "tm", [(i, i ^ mask) for i in range(ranks)])

    def outward(value, flip):
        pairs = []
        for t in range(ranks):
            for g in range(slabs):
                down = (t + flip) % 2 == 1
                to = g - 1 if down else g + 1
                if 0 <= to < slabs:
                    pairs.append((t * slabs + g, (t ^ flip) * slabs + to))
        return lax.ppermute(value, ("tm", "gz"), pairs)

    def call(kernel, name, out_shape, *args, room=32, **kwargs):
        shapes = [jax.ShapeDtypeStruct(s, f32) for s in out_shape]
        return pl.pallas_call(
            kernel,
            out_shape=shapes,
            compiler_params=pltpu.CompilerParams(vmem_limit_bytes=room * 1024 * 1024),
            name=name,
            **kwargs,
        )(*args)

    layer = (groups, LANES)
    halves = (2, steps_local, half, cells)
    keep, send, slab, cross, straight, inner_keep, inner_send, layers = call(
        pack_kernel,
        "halves_and_layers",
        [halves, halves, (depth, cells), (steps + 2,) + layer, (steps,) + layer, (steps,) + layer, (steps,) + layer, (4,) + layer],
        state_rhs,
        adjoint_rhs,
        diffusivity,
        in_specs=[pl.BlockSpec(memory_space=pltpu.HBM)] * 3,
        scratch_shapes=[pltpu.SemaphoreType.DMA((5,))],
    )
    other = partner(send, 1)
    inner_other = partner(inner_send, 1)
    cross = outward(cross, 1)
    straight = outward(straight, 0)

    def first_ends(side, *args):
        return call(
            functools.partial(ends_kernel, side, ratio, chips),
            ("outer", "inner")[side] + "_ends",
            [(2 * steps, tile, wide), (4, tile, wide), (2, tile, wide)],
            keep,
            other,
            slab,
            *args,
        )

    inner_raw, inner_factors, inner_ends = first_ends(INNER, inner_keep, inner_other, layers)
    outer_raw, outer_factors, outer_ends = first_ends(OUTER, straight, cross, layers, cross)

    def exchange(side, mine, factors):
        width = mine.shape[2]
        if chips != 4:
            gathered = lax.dynamic_index_in_dim(
                lax.all_gather(mine, "tm").reshape((chips, 2) + mine.shape), core, 1, keepdims=False
            )
            block, response, closing = ring_factors([factors[i, :, :width] for i in range(4)], steps, chips)
            at = lambda array, index: lax.dynamic_index_in_dim(array, lax.rem(index + 2 * chips, chips), 0, keepdims=False)
            chip = this_chip()

            def entering_back(where):
                value = jnp.zeros((tile, width), f32)
                for offset in reversed(range(chips)):
                    value = block * value + at(gathered[:, 0], where + 1 + offset)
                return value * closing

            value = jnp.zeros((tile, width), f32)
            for offset in reversed(range(chips)):
                source = chip - 1 - offset
                value = block * value + at(gathered[:, 1], source) + response * entering_back(source)
            return [jnp.stack([entering_back(chip), value * closing])]
        masks = (2, 4) if side == OUTER else (4, 2)
        theirs = partner(mine, masks[0])
        (passed,) = call(
            functools.partial(relay_kernel, side, steps),
            ("outer", "inner")[side] + "_relay",
            [mine.shape],
            factors,
            mine,
            theirs,
        )
        return [mine, theirs, partner(passed, masks[1])]

    def first_sweep(side, raw, factors, ends):
        return call(
            functools.partial(sweep_kernel, side, ratio),
            ("outer", "inner")[side] + "_first_sweep",
            [(2 * steps, tile, cells)] * 2 + [(2 * steps,) + layer],
            raw,
            factors,
            *ends,
        )

    inner_first, inner_turned, inner_layer = first_sweep(
        INNER, inner_raw, inner_factors, exchange(INNER, inner_ends, inner_factors)
    )
    outer_first, outer_turned, outer_layer = first_sweep(
        OUTER, outer_raw, outer_factors, exchange(OUTER, outer_ends, outer_factors)
    )
    inner_factors_other = partner(inner_factors, 1)
    outer_factors_other = partner(outer_factors, 1)

    def couplings(side, *args):
        return call(
            functools.partial(couplings_kernel, side),
            ("outer", "inner")[side] + "_couplings",
            [(2 * steps, tile, cells), (2, tile, cells)],
            *args,
        )

    inner_coupled, inner_ends = couplings(
        INNER, inner_first, inner_turned, outer_first, inner_layer, slab, velocity, inner_factors
    )
    outer_coupled, outer_ends = couplings(
        OUTER, outer_first, outer_turned, inner_first, outer_layer, slab, velocity, outer_factors, cross
    )
    inner_entered = exchange(INNER, inner_ends, inner_factors)
    outer_entered = exchange(OUTER, outer_ends, outer_factors)
    keep, send, middle = call(
        functools.partial(parts_kernel, ratio),
        "own_steps",
        [halves, halves, (2, half, cells)],
        outer_coupled,
        outer_first,
        outer_factors,
        inner_coupled,
        inner_first,
        inner_factors,
    )
    other = partner(send, 1)

    def finish(side, entered, factors, factors_other, results):
        keep_in, send_in = call(
            functools.partial(carry_kernel, side, steps_local),
            ("outer", "inner")[side] + "_entering",
            [(2, tile, cells)] * 2,
            factors,
            middle,
            *entered,
        )
        other_in = partner(send_in, 1)
        vmem = pl.BlockSpec(memory_space=pltpu.VMEM)
        return call(
            functools.partial(finish_kernel, side, ratio, chips),
            ("outer", "inner")[side] + "_finish",
            [(steps_local, depth, cells)] * 2,
            keep,
            other,
            keep_in,
            other_in,
            factors,
            factors_other,
            *results,
            in_specs=[vmem] * 6 + [anywhere] * len(results),
            out_specs=[anywhere] * 2,
            scratch_shapes=[pltpu.VMEM((2, 2, steps_local, tile, cells), f32), pltpu.SemaphoreType.DMA((2, 2))],
            input_output_aliases={6 + i: i for i in range(len(results))},
            room=40,
        )

    results = finish(INNER, inner_entered, inner_factors, inner_factors_other, ())
    return finish(OUTER, outer_entered, outer_factors, outer_factors_other, results)


def solution(mesh):
    placed = (P("tm", "gz", None), P("tm", "gz", None), P("gz", None), P(None, "gz", None))
    return jax.shard_map(
        body,
        mesh=mesh,
        in_specs=placed,
        out_specs=(P("tm", "gz", None), P("tm", "gz", None)),
        check_vma=False,
    )
```

```python
import functools
import math

import jax
import jax.numpy as jnp
from jax import lax
from jax.experimental import pallas as pl
from jax.experimental.pallas import tpu as pltpu
from jax.sharding import PartitionSpec as P

NY = 64
LANES = 128

alpha_wrap = 0.1
beta_couple = 0.5
gamma_couple = 0.5


def this_core():
    return lax.rem(lax.axis_index("tm"), 2)


def this_chip():
    return lax.div(lax.axis_index("tm"), 2)


def lane_block(start, width=LANES):
    return pl.ds(pl.multiple_of(start, LANES), width)


def each_block(cells, width, work):
    def one(index, carry):
        work(lane_block(index * width, width))
        return carry

    lax.fori_loop(0, cells // width, one, 0)
    if cells % width:
        work(slice(cells - cells % width, cells))


def power(value, count):
    result = None
    while count:
        if count & 1:
            result = value if result is None else result * value
        count >>= 1
        if count:
            value = value * value
    return result


def step_scale(ratio, steps, chips, sign):
    chip = this_chip()
    base = jnp.float32(1.0)
    bit = 0
    while 1 << bit < chips:
        factor = ratio ** (sign * steps * (1 << bit))
        base = base * jnp.where(lax.rem(lax.div(chip, 1 << bit), 2) == 1, factor, 1.0)
        bit += 1
    return [base * (ratio ** (sign * step)) for step in range(steps)]


OUTER, INNER = 0, 1
MICROSECONDS = {
    'halves': 2,
    'outermost': 0.3,
    'ends': 1,
    'relay': 0.2,
    'first_sweep': 1.1,
    'couplings': 1.5,
    'own_steps': 0.7,
    'entering': 0.2,
    'finish_own': 1.2,
    'finish_other': 1.2,
}
UNROLL_ENDS = 4
UNROLL_COUPLINGS = 2


def tile_rows(side, half, depth):
    core = this_core()
    tile = half // 2
    return core * (depth - tile) if side == OUTER else tile + core * tile


def faces(side, slab, outer, group, half):
    core = this_core()
    depth, cells = slab.shape
    tile = half // 2
    groups = cells // LANES
    own = pl.ds(pl.multiple_of(tile_rows(side, half, depth), 8), tile)
    here = lane_block(group * LANES)
    kappa = slab[own, here]
    left = slab[own, lane_block(jnp.maximum(group - 1, 0) * LANES)]
    right = slab[own, lane_block(jnp.minimum(group + 1, groups - 1) * LANES)]
    mirrored = lambda row: jnp.where(core == 0, slab[row : row + 1, here], slab[depth - 1 - row : depth - row, here])
    outward = outer if side == OUTER else mirrored(tile - 1)
    inward = mirrored(tile if side == OUTER else half)
    first, last = edge_rows(kappa.shape)
    shift, back = z_shifts(tile)
    lane = lax.broadcasted_iota(jnp.int32, kappa.shape, 1)
    column = lax.rem(lane, NY)
    low = lane < NY
    turned = pltpu.roll(kappa, NY, 1)
    outward = jnp.where(first, outward, pltpu.roll(kappa, shift, 0))
    inward = jnp.where(last, inward, pltpu.roll(kappa, back, 0))
    pairs = (
        ((outward, outward > 0.0), (inward, inward > 0.0)),
        (
            (jnp.where(low, turned, pltpu.roll(right, NY, 1)), jnp.logical_or(low, group < groups - 1)),
            (jnp.where(low, pltpu.roll(left, NY, 1), turned), jnp.logical_or(lane >= NY, group > 0)),
        ),
        ((pltpu.roll(kappa, LANES - 1, 1), column < NY - 1), (pltpu.roll(kappa, 1, 1), column > 0)),
    )
    return [[(jnp.where(ok, 0.5 * (kappa + value), kappa), ok) for value, ok in pair] for pair in pairs]


def edge_rows(shape):
    core = this_core()
    row = lax.broadcasted_iota(jnp.int32, shape, 0)
    last = shape[0] - 1
    return row == core * last, row == (1 - core) * last


def z_shifts(tile):
    core = this_core()
    return 1 + core * (tile - 2), tile - 1 - core * (tile - 2)


def total_weight(weights):
    total = None
    for pair in weights:
        for weight, _ in pair:
            total = weight if total is None else total + weight
    return total


def layer_diagonal(kappa, ahead, behind):
    rows = kappa.shape[0]
    lane = lax.broadcasted_iota(jnp.int32, kappa.shape, 1)
    row = lax.broadcasted_iota(jnp.int32, kappa.shape, 0)
    column = lax.rem(lane, NY)
    turned = pltpu.roll(kappa, NY, 1)
    x_ahead = jnp.where(lane < NY, turned, pltpu.roll(turned, rows - 1, 0))
    x_behind = jnp.where(lane < NY, pltpu.roll(turned, 1, 0), turned)
    pairs = (
        (ahead, ahead > 0.0),
        (behind, behind > 0.0),
        (x_ahead, jnp.logical_or(lane < NY, row < rows - 1)),
        (x_behind, jnp.logical_or(lane >= NY, row > 0)),
        (pltpu.roll(kappa, LANES - 1, 1), column < NY - 1),
        (pltpu.roll(kappa, 1, 1), column > 0),
    )
    total = None
    for value, ok in pairs:
        weight = jnp.where(ok, 0.5 * (kappa + value), kappa)
        total = weight if total is None else total + weight
    return total


def cell_factors(diagonal, ratio):
    shifted = 1.0 + diagonal
    lifted = shifted * shifted - (ratio * ratio + beta_couple * gamma_couple)
    mix = shifted / (lifted + jnp.sqrt(lifted * lifted + shifted * shifted))
    inverse = 1.0 / (shifted + 0.5 * mix)
    return ratio * inverse, inverse, mix * inverse, 1.0 / shifted


def local_ends(values, decay, inverse, mixed, upright, steps):
    back = None
    last = None
    weight = None
    for step in reversed(range(steps)):
        state, adjoint = values(step)
        drive = inverse * adjoint - mixed * state
        back = drive if back is None else decay * back + drive
        term = state + 0.5 * back
        last = term if last is None else last + weight * term
        weight = decay if weight is None else weight * decay
    return back, last * upright


def solve_steps(values, decay, inverse, mixed, upright, ratio, back_in, state_in, steps, put):
    backs = [None] * steps
    back = back_in
    for step in reversed(range(steps)):
        state, adjoint = values(step)
        drive = inverse * adjoint - mixed * state
        back = drive if back is None else decay * back + drive
        backs[step] = back
    gain = ratio * mixed
    half_up = 0.5 * upright
    previous = state_in
    for step in range(steps):
        state, _ = values(step)
        current = upright * state + half_up * backs[step]
        adjoint = backs[step]
        if previous is not None:
            current = current + decay * previous
            adjoint = adjoint - gain * previous
        put(step, current, adjoint)
        previous = current
    return backs[0], previous


def pack_kernel(state, adjoint, kappa, keep, send, slab, edge, edge_send, layers, sems):
    steps_local, depth, cells = state.shape
    half = depth // 2
    core = this_core()
    mine = pl.ds(pl.multiple_of(core * half, 8), half)
    others = pl.ds(pl.multiple_of((1 - core) * half, 8), half)
    within = pl.ds(0, cells)
    copies = [pltpu.make_async_copy(kappa, slab, sems.at[4])]
    for field, source in enumerate((state, adjoint)):
        copies.append(pltpu.make_async_copy(source.at[:, mine, :], keep.at[field, :, :, within], sems.at[2 * field]))
        copies.append(pltpu.make_async_copy(source.at[:, others, :], send.at[field, :, :, within], sems.at[2 * field + 1]))
    for copy in copies:
        copy.start()

    def lay(source, rows, target):
        for group in range(cells // LANES):
            lanes = slice(group * LANES, (group + 1) * LANES)
            one, other = [source[row : row + 1, lanes] for row in rows]
            target[group : group + 1, :] = jnp.where(core == 0, one, other)

    copies[0].wait()
    last = depth - 1
    lay(slab, (0, last), edge.at[2 * steps_local])
    lay(slab, (1, last - 1), edge.at[2 * steps_local + 1])
    for slot, row in enumerate((0, half - 1, half, half + 1)):
        lay(slab, (row, last - row), layers.at[slot])
    for copy in copies[1:]:
        copy.wait()
    near, far = (0, half - 1), (half - 1, 0)
    beyond = pl.ds(cells, LANES)
    for index in range(steps_local):
        for field in range(2):
            slot = 2 * index + field
            lay(keep.at[field, index], near, edge.at[slot])
            lay(send.at[field, index], far, edge_send.at[slot])
            lay(send.at[field, index], near, keep.at[field, index, :, beyond])
            lay(keep.at[field, index], far, send.at[field, index, :, beyond])


def join_kernel(edge, edge_other, swap, both, swap_out):
    count = edge.shape[0]
    both[:count] = edge[...]
    both[count:] = edge_other[...]


def ends_kernel(side, ratio, chips, keep, other, slab, layers, *rest):
    cut = rest[0] if side == OUTER else None
    raw_ref, factor_ref, ends_ref = rest[-3:]
    steps_local, half, cells = keep.shape[1:]
    cells = cells - LANES
    steps = 2 * steps_local
    tile = half // 2
    groups = cells // LANES
    core = this_core()
    scales = step_scale(ratio, steps, chips, 1)
    own = pl.ds(pl.multiple_of((core if side == OUTER else 1 - core) * tile, 8), tile)
    places = []
    for position in range(2):
        sub = core if position == 0 else 1 - core
        for index in range(steps_local):
            scale = jnp.where(sub == 0, scales[index], scales[steps_local + index])
            places.append((position, index, sub * steps + 2 * index, scale))

    def work(diagonal, loads, stores):
        factors = cell_factors(diagonal, ratio)
        for slot, value in enumerate(factors):
            stores(factor_ref, slot, value)
        for position, index, slot, scale in places:
            for field in range(2):
                stores(raw_ref, slot + field, loads(position, index, field) * scale)

    def put_ends(here):
        factors = [factor_ref[slot, :, here] for slot in range(4)]
        values = lambda step: (raw_ref[2 * step, :, here], raw_ref[2 * step + 1, :, here])
        for slot, value in enumerate(local_ends(values, *factors, steps)):
            ends_ref[slot, :, here] = value

    def one(group, carry):
        here = lane_block(group * LANES)
        beyond = cut[steps, pl.ds(group, 1), :] if side == OUTER else None
        diagonal = total_weight(faces(side, slab, beyond, group, half))

        def stores(ref, slot, value):
            ref[slot, :, here] = value

        work(diagonal, lambda position, index, field: (keep, other)[position][field, index, own, here], stores)
        put_ends(here)
        return carry

    lax.fori_loop(0, groups, one, 0, unroll=UNROLL_ENDS)

    def stores_cut(ref, slot, value):
        for part in range(2):
            lanes = slice(cells + part * LANES, cells + (part + 1) * LANES)
            ref[slot, :, lanes] = value[part * tile : (part + 1) * tile]

    if side == OUTER:
        diagonal = layer_diagonal(cut[steps], layers[0], cut[steps + 1])
        starts = (steps + 2, 0)
        loads = lambda position, index, field: cut[starts[position] + 2 * index + field]
    else:
        diagonal = layer_diagonal(layers[2], layers[1], layers[3])
        loads = lambda position, index, field: (keep, other)[position][field, index, :, cells:]
    work(diagonal, loads, stores_cut)
    for part in range(2):
        put_ends(slice(cells + part * LANES, cells + (part + 1) * LANES))


def power_sum(value, count):
    total = None
    for _ in range(count):
        total = 1.0 if total is None else 1.0 + value * total
    return total


def response_of(decay, upright, steps):
    return (0.5 * upright) * decay * power_sum(decay * decay, steps)


def ring_factors(factors, steps, chips):
    decay, _, _, upright = factors
    block = power(decay, steps)
    return block, response_of(decay, upright, steps), 1.0 / (1.0 - power(block, chips))


def contribution(ends, offset, block, response, closing):
    back, last = ends
    square = block * block
    if offset == 0:
        up, down, cross = square * block, square * block, 1.0 + square + square * square * (1.0 + square)
    elif offset == 1:
        up, down, cross = None, square, block * (1.0 + square) * (1.0 + square)
    elif offset == 2:
        up, down, cross = block, block, 2.0 * square * (1.0 + square)
    else:
        up, down, cross = square, None, block * (1.0 + square) * (1.0 + square)
    entering_back = back if up is None else up * back
    entering_state = last if down is None else down * last
    entering_state = entering_state + (cross * response * closing) * back
    return closing * entering_back, closing * entering_state


def either(flag, one, other):
    return tuple(jnp.where(flag, a, b) for a, b in zip(one, other))


def relay_kernel(side, steps, factor_ref, mine, theirs, out):
    odd = lax.rem(this_chip(), 2) == 1

    def one(here):
        ring = ring_factors([factor_ref[slot, :, here] for slot in range(4)], steps, 4)
        a = (mine[0, :, here], mine[1, :, here])
        b = (theirs[0, :, here], theirs[1, :, here])
        if side == OUTER:
            one_part = contribution(a, 2, *ring)
            other_part = either(odd, contribution(b, 1, *ring), contribution(b, 3, *ring))
        else:
            one_part = either(odd, contribution(a, 1, *ring), contribution(a, 3, *ring))
            other_part = either(odd, contribution(b, 3, *ring), contribution(b, 1, *ring))
        out[0, :, here] = one_part[0] + other_part[0]
        out[1, :, here] = one_part[1] + other_part[1]

    each_block(mine.shape[2], 4 * LANES, one)


def entering(side, factors, ends, here, steps):
    if len(ends) == 1:
        return ends[0][0, :, here], ends[0][1, :, here]
    odd = lax.rem(this_chip(), 2) == 1
    mine, theirs, tail = ends
    ring = ring_factors(factors, steps, 4)
    own = contribution((mine[0, :, here], mine[1, :, here]), 0, *ring)
    b = (theirs[0, :, here], theirs[1, :, here])
    if side == OUTER:
        near_by = either(odd, contribution(b, 3, *ring), contribution(b, 1, *ring))
    else:
        near_by = contribution(b, 2, *ring)
    return own[0] + near_by[0] + tail[0, :, here], own[1] + near_by[1] + tail[1, :, here]


def sweep_kernel(side, ratio, raw_ref, factor_ref, *rest):
    *ends, first_ref, turned_ref, layer_ref = rest
    tile = raw_ref.shape[1]
    steps = raw_ref.shape[0] // 2
    cells = first_ref.shape[2]

    def sweep(put, here):
        factors = [factor_ref[slot, :, here] for slot in range(4)]
        values = lambda step: (raw_ref[2 * step, :, here], raw_ref[2 * step + 1, :, here])
        solve_steps(values, *factors, ratio, *entering(side, factors, ends, here, steps), steps, put)

    def own(here):
        def put(step, state, adjoint):
            for field, value in enumerate((state, adjoint)):
                slot = 2 * step + field
                first_ref[slot, :, here] = value
                turned_ref[slot, :, here] = turned(value)

        sweep(put, here)

    each_block(cells, 2 * LANES, own)

    def put_layer(step, state, adjoint):
        for field, value in enumerate((state, adjoint)):
            for part in range(2):
                layer_ref[2 * step + field, part * tile : (part + 1) * tile, :] = value[:, part * LANES : (part + 1) * LANES]

    sweep(put_layer, slice(cells, cells + 2 * LANES))


def turned(value):
    parts = [pltpu.roll(value[:, i : i + LANES], NY, 1) for i in range(0, value.shape[1], LANES)]
    return parts[0] if len(parts) == 1 else jnp.concatenate(parts, axis=1)


def couplings_kernel(side, first_ref, turned_ref, next_ref, layer_ref, slab, velocity_ref, factor_ref, *rest):
    coupled_ref, ends_ref = rest[-2:]
    slots, tile, cells = first_ref.shape
    steps = slots // 2
    depth = slab.shape[0]
    half = 2 * tile
    groups = cells // LANES
    core = this_core()
    own = pl.ds(pl.multiple_of(tile_rows(side, half, depth), 8), tile)
    out_shift, in_shift = z_shifts(tile)

    def one(group, carry):
        here = lane_block(group * LANES)
        left = lane_block(jnp.maximum(group - 1, 0) * LANES)
        right = lane_block(jnp.minimum(group + 1, groups - 1) * LANES)
        row = pl.ds(group, 1)
        beyond = rest[0][steps, row, :] if side == OUTER else None
        weights = faces(side, slab, beyond, group, half)
        lane = lax.broadcasted_iota(jnp.int32, (tile, LANES), 1)
        low = lane < NY
        first, last = edge_rows((tile, LANES))
        drifts = [0.5 * velocity_ref[component, own, here] for component in (2, 0, 1)]
        drifts[0] = jnp.where(core == 0, -drifts[0], drifts[0])
        tables = []
        for sign in (1.0, -1.0):
            one_way, other_way = [], []
            for ((ahead, ok_ahead), (behind, ok_behind)), drift in zip(weights, drifts):
                one_way.append(jnp.where(ok_ahead, ahead - sign * drift, 0.0))
                other_way.append(jnp.where(ok_behind, behind + sign * drift, 0.0))
            x_same = jnp.where(low, one_way[1], other_way[1])
            x_next = jnp.where(low, other_way[1], one_way[1])
            tables.append((one_way[0], other_way[0], x_same, x_next, one_way[2], other_way[2]))
        factors = [factor_ref[slot, :, here] for slot in range(4)]

        def values(step):
            results = []
            for field in range(2):
                slot = 2 * step + field
                c_out, c_in, x_same, x_next, c_ahead, c_behind = tables[field]
                value = first_ref[slot, :, here]
                following = next_ref[slot, :, here]
                cut = layer_ref[slot, row, :]
                if side == OUTER:
                    outward = jnp.where(first, cut, pltpu.roll(value, out_shift, 0))
                    inward = pltpu.roll(jnp.where(first, following, value), in_shift, 0)
                else:
                    outward = pltpu.roll(jnp.where(last, following, value), out_shift, 0)
                    inward = jnp.where(last, cut, pltpu.roll(value, in_shift, 0))
                result = c_out * outward + c_in * inward
                beside = jnp.where(low, turned_ref[slot, :, left], turned_ref[slot, :, right])
                result = result + (x_same * turned_ref[slot, :, here] + x_next * beside)
                result = result + (c_ahead * pltpu.roll(value, LANES - 1, 1) + c_behind * pltpu.roll(value, 1, 1))
                coupled_ref[slot, :, here] = result
                results.append(result)
            return results

        for slot, value in enumerate(local_ends(values, *factors, steps)):
            ends_ref[slot, :, here] = value
        return carry

    lax.fori_loop(0, groups, one, 0, unroll=UNROLL_COUPLINGS)


def finish_factors(ratio, factors):
    decay, _, mixed, upright = factors
    return decay, ratio * mixed, 0.5 * upright


def parts_kernel(ratio, outer, outer_first, outer_factors, inner, inner_first, inner_factors, *rest):
    keep, send, middle = rest[-3:]
    steps_local = keep.shape[0] // 2
    tile, cells = outer.shape[1:]
    core = this_core()
    for side, (coupled_ref, first_ref, factor_ref) in enumerate(
        ((outer, outer_first, outer_factors), (inner, inner_first, inner_factors))
    ):
        rows = slice(side * tile, (side + 1) * tile)

        def one(here):
            factors = [factor_ref[slot, :, here] for slot in range(4)]
            for slot, value in enumerate(finish_factors(ratio, factors)):
                send[2 * steps_local + slot, rows, here] = value
            results = {}
            for sub in range(2):
                offset = 2 * steps_local * sub

                def values(step):
                    return coupled_ref[offset + 2 * step, :, here], coupled_ref[offset + 2 * step + 1, :, here]

                def put(step, state, adjoint):
                    results[sub, step] = (state, adjoint)

                back, last = solve_steps(values, *factors, ratio, None, None, steps_local, put)
                middle[1 - sub, rows, here] = last if sub == 0 else back
            for step in range(steps_local):
                for field in range(2):
                    early, late = [
                        first_ref[2 * steps_local * sub + 2 * step + field, :, here] + results[sub, step][field]
                        for sub in range(2)
                    ]
                    slot = 2 * step + field
                    keep[slot, rows, here] = jnp.where(core == 0, early, late)
                    send[slot, rows, here] = jnp.where(core == 0, late, early)

        each_block(cells, 2 * LANES, one)


def carry_kernel(side, steps_local, factor_ref, middle, *rest):
    *ends, keep, send = rest
    tile, cells = keep.shape[1:]
    rows = slice(side * tile, (side + 1) * tile)
    core = this_core()

    def one(here):
        factors = [factor_ref[slot, :, here] for slot in range(4)]
        decay, _, _, upright = factors
        back, state = entering(side, factors, ends, here, 2 * steps_local)
        block = power(decay, steps_local)
        early_back = middle[0, rows, here] + block * back
        late_state = middle[1, rows, here] + block * state + response_of(decay, upright, steps_local) * early_back
        for slot, (early, late) in enumerate(((early_back, back), (state, late_state))):
            keep[slot, :, here] = jnp.where(core == 0, early, late)
            send[slot, :, here] = jnp.where(core == 0, late, early)

    each_block(cells, 4 * LANES, one)


def finish_kernel(theirs, ratio, chips, parts, *rest):
    state_out, adjoint_out, result, sems = rest[-4:]
    tile, cells = rest[0].shape[1:]
    steps_local, depth = state_out.shape[:2]
    core = this_core()
    whole = step_scale(ratio, 2 * steps_local, chips, -1)
    scales = [jnp.where(core == 0, whole[step], whole[steps_local + step]) for step in range(steps_local)]
    copies = []
    for side in (OUTER, INNER):
        entered = rest[side]
        held = slice(side * tile, (side + 1) * tile)
        start = tile_rows(side, 2 * tile, depth)
        rows = pl.ds(pl.multiple_of(depth - tile - start if theirs else start, 8), tile)

        def one(here):
            if theirs:
                decay, gain, half_up = [parts[2 * steps_local + slot, held, here] for slot in range(3)]
            else:
                decay, gain, half_up = finish_factors(ratio, [rest[2 + side][slot, :, here] for slot in range(4)])
            backs = [entered[0, :, here]]
            for _ in range(steps_local):
                backs.append(decay * backs[-1])
            backs = backs[:0:-1]
            previous = entered[1, :, here]
            for step in range(steps_local):
                current = decay * previous + half_up * backs[step]
                adjoint = backs[step] - gain * previous
                result[side, 0, step, :, here] = (parts[2 * step, held, here] + current) * scales[step]
                result[side, 1, step, :, here] = (parts[2 * step + 1, held, here] + adjoint) * scales[step]
                previous = current

        each_block(cells, 4 * LANES, one)
        for field, out in enumerate((state_out, adjoint_out)):
            copies.append(pltpu.make_async_copy(result.at[side, field], out.at[:, rows, :], sems.at[side, field]))
            copies[-1].start()
    for copy in copies:
        copy.wait()


def body(state_rhs, adjoint_rhs, diffusivity, velocity):
    steps_local, depth, cells = state_rhs.shape
    ranks = lax.axis_size("tm")
    slabs = lax.axis_size("gz")
    chips = ranks // 2
    total = steps_local * ranks
    steps = 2 * steps_local
    half = depth // 2
    tile = half // 2
    groups = cells // LANES
    wide = cells + 2 * LANES
    ratio = alpha_wrap ** (1.0 / total)
    core = this_core()
    f32 = jnp.float32
    anywhere = pl.BlockSpec(memory_space=pl.ANY)
    vmem = pl.BlockSpec(memory_space=pltpu.VMEM)

    def partner(value, mask):
        return lax.ppermute(value, "tm", [(i, i ^ mask) for i in range(ranks)])

    def outward(value):
        pairs = []
        for t in range(ranks):
            for g in range(slabs):
                to = g - 1 if t % 2 == 0 else g + 1
                if 0 <= to < slabs:
                    pairs.append((t * slabs + g, (t ^ 1) * slabs + to))
        return lax.ppermute(value, ("tm", "gz"), pairs)

    def call(kernel, name, out_shape, *args, **kwargs):
        shapes = [jax.ShapeDtypeStruct(s, f32) for s in out_shape]
        micros = next(value for word, value in MICROSECONDS.items() if word in name)
        return pl.pallas_call(
            kernel,
            out_shape=shapes,
            compiler_params=pltpu.CompilerParams(vmem_limit_bytes=32 * 1024 * 1024),
            cost_estimate=pl.CostEstimate(flops=0, transcendentals=0, bytes_accessed=int(micros * 3.7e6)),
            name=name,
            **kwargs,
        )(*args)

    layer = (groups, LANES)
    halves = (2, steps_local, half, cells + LANES)
    keep, send, slab, edge, edge_send, layers = call(
        pack_kernel,
        "halves_and_layers",
        [halves, halves, (depth, cells), (steps + 2,) + layer, (steps,) + layer, (4,) + layer],
        *[pltpu.with_memory_space_constraint(x, pltpu.HBM) for x in (state_rhs, adjoint_rhs, diffusivity)],
        in_specs=[anywhere] * 3,
        scratch_shapes=[pltpu.SemaphoreType.DMA((5,))],
    )
    cut, send = call(
        join_kernel,
        "outermost_layer",
        [(2 * steps + 2,) + layer, halves],
        edge,
        partner(edge_send, 1),
        send,
        in_specs=[vmem, vmem, anywhere],
        out_specs=[vmem, anywhere],
        input_output_aliases={2: 1},
    )
    other = partner(send, 1)
    cut = outward(cut)

    def first_ends(side, *args):
        return call(
            functools.partial(ends_kernel, side, ratio, chips),
            ("outer", "inner")[side] + "_ends",
            [(2 * steps, tile, wide), (4, tile, wide), (2, tile, wide)],
            keep,
            other,
            slab,
            layers,
            *args,
        )

    inner_raw, inner_factors, inner_ends = first_ends(INNER)
    outer_raw, outer_factors, outer_ends = first_ends(OUTER, cut, inner_ends)

    def exchange(side, mine, factors):
        width = mine.shape[2]
        if chips != 4:
            gathered = lax.dynamic_index_in_dim(
                lax.all_gather(mine, "tm").reshape((chips, 2) + mine.shape), core, 1, keepdims=False
            )
            block, response, closing = ring_factors([factors[i, :, :width] for i in range(4)], steps, chips)
            at = lambda array, index: lax.dynamic_index_in_dim(array, lax.rem(index + 2 * chips, chips), 0, keepdims=False)
            chip = this_chip()

            def entering_back(where):
                value = jnp.zeros((tile, width), f32)
                for offset in reversed(range(chips)):
                    value = block * value + at(gathered[:, 0], where + 1 + offset)
                return value * closing

            value = jnp.zeros((tile, width), f32)
            for offset in reversed(range(chips)):
                source = chip - 1 - offset
                value = block * value + at(gathered[:, 1], source) + response * entering_back(source)
            return [jnp.stack([entering_back(chip), value * closing])]
        masks = (2, 4) if side == OUTER else (4, 2)
        theirs = partner(mine, masks[0])
        (passed,) = call(
            functools.partial(relay_kernel, side, steps),
            ("outer", "inner")[side] + "_relay",
            [mine.shape],
            factors,
            mine,
            theirs,
        )
        return [mine, theirs, partner(passed, masks[1])]

    def first_sweep(side, raw, factors, ends):
        return call(
            functools.partial(sweep_kernel, side, ratio),
            ("outer", "inner")[side] + "_first_sweep",
            [(2 * steps, tile, cells)] * 2 + [(2 * steps,) + layer],
            raw,
            factors,
            *ends,
        )

    inner_first, inner_turned, inner_layer = first_sweep(
        INNER, inner_raw, inner_factors, exchange(INNER, inner_ends, inner_factors)
    )
    outer_first, outer_turned, outer_layer = first_sweep(
        OUTER, outer_raw, outer_factors, exchange(OUTER, outer_ends, outer_factors)
    )

    def couplings(side, *args):
        return call(
            functools.partial(couplings_kernel, side),
            ("outer", "inner")[side] + "_couplings",
            [(2 * steps, tile, cells), (2, tile, cells)],
            *args,
        )

    inner_coupled, inner_ends = couplings(
        INNER, inner_first, inner_turned, outer_first, inner_layer, slab, velocity, inner_factors
    )
    outer_coupled, outer_ends = couplings(
        OUTER, outer_first, outer_turned, inner_first, outer_layer, slab, velocity, outer_factors, cut
    )
    inner_entered = exchange(INNER, inner_ends, inner_factors)
    outer_entered = exchange(OUTER, outer_ends, outer_factors)
    keep, send, middle = call(
        functools.partial(parts_kernel, ratio),
        "own_steps",
        [(steps, half, cells), (steps + 3, half, cells), (2, half, cells)],
        outer_coupled,
        outer_first,
        outer_factors,
        inner_coupled,
        inner_first,
        inner_factors,
    )
    other = partner(send, 1)

    def enter(side, entered, factors):
        keep_in, send_in = call(
            functools.partial(carry_kernel, side, steps_local),
            ("outer", "inner")[side] + "_entering",
            [(2, tile, cells)] * 2,
            factors,
            middle,
            *entered,
        )
        return keep_in, partner(send_in, 1)

    def finish(theirs, results, *args):
        return call(
            functools.partial(finish_kernel, theirs, ratio, chips),
            ("finish_own", "finish_other")[theirs],
            [(steps_local, depth, cells)] * 2,
            *args,
            *results,
            in_specs=[vmem] * len(args) + [anywhere] * len(results),
            out_specs=[anywhere] * 2,
            scratch_shapes=[pltpu.VMEM((2, 2, steps_local, tile, cells), f32), pltpu.SemaphoreType.DMA((2, 2))],
            input_output_aliases={len(args) + i: i for i in range(len(results))},
        )

    outer_own, outer_other = enter(OUTER, outer_entered, outer_factors)
    inner_own, inner_other = enter(INNER, inner_entered, inner_factors)
    results = finish(False, (), keep, outer_own, inner_own, outer_factors, inner_factors)
    return finish(True, results, other, outer_other, inner_other)


def solution(mesh):
    placed = (P("tm", "gz", None), P("tm", "gz", None), P("gz", None), P(None, "gz", None))
    return jax.shard_map(
        body,
        mesh=mesh,
        in_specs=placed,
        out_specs=(P("tm", "gz", None), P("tm", "gz", None)),
        check_vma=False,
    )
```

```python
import functools
import math

import jax
import jax.numpy as jnp
from jax import lax
from jax.experimental import pallas as pl
from jax.experimental.pallas import tpu as pltpu
from jax.sharding import PartitionSpec as P

NY = 64
LANES = 128

alpha_wrap = 0.1
beta_couple = 0.5
gamma_couple = 0.5


def this_core():
    return lax.rem(lax.axis_index("tm"), 2)


def this_chip():
    return lax.div(lax.axis_index("tm"), 2)


def lane_block(start, width=LANES):
    return pl.ds(pl.multiple_of(start, LANES), width)


def each_block(cells, width, work):
    def one(index, carry):
        work(lane_block(index * width, width))
        return carry

    lax.fori_loop(0, cells // width, one, 0)
    if cells % width:
        work(slice(cells - cells % width, cells))


def power(value, count):
    result = None
    while count:
        if count & 1:
            result = value if result is None else result * value
        count >>= 1
        if count:
            value = value * value
    return result


def step_scale(ratio, steps, chips, sign):
    chip = this_chip()
    base = jnp.float32(1.0)
    bit = 0
    while 1 << bit < chips:
        factor = ratio ** (sign * steps * (1 << bit))
        base = base * jnp.where(lax.rem(lax.div(chip, 1 << bit), 2) == 1, factor, 1.0)
        bit += 1
    return [base * (ratio ** (sign * step)) for step in range(steps)]


OUTER, INNER = 0, 1
MICROSECONDS = {
    'halves': 2,
    'outermost': 0.3,
    'ends': 1,
    'relay': 0.2,
    'first_sweep': 1.1,
    'couplings': 3,
    'entering': 0.2,
    'finish_own': 1.2,
    'finish_other': 1.2,
}
UNROLL_ENDS = 8
UNROLL_COUPLINGS = 2


def tile_rows(side, half, depth):
    core = this_core()
    tile = half // 2
    return core * (depth - tile) if side == OUTER else tile + core * tile


def faces(side, slab, outer, group, half):
    core = this_core()
    depth, cells = slab.shape
    tile = half // 2
    groups = cells // LANES
    own = pl.ds(pl.multiple_of(tile_rows(side, half, depth), 8), tile)
    here = lane_block(group * LANES)
    kappa = slab[own, here]
    left = slab[own, lane_block(jnp.maximum(group - 1, 0) * LANES)]
    right = slab[own, lane_block(jnp.minimum(group + 1, groups - 1) * LANES)]
    mirrored = lambda row: jnp.where(core == 0, slab[row : row + 1, here], slab[depth - 1 - row : depth - row, here])
    outward = outer if side == OUTER else mirrored(tile - 1)
    inward = mirrored(tile if side == OUTER else half)
    first, last = edge_rows(kappa.shape)
    shift, back = z_shifts(tile)
    lane = lax.broadcasted_iota(jnp.int32, kappa.shape, 1)
    column = lax.rem(lane, NY)
    low = lane < NY
    turned = pltpu.roll(kappa, NY, 1)
    outward = jnp.where(first, outward, pltpu.roll(kappa, shift, 0))
    inward = jnp.where(last, inward, pltpu.roll(kappa, back, 0))
    pairs = (
        ((outward, outward > 0.0), (inward, inward > 0.0)),
        (
            (jnp.where(low, turned, pltpu.roll(right, NY, 1)), jnp.logical_or(low, group < groups - 1)),
            (jnp.where(low, pltpu.roll(left, NY, 1), turned), jnp.logical_or(lane >= NY, group > 0)),
        ),
        ((pltpu.roll(kappa, LANES - 1, 1), column < NY - 1), (pltpu.roll(kappa, 1, 1), column > 0)),
    )
    return [[(jnp.where(ok, 0.5 * (kappa + value), kappa), ok) for value, ok in pair] for pair in pairs]


def edge_rows(shape):
    core = this_core()
    row = lax.broadcasted_iota(jnp.int32, shape, 0)
    last = shape[0] - 1
    return row == core * last, row == (1 - core) * last


def z_shifts(tile):
    core = this_core()
    return 1 + core * (tile - 2), tile - 1 - core * (tile - 2)


def total_weight(weights):
    total = None
    for pair in weights:
        for weight, _ in pair:
            total = weight if total is None else total + weight
    return total


def layer_diagonal(kappa, ahead, behind):
    rows = kappa.shape[0]
    lane = lax.broadcasted_iota(jnp.int32, kappa.shape, 1)
    row = lax.broadcasted_iota(jnp.int32, kappa.shape, 0)
    column = lax.rem(lane, NY)
    turned = pltpu.roll(kappa, NY, 1)
    x_ahead = jnp.where(lane < NY, turned, pltpu.roll(turned, rows - 1, 0))
    x_behind = jnp.where(lane < NY, pltpu.roll(turned, 1, 0), turned)
    pairs = (
        (ahead, ahead > 0.0),
        (behind, behind > 0.0),
        (x_ahead, jnp.logical_or(lane < NY, row < rows - 1)),
        (x_behind, jnp.logical_or(lane >= NY, row > 0)),
        (pltpu.roll(kappa, LANES - 1, 1), column < NY - 1),
        (pltpu.roll(kappa, 1, 1), column > 0),
    )
    total = None
    for value, ok in pairs:
        weight = jnp.where(ok, 0.5 * (kappa + value), kappa)
        total = weight if total is None else total + weight
    return total


def cell_factors(diagonal, ratio):
    shifted = 1.0 + diagonal
    lifted = shifted * shifted - (ratio * ratio + beta_couple * gamma_couple)
    mix = shifted / (lifted + jnp.sqrt(lifted * lifted + shifted * shifted))
    inverse = 1.0 / (shifted + 0.5 * mix)
    return ratio * inverse, inverse, mix * inverse, 1.0 / shifted


def local_ends(values, decay, inverse, mixed, upright, steps):
    back = None
    last = None
    weight = None
    for step in reversed(range(steps)):
        state, adjoint = values(step)
        drive = inverse * adjoint - mixed * state
        back = drive if back is None else decay * back + drive
        term = state + 0.5 * back
        last = term if last is None else last + weight * term
        weight = decay if weight is None else weight * decay
    return back, last * upright


def solve_steps(values, decay, inverse, mixed, upright, ratio, back_in, state_in, steps, put):
    backs = [None] * steps
    back = back_in
    for step in reversed(range(steps)):
        state, adjoint = values(step)
        drive = inverse * adjoint - mixed * state
        back = drive if back is None else decay * back + drive
        backs[step] = back
    gain = ratio * mixed
    half_up = 0.5 * upright
    previous = state_in
    for step in range(steps):
        state, _ = values(step)
        current = upright * state + half_up * backs[step]
        adjoint = backs[step]
        if previous is not None:
            current = current + decay * previous
            adjoint = adjoint - gain * previous
        put(step, current, adjoint)
        previous = current
    return backs[0], previous


def pack_kernel(state, adjoint, kappa, keep, send, slab, edge, edge_send, layers, sems):
    steps_local, depth, cells = state.shape
    half = depth // 2
    core = this_core()
    mine = pl.ds(pl.multiple_of(core * half, 8), half)
    others = pl.ds(pl.multiple_of((1 - core) * half, 8), half)
    within = pl.ds(0, cells)
    copies = [pltpu.make_async_copy(kappa, slab, sems.at[4])]
    for field, source in enumerate((state, adjoint)):
        copies.append(pltpu.make_async_copy(source.at[:, mine, :], keep.at[field, :, :, within], sems.at[2 * field]))
        copies.append(pltpu.make_async_copy(source.at[:, others, :], send.at[field, :, :, within], sems.at[2 * field + 1]))
    for copy in copies:
        copy.start()

    def lay(source, rows, target):
        for group in range(cells // LANES):
            lanes = slice(group * LANES, (group + 1) * LANES)
            one, other = [source[row : row + 1, lanes] for row in rows]
            target[group : group + 1, :] = jnp.where(core == 0, one, other)

    copies[0].wait()
    last = depth - 1
    lay(slab, (0, last), edge.at[2 * steps_local])
    lay(slab, (1, last - 1), edge.at[2 * steps_local + 1])
    for slot, row in enumerate((0, half - 1, half, half + 1)):
        lay(slab, (row, last - row), layers.at[slot])
    for copy in copies[1:]:
        copy.wait()
    near, far = (0, half - 1), (half - 1, 0)
    beyond = pl.ds(cells, LANES)
    for index in range(steps_local):
        for field in range(2):
            slot = 2 * index + field
            lay(keep.at[field, index], near, edge.at[slot])
            lay(send.at[field, index], far, edge_send.at[slot])
            lay(send.at[field, index], near, keep.at[field, index, :, beyond])
            lay(keep.at[field, index], far, send.at[field, index, :, beyond])


def join_kernel(edge, edge_other, swap, both, swap_out):
    count = edge.shape[0]
    both[:count] = edge[...]
    both[count:] = edge_other[...]


def ends_kernel(side, ratio, chips, keep, other, slab, layers, *rest):
    cut = rest[0] if side == OUTER else None
    raw_ref, factor_ref, ends_ref = rest[-3:]
    steps_local, half, cells = keep.shape[1:]
    cells = cells - LANES
    steps = 2 * steps_local
    tile = half // 2
    groups = cells // LANES
    core = this_core()
    scales = step_scale(ratio, steps, chips, 1)
    own = pl.ds(pl.multiple_of((core if side == OUTER else 1 - core) * tile, 8), tile)
    places = []
    for position in range(2):
        sub = core if position == 0 else 1 - core
        for index in range(steps_local):
            scale = jnp.where(sub == 0, scales[index], scales[steps_local + index])
            places.append((position, index, sub * steps + 2 * index, scale))

    def work(diagonal, loads, stores):
        factors = cell_factors(diagonal, ratio)
        for slot, value in enumerate(factors):
            stores(factor_ref, slot, value)
        for position, index, slot, scale in places:
            for field in range(2):
                stores(raw_ref, slot + field, loads(position, index, field) * scale)

    def put_ends(here):
        factors = [factor_ref[slot, :, here] for slot in range(4)]
        values = lambda step: (raw_ref[2 * step, :, here], raw_ref[2 * step + 1, :, here])
        for slot, value in enumerate(local_ends(values, *factors, steps)):
            ends_ref[slot, :, here] = value

    def one(group, carry):
        here = lane_block(group * LANES)
        beyond = cut[steps, pl.ds(group, 1), :] if side == OUTER else None
        diagonal = total_weight(faces(side, slab, beyond, group, half))

        def stores(ref, slot, value):
            ref[slot, :, here] = value

        work(diagonal, lambda position, index, field: (keep, other)[position][field, index, own, here], stores)
        put_ends(here)
        return carry

    lax.fori_loop(0, groups, one, 0, unroll=UNROLL_ENDS)

    def stores_cut(ref, slot, value):
        for part in range(2):
            lanes = slice(cells + part * LANES, cells + (part + 1) * LANES)
            ref[slot, :, lanes] = value[part * tile : (part + 1) * tile]

    if side == OUTER:
        diagonal = layer_diagonal(cut[steps], layers[0], cut[steps + 1])
        starts = (steps + 2, 0)
        loads = lambda position, index, field: cut[starts[position] + 2 * index + field]
    else:
        diagonal = layer_diagonal(layers[2], layers[1], layers[3])
        loads = lambda position, index, field: (keep, other)[position][field, index, :, cells:]
    work(diagonal, loads, stores_cut)
    for part in range(2):
        put_ends(slice(cells + part * LANES, cells + (part + 1) * LANES))


def power_sum(value, count):
    total = None
    for _ in range(count):
        total = 1.0 if total is None else 1.0 + value * total
    return total


def response_of(decay, upright, steps):
    return (0.5 * upright) * decay * power_sum(decay * decay, steps)


def ring_factors(factors, steps, chips):
    decay, _, _, upright = factors
    block = power(decay, steps)
    return block, response_of(decay, upright, steps), 1.0 / (1.0 - power(block, chips))


def choose(flag, one, other):
    return tuple(jnp.where(flag, a, b) for a, b in zip(one, other))


def ring_weights(factors, steps):
    block, response, closing = ring_factors(factors, steps, 4)
    square = block * block
    cross = response * closing * closing
    near = cross * block * (1.0 + square) * (1.0 + square)
    once = closing * block
    twice = closing * square
    thrice = once * square
    return (
        (thrice, thrice, cross * (1.0 + square) * (1.0 + square * square)),
        (closing, twice, near),
        (once, once, 2.0 * cross * square * (1.0 + square)),
        (twice, closing, near),
    )


def weighted(weights, ends):
    back, last = ends
    return weights[0] * back, weights[1] * last + weights[2] * back


def relay_kernel(steps, factor_ref, mine, theirs, passed):
    odd = lax.rem(this_chip(), 2) == 1
    along_x = this_core() == 0

    def one(here):
        _, next_, across, before = ring_weights([factor_ref[slot, :, here] for slot in range(4)], steps)
        beside = choose(odd, next_, before)
        a = weighted(choose(along_x, across, beside), (mine[0, :, here], mine[1, :, here]))
        b = weighted(choose(along_x, beside, choose(odd, before, next_)), (theirs[0, :, here], theirs[1, :, here]))
        passed[0, :, here] = a[0] + b[0]
        passed[1, :, here] = a[1] + b[1]

    each_block(mine.shape[2], 4 * LANES, one)


def entering(factors, ends, here, steps):
    if len(ends) == 1:
        return ends[0][0, :, here], ends[0][1, :, here]
    mine, theirs, tail = ends
    own, next_, across, before = ring_weights(factors, steps)
    odd = lax.rem(this_chip(), 2) == 1
    along_x = this_core() == 0
    a = weighted(own, (mine[0, :, here], mine[1, :, here]))
    b = weighted(choose(along_x, choose(odd, before, next_), across), (theirs[0, :, here], theirs[1, :, here]))
    return a[0] + b[0] + tail[0, :, here], a[1] + b[1] + tail[1, :, here]


def sweep_kernel(ratio, raw_ref, factor_ref, *rest):
    *ends, first_ref, turned_ref, layer_ref = rest
    tile = raw_ref.shape[1]
    steps = raw_ref.shape[0] // 2
    cells = first_ref.shape[2]

    def sweep(put, here):
        factors = [factor_ref[slot, :, here] for slot in range(4)]
        values = lambda step: (raw_ref[2 * step, :, here], raw_ref[2 * step + 1, :, here])
        solve_steps(values, *factors, ratio, *entering(factors, ends, here, steps), steps, put)

    def own(here):
        def put(step, state, adjoint):
            for field, value in enumerate((state, adjoint)):
                slot = 2 * step + field
                first_ref[slot, :, here] = value
                turned_ref[slot, :, here] = turned(value)

        sweep(put, here)

    each_block(cells, 2 * LANES, own)

    def put_layer(step, state, adjoint):
        for field, value in enumerate((state, adjoint)):
            for part in range(2):
                layer_ref[2 * step + field, part * tile : (part + 1) * tile, :] = value[:, part * LANES : (part + 1) * LANES]

    sweep(put_layer, slice(cells, cells + 2 * LANES))


def turned(value):
    parts = [pltpu.roll(value[:, i : i + LANES], NY, 1) for i in range(0, value.shape[1], LANES)]
    return parts[0] if len(parts) == 1 else jnp.concatenate(parts, axis=1)


def couplings_kernel(ratio, slab, velocity_ref, cut_ref, *refs):
    *results, outer_ends, inner_ends = refs[-5:]
    outer, inner = refs[:4], refs[4:8]
    work = functools.partial(couple_tile, ratio, slab, velocity_ref, cut_ref)
    work(OUTER, *outer, inner[0], *results, outer_ends)
    work(INNER, *inner, outer[0], *results, inner_ends)


def couple_tile(ratio, slab, velocity_ref, cut_ref, side, first_ref, turned_ref, layer_ref, factor_ref, next_ref, keep, send, middle, ends_ref):
    slots, tile, cells = first_ref.shape
    steps = slots // 2
    steps_local = steps // 2
    depth = slab.shape[0]
    half = 2 * tile
    groups = cells // LANES
    core = this_core()
    own = pl.ds(pl.multiple_of(tile_rows(side, half, depth), 8), tile)
    held = slice(side * tile, (side + 1) * tile)
    out_shift, in_shift = z_shifts(tile)

    def one(group, carry):
        here = lane_block(group * LANES)
        left = lane_block(jnp.maximum(group - 1, 0) * LANES)
        right = lane_block(jnp.minimum(group + 1, groups - 1) * LANES)
        row = pl.ds(group, 1)
        beyond = cut_ref[steps, row, :] if side == OUTER else None
        weights = faces(side, slab, beyond, group, half)
        lane = lax.broadcasted_iota(jnp.int32, (tile, LANES), 1)
        low = lane < NY
        first, last = edge_rows((tile, LANES))
        drifts = [0.5 * velocity_ref[component, own, here] for component in (2, 0, 1)]
        drifts[0] = jnp.where(core == 0, -drifts[0], drifts[0])
        tables = []
        for sign in (1.0, -1.0):
            one_way, other_way = [], []
            for ((ahead, ok_ahead), (behind, ok_behind)), drift in zip(weights, drifts):
                one_way.append(jnp.where(ok_ahead, ahead - sign * drift, 0.0))
                other_way.append(jnp.where(ok_behind, behind + sign * drift, 0.0))
            x_same = jnp.where(low, one_way[1], other_way[1])
            x_next = jnp.where(low, other_way[1], one_way[1])
            tables.append((one_way[0], other_way[0], x_same, x_next, one_way[2], other_way[2]))
        factors = [factor_ref[slot, :, here] for slot in range(4)]

        def coupled(slot):
            c_out, c_in, x_same, x_next, c_ahead, c_behind = tables[slot % 2]
            value = first_ref[slot, :, here]
            following = next_ref[slot, :, here]
            cut = layer_ref[slot, row, :]
            if side == OUTER:
                outward = jnp.where(first, cut, pltpu.roll(value, out_shift, 0))
                inward = pltpu.roll(jnp.where(first, following, value), in_shift, 0)
            else:
                outward = pltpu.roll(jnp.where(last, following, value), out_shift, 0)
                inward = jnp.where(last, cut, pltpu.roll(value, in_shift, 0))
            result = c_out * outward + c_in * inward
            beside = jnp.where(low, turned_ref[slot, :, left], turned_ref[slot, :, right])
            result = result + (x_same * turned_ref[slot, :, here] + x_next * beside)
            return result + (c_ahead * pltpu.roll(value, LANES - 1, 1) + c_behind * pltpu.roll(value, 1, 1))

        results = {}
        ends = []
        for sub in range(2):
            offset = 2 * steps_local * sub
            drives = [coupled(offset + slot) for slot in range(2 * steps_local)]

            def put(step, state, adjoint):
                results[sub, step] = (state, adjoint)

            values = lambda step: (drives[2 * step], drives[2 * step + 1])
            ends.append(solve_steps(values, *factors, ratio, None, None, steps_local, put))
        for step in range(steps_local):
            for field in range(2):
                slot = 2 * step + field
                early, late = [
                    first_ref[2 * steps_local * sub + slot, :, here] + results[sub, step][field] for sub in range(2)
                ]
                keep[slot, held, here] = jnp.where(core == 0, early, late)
                send[slot, held, here] = jnp.where(core == 0, late, early)
        for slot, value in enumerate(finish_factors(ratio, factors)):
            send[2 * steps_local + slot, held, here] = value
        (early_back, early_last), (late_back, late_last) = ends
        decay, _, _, upright = factors
        block = power(decay, steps_local)
        middle[0, held, here] = late_back
        middle[1, held, here] = early_last
        ends_ref[0, :, here] = early_back + block * late_back
        ends_ref[1, :, here] = late_last + block * (early_last + response_of(decay, upright, steps_local) * late_back)
        return carry

    lax.fori_loop(0, groups, one, 0, unroll=UNROLL_COUPLINGS)


def finish_factors(ratio, factors):
    decay, _, mixed, upright = factors
    return decay, ratio * mixed, 0.5 * upright


def carry_kernel(steps_local, middle, outer_factors, inner_factors, *rest):
    *ends, keep, send = rest
    half, cells = middle.shape[1:]
    tile = half // 2
    core = this_core()
    for side, factor_ref in enumerate((outer_factors, inner_factors)):
        held = slice(side * tile, (side + 1) * tile)

        def one(here):
            factors = [factor_ref[slot, :, here] for slot in range(4)]
            decay, _, _, upright = factors
            back, state = entering(factors, ends[side * len(ends) // 2 : (side + 1) * len(ends) // 2], here, 2 * steps_local)
            block = power(decay, steps_local)
            early_back = middle[0, held, here] + block * back
            late_state = middle[1, held, here] + block * state + response_of(decay, upright, steps_local) * early_back
            for slot, (early, late) in enumerate(((early_back, back), (state, late_state))):
                keep[slot, held, here] = jnp.where(core == 0, early, late)
                send[slot, held, here] = jnp.where(core == 0, late, early)

        each_block(cells, 4 * LANES, one)


def finish_kernel(theirs, ratio, chips, *rest):
    state_out, adjoint_out, result, sems = rest[-4:]
    parts, entered = rest[:2]
    steps_local, depth, cells = state_out.shape
    tile = depth // 4
    core = this_core()
    whole = step_scale(ratio, 2 * steps_local, chips, -1)
    scales = [jnp.where(core == 0, whole[step], whole[steps_local + step]) for step in range(steps_local)]
    copies = []
    for side in (OUTER, INNER):
        held = slice(side * tile, (side + 1) * tile)
        start = tile_rows(side, 2 * tile, depth)
        rows = pl.ds(pl.multiple_of(depth - tile - start if theirs else start, 8), tile)

        def one(here):
            if theirs:
                decay, gain, half_up = [parts[2 * steps_local + slot, held, here] for slot in range(3)]
            else:
                decay, gain, half_up = finish_factors(ratio, [rest[2 + side][slot, :, here] for slot in range(4)])
            backs = [entered[0, held, here]]
            for _ in range(steps_local):
                backs.append(decay * backs[-1])
            backs = backs[:0:-1]
            previous = entered[1, held, here]
            for step in range(steps_local):
                current = decay * previous + half_up * backs[step]
                adjoint = backs[step] - gain * previous
                result[side, 0, step, :, here] = (parts[2 * step, held, here] + current) * scales[step]
                result[side, 1, step, :, here] = (parts[2 * step + 1, held, here] + adjoint) * scales[step]
                previous = current

        each_block(cells, 4 * LANES, one)
        for field, out in enumerate((state_out, adjoint_out)):
            copies.append(pltpu.make_async_copy(result.at[side, field], out.at[:, rows, :], sems.at[side, field]))
            copies[-1].start()
    for copy in copies:
        copy.wait()


def body(state_rhs, adjoint_rhs, diffusivity, velocity):
    steps_local, depth, cells = state_rhs.shape
    ranks = lax.axis_size("tm")
    slabs = lax.axis_size("gz")
    chips = ranks // 2
    total = steps_local * ranks
    steps = 2 * steps_local
    half = depth // 2
    tile = half // 2
    groups = cells // LANES
    wide = cells + 2 * LANES
    ratio = alpha_wrap ** (1.0 / total)
    core = this_core()
    f32 = jnp.float32
    anywhere = pl.BlockSpec(memory_space=pl.ANY)
    vmem = pl.BlockSpec(memory_space=pltpu.VMEM)

    def partner(value, mask):
        return lax.ppermute(value, "tm", [(i, i ^ mask) for i in range(ranks)])

    def outward(value):
        pairs = []
        for t in range(ranks):
            for g in range(slabs):
                to = g - 1 if t % 2 == 0 else g + 1
                if 0 <= to < slabs:
                    pairs.append((t * slabs + g, (t ^ 1) * slabs + to))
        return lax.ppermute(value, ("tm", "gz"), pairs)

    def call(kernel, name, out_shape, *args, **kwargs):
        shapes = [jax.ShapeDtypeStruct(s, f32) for s in out_shape]
        micros = next(value for word, value in MICROSECONDS.items() if word in name)
        return pl.pallas_call(
            kernel,
            out_shape=shapes,
            compiler_params=pltpu.CompilerParams(vmem_limit_bytes=32 * 1024 * 1024),
            cost_estimate=pl.CostEstimate(flops=0, transcendentals=0, bytes_accessed=int(micros * 3.7e6)),
            name=name,
            **kwargs,
        )(*args)

    layer = (groups, LANES)
    halves = (2, steps_local, half, cells + LANES)
    keep, send, slab, edge, edge_send, layers = call(
        pack_kernel,
        "halves_and_layers",
        [halves, halves, (depth, cells), (steps + 2,) + layer, (steps,) + layer, (4,) + layer],
        *[pltpu.with_memory_space_constraint(x, pltpu.HBM) for x in (state_rhs, adjoint_rhs, diffusivity)],
        in_specs=[anywhere] * 3,
        scratch_shapes=[pltpu.SemaphoreType.DMA((5,))],
    )
    cut, send = call(
        join_kernel,
        "outermost_layer",
        [(2 * steps + 2,) + layer, halves],
        edge,
        partner(edge_send, 1),
        send,
        in_specs=[vmem, vmem, anywhere],
        out_specs=[vmem, anywhere],
        input_output_aliases={2: 1},
    )
    other = partner(send, 1)
    cut = outward(cut)

    def first_ends(side, *args):
        return call(
            functools.partial(ends_kernel, side, ratio, chips),
            ("outer", "inner")[side] + "_ends",
            [(2 * steps, tile, wide), (4, tile, wide), (2, tile, wide)],
            keep,
            other,
            slab,
            layers,
            *args,
        )

    inner_raw, inner_factors, inner_ends = first_ends(INNER)
    outer_raw, outer_factors, outer_ends = first_ends(OUTER, cut, inner_ends)

    def beside(value, masks):
        return lax.ppermute(value, "tm", [(i, i ^ masks[i % 2]) for i in range(ranks)])

    def exchange(mine, factors):
        if chips != 4:
            return [gathered(mine, factors)]
        theirs = beside(mine, (2, 4))
        (passed,) = call(functools.partial(relay_kernel, steps), "relay", [mine.shape], factors, mine, theirs)
        return [mine, theirs, beside(passed, (4, 2))]

    def gathered(mine, factors):
        width = mine.shape[2]
        every = lax.dynamic_index_in_dim(
            lax.all_gather(mine, "tm").reshape((chips, 2) + mine.shape), core, 1, keepdims=False
        )
        block, response, closing = ring_factors([factors[i, :, :width] for i in range(4)], steps, chips)
        at = lambda array, index: lax.dynamic_index_in_dim(array, lax.rem(index + 2 * chips, chips), 0, keepdims=False)
        chip = this_chip()

        def entering_back(where):
            value = jnp.zeros((tile, width), f32)
            for offset in reversed(range(chips)):
                value = block * value + at(every[:, 0], where + 1 + offset)
            return value * closing

        value = jnp.zeros((tile, width), f32)
        for offset in reversed(range(chips)):
            source = chip - 1 - offset
            value = block * value + at(every[:, 1], source) + response * entering_back(source)
        return jnp.stack([entering_back(chip), value * closing])

    def first_sweep(side, raw, factors, ends):
        return call(
            functools.partial(sweep_kernel, ratio),
            ("outer", "inner")[side] + "_first_sweep",
            [(2 * steps, tile, cells)] * 2 + [(2 * steps,) + layer],
            raw,
            factors,
            *ends,
        )

    inner_first, inner_turned, inner_layer = first_sweep(
        INNER, inner_raw, inner_factors, exchange(inner_ends, inner_factors)
    )
    outer_first, outer_turned, outer_layer = first_sweep(
        OUTER, outer_raw, outer_factors, exchange(outer_ends, outer_factors)
    )

    keep, send, middle, *ends = call(
        functools.partial(couplings_kernel, ratio),
        "couplings",
        [(steps, half, cells), (steps + 3, half, cells), (2, half, cells), (2, tile, cells), (2, tile, cells)],
        slab,
        velocity,
        cut,
        outer_first,
        outer_turned,
        outer_layer,
        outer_factors,
        inner_first,
        inner_turned,
        inner_layer,
        inner_factors,
    )
    other = partner(send, 1)
    entered = [exchange(mine, table) for mine, table in zip(ends, (outer_factors, inner_factors))]
    own_in, send_in = call(
        functools.partial(carry_kernel, steps_local),
        "entering",
        [(2, half, cells)] * 2,
        middle,
        outer_factors,
        inner_factors,
        *entered[OUTER],
        *entered[INNER],
    )
    other_in = partner(send_in, 1)

    def finish(theirs, results, *args):
        return call(
            functools.partial(finish_kernel, theirs, ratio, chips),
            ("finish_own", "finish_other")[theirs],
            [(steps_local, depth, cells)] * 2,
            *args,
            *results,
            in_specs=[vmem] * len(args) + [anywhere] * len(results),
            out_specs=[anywhere] * 2,
            scratch_shapes=[pltpu.VMEM((2, 2, steps_local, tile, cells), f32), pltpu.SemaphoreType.DMA((2, 2))],
            input_output_aliases={len(args) + i: i for i in range(len(results))},
        )

    results = finish(False, (), keep, own_in, outer_factors, inner_factors)
    return finish(True, results, other, other_in)


def solution(mesh):
    placed = (P("tm", "gz", None), P("tm", "gz", None), P("gz", None), P(None, "gz", None))
    return jax.shard_map(
        body,
        mesh=mesh,
        in_specs=placed,
        out_specs=(P("tm", "gz", None), P("tm", "gz", None)),
        check_vma=False,
    )
```

```python
import functools
import math

import jax
import jax.numpy as jnp
from jax import lax
from jax.experimental import pallas as pl
from jax.experimental.pallas import tpu as pltpu
from jax.sharding import PartitionSpec as P

NY = 64
LANES = 128

alpha_wrap = 0.1
beta_couple = 0.5
gamma_couple = 0.5


def this_core():
    return lax.rem(lax.axis_index("tm"), 2)


def this_chip():
    return lax.div(lax.axis_index("tm"), 2)


def lane_block(start, width=LANES):
    return pl.ds(pl.multiple_of(start, LANES), width)


def each_block(cells, width, work):
    def one(index, carry):
        work(lane_block(index * width, width))
        return carry

    lax.fori_loop(0, cells // width, one, 0)
    if cells % width:
        work(slice(cells - cells % width, cells))


def power(value, count):
    result = None
    while count:
        if count & 1:
            result = value if result is None else result * value
        count >>= 1
        if count:
            value = value * value
    return result


def step_scale(ratio, steps, chips, sign):
    chip = this_chip()
    base = jnp.float32(1.0)
    bit = 0
    while 1 << bit < chips:
        factor = ratio ** (sign * steps * (1 << bit))
        base = base * jnp.where(lax.rem(lax.div(chip, 1 << bit), 2) == 1, factor, 1.0)
        bit += 1
    return [base * (ratio ** (sign * step)) for step in range(steps)]


OUTER, INNER = 0, 1
MICROSECONDS = {
    'halves': 2,
    'outermost': 0.3,
    'ends': 1,
    'relay': 0.2,
    'first_sweep': 1,
    'couplings': 3,
    'entering': 0.2,
    'finish': 1,
}
UNROLL_ENDS = 8
UNROLL_COUPLINGS = 4


def tile_rows(side, half, depth):
    core = this_core()
    tile = half // 2
    return core * (depth - tile) if side == OUTER else tile + core * tile


def faces(side, slab, outer, group, half):
    core = this_core()
    depth, cells = slab.shape
    tile = half // 2
    groups = cells // LANES
    own = pl.ds(pl.multiple_of(tile_rows(side, half, depth), 8), tile)
    here = lane_block(group * LANES)
    kappa = slab[own, here]
    left = slab[own, lane_block(jnp.maximum(group - 1, 0) * LANES)]
    right = slab[own, lane_block(jnp.minimum(group + 1, groups - 1) * LANES)]
    mirrored = lambda row: jnp.where(core == 0, slab[row : row + 1, here], slab[depth - 1 - row : depth - row, here])
    outward = outer if side == OUTER else mirrored(tile - 1)
    inward = mirrored(tile if side == OUTER else half)
    first, last = edge_rows(kappa.shape)
    shift, back = z_shifts(tile)
    lane = lax.broadcasted_iota(jnp.int32, kappa.shape, 1)
    column = lax.rem(lane, NY)
    low = lane < NY
    turned = pltpu.roll(kappa, NY, 1)
    outward = jnp.where(first, outward, pltpu.roll(kappa, shift, 0))
    inward = jnp.where(last, inward, pltpu.roll(kappa, back, 0))
    pairs = (
        ((outward, outward > 0.0), (inward, inward > 0.0)),
        (
            (jnp.where(low, turned, pltpu.roll(right, NY, 1)), jnp.logical_or(low, group < groups - 1)),
            (jnp.where(low, pltpu.roll(left, NY, 1), turned), jnp.logical_or(lane >= NY, group > 0)),
        ),
        ((pltpu.roll(kappa, LANES - 1, 1), column < NY - 1), (pltpu.roll(kappa, 1, 1), column > 0)),
    )
    return [[(jnp.where(ok, 0.5 * (kappa + value), kappa), ok) for value, ok in pair] for pair in pairs]


def cut_inside():
    slab = lax.axis_index("gz")
    return jnp.where(this_core() == 0, slab > 0, slab < lax.axis_size("gz") - 1)


def edge_rows(shape):
    core = this_core()
    row = lax.broadcasted_iota(jnp.int32, shape, 0)
    last = shape[0] - 1
    return row == core * last, row == (1 - core) * last


def z_shifts(tile):
    core = this_core()
    return 1 + core * (tile - 2), tile - 1 - core * (tile - 2)


def total_weight(weights):
    total = None
    for pair in weights:
        for weight, _ in pair:
            total = weight if total is None else total + weight
    return total


def layer_diagonal(kappa, ahead, behind):
    rows = kappa.shape[0]
    lane = lax.broadcasted_iota(jnp.int32, kappa.shape, 1)
    row = lax.broadcasted_iota(jnp.int32, kappa.shape, 0)
    column = lax.rem(lane, NY)
    turned = pltpu.roll(kappa, NY, 1)
    x_ahead = jnp.where(lane < NY, turned, pltpu.roll(turned, rows - 1, 0))
    x_behind = jnp.where(lane < NY, pltpu.roll(turned, 1, 0), turned)
    pairs = (
        (ahead, ahead > 0.0),
        (behind, behind > 0.0),
        (x_ahead, jnp.logical_or(lane < NY, row < rows - 1)),
        (x_behind, jnp.logical_or(lane >= NY, row > 0)),
        (pltpu.roll(kappa, LANES - 1, 1), column < NY - 1),
        (pltpu.roll(kappa, 1, 1), column > 0),
    )
    total = None
    for value, ok in pairs:
        weight = jnp.where(ok, 0.5 * (kappa + value), kappa)
        total = weight if total is None else total + weight
    return total


def cell_factors(diagonal, ratio):
    shifted = 1.0 + diagonal
    lifted = shifted * shifted - (ratio * ratio + beta_couple * gamma_couple)
    mix = shifted / (lifted + jnp.sqrt(lifted * lifted + shifted * shifted))
    inverse = 1.0 / (shifted + 0.5 * mix)
    return ratio * inverse, inverse, mix * inverse, 1.0 / shifted


def local_ends(values, decay, inverse, mixed, upright, steps):
    back = None
    last = None
    weight = None
    for step in reversed(range(steps)):
        state, adjoint = values(step)
        drive = inverse * adjoint - mixed * state
        back = drive if back is None else decay * back + drive
        term = state + 0.5 * back
        last = term if last is None else last + weight * term
        weight = decay if weight is None else weight * decay
    return back, last * upright


def solve_steps(values, decay, inverse, mixed, upright, ratio, back_in, state_in, steps, put):
    backs = [None] * steps
    back = back_in
    for step in reversed(range(steps)):
        state, adjoint = values(step)
        drive = inverse * adjoint - mixed * state
        back = drive if back is None else decay * back + drive
        backs[step] = back
    gain = ratio * mixed
    half_up = 0.5 * upright
    previous = state_in
    for step in range(steps):
        state, _ = values(step)
        current = upright * state + half_up * backs[step]
        adjoint = backs[step]
        if previous is not None:
            current = current + decay * previous
            adjoint = adjoint - gain * previous
        put(step, current, adjoint)
        previous = current
    return backs[0], previous


def pack_kernel(state, adjoint, kappa, keep, send, slab, edge, edge_send, layers, sems):
    steps_local, depth, cells = state.shape
    half = depth // 2
    core = this_core()
    mine = pl.ds(pl.multiple_of(core * half, 8), half)
    others = pl.ds(pl.multiple_of((1 - core) * half, 8), half)
    within = pl.ds(0, cells)
    copies = [pltpu.make_async_copy(kappa, slab, sems.at[4])]
    for field, source in enumerate((state, adjoint)):
        copies.append(pltpu.make_async_copy(source.at[:, mine, :], keep.at[field, :, :, within], sems.at[2 * field]))
        copies.append(pltpu.make_async_copy(source.at[:, others, :], send.at[field, :, :, within], sems.at[2 * field + 1]))
    for copy in copies:
        copy.start()

    def lay(source, rows, target):
        for group in range(cells // LANES):
            lanes = slice(group * LANES, (group + 1) * LANES)
            one, other = [source[row : row + 1, lanes] for row in rows]
            target[group : group + 1, :] = jnp.where(core == 0, one, other)

    copies[0].wait()
    last = depth - 1
    lay(slab, (0, last), edge.at[2 * steps_local])
    lay(slab, (1, last - 1), edge.at[2 * steps_local + 1])
    for slot, row in enumerate((0, half - 1, half, half + 1)):
        lay(slab, (row, last - row), layers.at[slot])
    for copy in copies[1:]:
        copy.wait()
    near, far = (0, half - 1), (half - 1, 0)
    beyond = pl.ds(cells, LANES)
    for index in range(steps_local):
        for field in range(2):
            slot = 2 * index + field
            lay(keep.at[field, index], near, edge.at[slot])
            lay(send.at[field, index], far, edge_send.at[slot])
            lay(send.at[field, index], near, keep.at[field, index, :, beyond])
            lay(keep.at[field, index], far, send.at[field, index, :, beyond])


def join_kernel(edge, edge_other, swap, both, swap_out):
    count = edge.shape[0]
    both[:count] = edge[...]
    both[count:] = edge_other[...]


def ends_kernel(side, ratio, chips, keep, other, slab, layers, *rest):
    cut = rest[0] if side == OUTER else None
    raw_ref, factor_ref, ends_ref = rest[-3:]
    steps_local, half, cells = keep.shape[1:]
    cells = cells - LANES
    steps = 2 * steps_local
    tile = half // 2
    groups = cells // LANES
    core = this_core()
    scales = step_scale(ratio, steps, chips, 1)
    own = pl.ds(pl.multiple_of((core if side == OUTER else 1 - core) * tile, 8), tile)
    places = []
    for position in range(2):
        sub = core if position == 0 else 1 - core
        for index in range(steps_local):
            scale = jnp.where(sub == 0, scales[index], scales[steps_local + index])
            places.append((position, index, sub * steps + 2 * index, scale))

    def work(diagonal, loads, stores):
        factors = cell_factors(diagonal, ratio)
        for slot, value in enumerate(factors):
            stores(factor_ref, slot, value)
        for position, index, slot, scale in places:
            for field in range(2):
                stores(raw_ref, slot + field, loads(position, index, field) * scale)

    def put_ends(here):
        factors = [factor_ref[slot, :, here] for slot in range(4)]
        values = lambda step: (raw_ref[2 * step, :, here], raw_ref[2 * step + 1, :, here])
        for slot, value in enumerate(local_ends(values, *factors, steps)):
            ends_ref[slot, :, here] = value

    def one(group, carry):
        here = lane_block(group * LANES)
        beyond = jnp.where(cut_inside(), cut[steps, pl.ds(group, 1), :], 0.0) if side == OUTER else None
        diagonal = total_weight(faces(side, slab, beyond, group, half))

        def stores(ref, slot, value):
            ref[slot, :, here] = value

        work(diagonal, lambda position, index, field: (keep, other)[position][field, index, own, here], stores)
        put_ends(here)
        return carry

    lax.fori_loop(0, groups, one, 0, unroll=UNROLL_ENDS)

    def stores_cut(ref, slot, value):
        for part in range(2):
            lanes = slice(cells + part * LANES, cells + (part + 1) * LANES)
            ref[slot, :, lanes] = value[part * tile : (part + 1) * tile]

    if side == OUTER:
        diagonal = layer_diagonal(cut[steps], layers[0], cut[steps + 1])
        starts = (steps + 2, 0)
        loads = lambda position, index, field: cut[starts[position] + 2 * index + field]
    else:
        diagonal = layer_diagonal(layers[2], layers[1], layers[3])
        loads = lambda position, index, field: (keep, other)[position][field, index, :, cells:]
    work(diagonal, loads, stores_cut)
    for part in range(2):
        put_ends(slice(cells + part * LANES, cells + (part + 1) * LANES))


def power_sum(value, count):
    total = None
    for _ in range(count):
        total = 1.0 if total is None else 1.0 + value * total
    return total


def response_of(decay, upright, steps):
    return (0.5 * upright) * decay * power_sum(decay * decay, steps)


def ring_factors(factors, steps, chips):
    decay, _, _, upright = factors
    block = power(decay, steps)
    return block, response_of(decay, upright, steps), 1.0 / (1.0 - power(block, chips))


def choose(flag, one, other):
    return tuple(jnp.where(flag, a, b) for a, b in zip(one, other))


def ring_weights(factors, steps):
    block, response, closing = ring_factors(factors, steps, 4)
    square = block * block
    cross = response * closing * closing
    near = cross * block * (1.0 + square) * (1.0 + square)
    once = closing * block
    twice = closing * square
    thrice = once * square
    return (
        (thrice, thrice, cross * (1.0 + square) * (1.0 + square * square)),
        (closing, twice, near),
        (once, once, 2.0 * cross * square * (1.0 + square)),
        (twice, closing, near),
    )


def weighted(weights, ends):
    back, last = ends
    return weights[0] * back, weights[1] * last + weights[2] * back


def relay_kernel(steps, factor_ref, mine, theirs, passed):
    odd = lax.rem(this_chip(), 2) == 1
    along_x = this_core() == 0

    def one(here):
        _, next_, across, before = ring_weights([factor_ref[slot, :, here] for slot in range(4)], steps)
        beside = choose(odd, next_, before)
        a = weighted(choose(along_x, across, beside), (mine[0, :, here], mine[1, :, here]))
        b = weighted(choose(along_x, beside, choose(odd, before, next_)), (theirs[0, :, here], theirs[1, :, here]))
        passed[0, :, here] = a[0] + b[0]
        passed[1, :, here] = a[1] + b[1]

    each_block(mine.shape[2], 4 * LANES, one)


def entering(factors, ends, here, steps):
    if len(ends) == 1:
        return ends[0][0, :, here], ends[0][1, :, here]
    mine, theirs, tail = ends
    own, next_, across, before = ring_weights(factors, steps)
    odd = lax.rem(this_chip(), 2) == 1
    along_x = this_core() == 0
    a = weighted(own, (mine[0, :, here], mine[1, :, here]))
    b = weighted(choose(along_x, choose(odd, before, next_), across), (theirs[0, :, here], theirs[1, :, here]))
    return a[0] + b[0] + tail[0, :, here], a[1] + b[1] + tail[1, :, here]


def sweep_kernel(ratio, raw_ref, factor_ref, *rest):
    *ends, first_ref, turned_ref, layer_ref = rest
    tile = raw_ref.shape[1]
    steps = raw_ref.shape[0] // 2
    cells = first_ref.shape[2]

    def sweep(put, here):
        factors = [factor_ref[slot, :, here] for slot in range(4)]
        values = lambda step: (raw_ref[2 * step, :, here], raw_ref[2 * step + 1, :, here])
        solve_steps(values, *factors, ratio, *entering(factors, ends, here, steps), steps, put)

    def own(here):
        def put(step, state, adjoint):
            for field, value in enumerate((state, adjoint)):
                slot = 2 * step + field
                first_ref[slot, :, here] = value
                turned_ref[slot, :, here] = turned(value)

        sweep(put, here)

    each_block(cells, 4 * LANES, own)

    def put_layer(step, state, adjoint):
        for field, value in enumerate((state, adjoint)):
            for part in range(2):
                layer_ref[2 * step + field, part * tile : (part + 1) * tile, :] = value[:, part * LANES : (part + 1) * LANES]

    sweep(put_layer, slice(cells, cells + 2 * LANES))


def turned(value):
    parts = [pltpu.roll(value[:, i : i + LANES], NY, 1) for i in range(0, value.shape[1], LANES)]
    return parts[0] if len(parts) == 1 else jnp.concatenate(parts, axis=1)


def couplings_kernel(ratio, slab, velocity_ref, cut_ref, *refs):
    *results, outer_ends, inner_ends = refs[-5:]
    outer, inner = refs[:4], refs[4:8]
    work = functools.partial(couple_tile, ratio, slab, velocity_ref, cut_ref)
    work(OUTER, *outer, inner[0], *results, outer_ends)
    work(INNER, *inner, outer[0], *results, inner_ends)


def couple_tile(ratio, slab, velocity_ref, cut_ref, side, first_ref, turned_ref, layer_ref, factor_ref, next_ref, keep, send, middle, ends_ref):
    slots, tile, cells = first_ref.shape
    steps = slots // 2
    steps_local = steps // 2
    depth = slab.shape[0]
    half = 2 * tile
    groups = cells // LANES
    core = this_core()
    own = pl.ds(pl.multiple_of(tile_rows(side, half, depth), 8), tile)
    held = slice(side * tile, (side + 1) * tile)
    out_shift, in_shift = z_shifts(tile)

    def one(group, carry):
        here = lane_block(group * LANES)
        left = lane_block(jnp.maximum(group - 1, 0) * LANES)
        right = lane_block(jnp.minimum(group + 1, groups - 1) * LANES)
        row = pl.ds(group, 1)
        beyond = jnp.where(cut_inside(), cut_ref[steps, row, :], 0.0) if side == OUTER else None
        weights = faces(side, slab, beyond, group, half)
        lane = lax.broadcasted_iota(jnp.int32, (tile, LANES), 1)
        low = lane < NY
        first, last = edge_rows((tile, LANES))
        drifts = [0.5 * velocity_ref[component, own, here] for component in (2, 0, 1)]
        drifts[0] = jnp.where(core == 0, -drifts[0], drifts[0])
        tables = []
        for sign in (1.0, -1.0):
            one_way, other_way = [], []
            for ((ahead, ok_ahead), (behind, ok_behind)), drift in zip(weights, drifts):
                one_way.append(jnp.where(ok_ahead, ahead - sign * drift, 0.0))
                other_way.append(jnp.where(ok_behind, behind + sign * drift, 0.0))
            x_same = jnp.where(low, one_way[1], other_way[1])
            x_next = jnp.where(low, other_way[1], one_way[1])
            tables.append((one_way[0], other_way[0], x_same, x_next, one_way[2], other_way[2]))
        factors = [factor_ref[slot, :, here] for slot in range(4)]

        def coupled(slot):
            c_out, c_in, x_same, x_next, c_ahead, c_behind = tables[slot % 2]
            value = first_ref[slot, :, here]
            following = next_ref[slot, :, here]
            cut = layer_ref[slot, row, :]
            if side == OUTER:
                outward = jnp.where(first, cut, pltpu.roll(value, out_shift, 0))
                inward = pltpu.roll(jnp.where(first, following, value), in_shift, 0)
            else:
                outward = pltpu.roll(jnp.where(last, following, value), out_shift, 0)
                inward = jnp.where(last, cut, pltpu.roll(value, in_shift, 0))
            result = c_out * outward + c_in * inward
            beside = jnp.where(low, turned_ref[slot, :, left], turned_ref[slot, :, right])
            result = result + (x_same * turned_ref[slot, :, here] + x_next * beside)
            return result + (c_ahead * pltpu.roll(value, LANES - 1, 1) + c_behind * pltpu.roll(value, 1, 1))

        results = {}
        ends = []
        for sub in range(2):
            offset = 2 * steps_local * sub
            drives = [coupled(offset + slot) for slot in range(2 * steps_local)]

            def put(step, state, adjoint):
                results[sub, step] = (state, adjoint)

            values = lambda step: (drives[2 * step], drives[2 * step + 1])
            ends.append(solve_steps(values, *factors, ratio, None, None, steps_local, put))
        for step in range(steps_local):
            for field in range(2):
                slot = 2 * step + field
                early, late = [
                    first_ref[2 * steps_local * sub + slot, :, here] + results[sub, step][field] for sub in range(2)
                ]
                keep[slot, held, here] = jnp.where(core == 0, early, late)
                send[slot, held, here] = jnp.where(core == 0, late, early)
        for slot, value in enumerate(finish_factors(ratio, factors)):
            send[2 * steps_local + slot, held, here] = value
        (early_back, early_last), (late_back, late_last) = ends
        decay, _, _, upright = factors
        block = power(decay, steps_local)
        middle[0, held, here] = late_back
        middle[1, held, here] = early_last
        ends_ref[0, :, here] = early_back + block * late_back
        ends_ref[1, :, here] = late_last + block * (early_last + response_of(decay, upright, steps_local) * late_back)
        return carry

    lax.fori_loop(0, groups, one, 0, unroll=UNROLL_COUPLINGS)


def finish_factors(ratio, factors):
    decay, _, mixed, upright = factors
    return decay, ratio * mixed, 0.5 * upright


def carry_kernel(side, steps_local, middle, factor_ref, *rest):
    *ends, keep, send = rest
    tile, cells = keep.shape[1:]
    held = slice(side * tile, (side + 1) * tile)
    core = this_core()

    def one(here):
        factors = [factor_ref[slot, :, here] for slot in range(4)]
        decay, _, _, upright = factors
        back, state = entering(factors, ends, here, 2 * steps_local)
        block = power(decay, steps_local)
        early_back = middle[0, held, here] + block * back
        late_state = middle[1, held, here] + block * state + response_of(decay, upright, steps_local) * early_back
        for slot, (early, late) in enumerate(((early_back, back), (state, late_state))):
            keep[slot, :, here] = jnp.where(core == 0, early, late)
            send[slot, :, here] = jnp.where(core == 0, late, early)

    each_block(cells, 4 * LANES, one)


def finish_kernel(jobs, ratio, chips, *refs):
    state_out, adjoint_out, result, sems = refs[-4:]
    steps_local, depth, cells = state_out.shape
    tile = depth // 4
    core = this_core()
    whole = step_scale(ratio, 2 * steps_local, chips, -1)
    scales = [jnp.where(core == 0, whole[step], whole[steps_local + step]) for step in range(steps_local)]
    copies = []
    for job, (theirs, side) in enumerate(jobs):
        parts, entered, factor_ref = refs[3 * job : 3 * job + 3]
        held = slice(side * tile, (side + 1) * tile)
        start = tile_rows(side, 2 * tile, depth)
        rows = pl.ds(pl.multiple_of(depth - tile - start if theirs else start, 8), tile)

        def one(here):
            if theirs:
                decay, gain, half_up = [parts[2 * steps_local + slot, held, here] for slot in range(3)]
            else:
                decay, gain, half_up = finish_factors(ratio, [factor_ref[slot, :, here] for slot in range(4)])
            backs = [entered[0, :, here]]
            for _ in range(steps_local):
                backs.append(decay * backs[-1])
            backs = backs[:0:-1]
            previous = entered[1, :, here]
            for step in range(steps_local):
                current = decay * previous + half_up * backs[step]
                adjoint = backs[step] - gain * previous
                result[job, 0, step, :, here] = (parts[2 * step, held, here] + current) * scales[step]
                result[job, 1, step, :, here] = (parts[2 * step + 1, held, here] + adjoint) * scales[step]
                previous = current

        each_block(cells, 4 * LANES, one)
        for field, out in enumerate((state_out, adjoint_out)):
            copies.append(pltpu.make_async_copy(result.at[job, field], out.at[:, rows, :], sems.at[job, field]))
            copies[-1].start()
    for copy in copies:
        copy.wait()


def body(state_rhs, adjoint_rhs, diffusivity, velocity):
    steps_local, depth, cells = state_rhs.shape
    ranks = lax.axis_size("tm")
    slabs = lax.axis_size("gz")
    chips = ranks // 2
    total = steps_local * ranks
    steps = 2 * steps_local
    half = depth // 2
    tile = half // 2
    groups = cells // LANES
    wide = cells + 2 * LANES
    ratio = alpha_wrap ** (1.0 / total)
    core = this_core()
    f32 = jnp.float32
    anywhere = pl.BlockSpec(memory_space=pl.ANY)
    vmem = pl.BlockSpec(memory_space=pltpu.VMEM)

    def partner(value, mask):
        return lax.ppermute(value, "tm", [(i, i ^ mask) for i in range(ranks)])

    def outward(value):
        pairs = []
        spare = (4, 2) if ranks % 8 == 0 else (0, 0)
        for t in range(ranks):
            for g in range(slabs):
                to = g - 1 if t % 2 == 0 else g + 1
                other = (t ^ 1) * slabs + to if 0 <= to < slabs else (t ^ spare[t % 2]) * slabs + g
                pairs.append((t * slabs + g, other))
        return lax.ppermute(value, ("tm", "gz"), pairs)

    def call(kernel, name, out_shape, *args, **kwargs):
        shapes = [jax.ShapeDtypeStruct(s, f32) for s in out_shape]
        micros = next(value for word, value in MICROSECONDS.items() if word in name)
        return pl.pallas_call(
            kernel,
            out_shape=shapes,
            compiler_params=pltpu.CompilerParams(vmem_limit_bytes=32 * 1024 * 1024),
            cost_estimate=pl.CostEstimate(flops=0, transcendentals=0, bytes_accessed=int(micros * 3.7e6)),
            name=name,
            **kwargs,
        )(*args)

    layer = (groups, LANES)
    halves = (2, steps_local, half, cells + LANES)
    keep, send, slab, edge, edge_send, layers = call(
        pack_kernel,
        "halves_and_layers",
        [halves, halves, (depth, cells), (steps + 2,) + layer, (steps,) + layer, (4,) + layer],
        *[pltpu.with_memory_space_constraint(x, pltpu.HBM) for x in (state_rhs, adjoint_rhs, diffusivity)],
        in_specs=[anywhere] * 3,
        scratch_shapes=[pltpu.SemaphoreType.DMA((5,))],
    )
    cut, send = call(
        join_kernel,
        "outermost_layer",
        [(2 * steps + 2,) + layer, halves],
        edge,
        partner(edge_send, 1),
        send,
        in_specs=[vmem, vmem, anywhere],
        out_specs=[vmem, anywhere],
        input_output_aliases={2: 1},
    )
    other = partner(send, 1)
    cut = outward(cut)

    def first_ends(side, *args):
        return call(
            functools.partial(ends_kernel, side, ratio, chips),
            ("outer", "inner")[side] + "_ends",
            [(2 * steps, tile, wide), (4, tile, wide), (2, tile, wide)],
            keep,
            other,
            slab,
            layers,
            *args,
        )

    inner_raw, inner_factors, inner_ends = first_ends(INNER)
    outer_raw, outer_factors, outer_ends = first_ends(OUTER, cut, inner_ends)

    def beside(value, masks):
        return lax.ppermute(value, "tm", [(i, i ^ masks[i % 2]) for i in range(ranks)])

    def exchange(mine, factors):
        if chips != 4:
            return [gathered(mine, factors)]
        theirs = beside(mine, (2, 4))
        (passed,) = call(functools.partial(relay_kernel, steps), "relay", [mine.shape], factors, mine, theirs)
        return [mine, theirs, beside(passed, (4, 2))]

    def gathered(mine, factors):
        width = mine.shape[2]
        every = lax.dynamic_index_in_dim(
            lax.all_gather(mine, "tm").reshape((chips, 2) + mine.shape), core, 1, keepdims=False
        )
        block, response, closing = ring_factors([factors[i, :, :width] for i in range(4)], steps, chips)
        at = lambda array, index: lax.dynamic_index_in_dim(array, lax.rem(index + 2 * chips, chips), 0, keepdims=False)
        chip = this_chip()

        def entering_back(where):
            value = jnp.zeros((tile, width), f32)
            for offset in reversed(range(chips)):
                value = block * value + at(every[:, 0], where + 1 + offset)
            return value * closing

        value = jnp.zeros((tile, width), f32)
        for offset in reversed(range(chips)):
            source = chip - 1 - offset
            value = block * value + at(every[:, 1], source) + response * entering_back(source)
        return jnp.stack([entering_back(chip), value * closing])

    def first_sweep(side, raw, factors, ends):
        return call(
            functools.partial(sweep_kernel, ratio),
            ("outer", "inner")[side] + "_first_sweep",
            [(2 * steps, tile, cells)] * 2 + [(2 * steps,) + layer],
            raw,
            factors,
            *ends,
        )

    inner_first, inner_turned, inner_layer = first_sweep(
        INNER, inner_raw, inner_factors, exchange(inner_ends, inner_factors)
    )
    outer_first, outer_turned, outer_layer = first_sweep(
        OUTER, outer_raw, outer_factors, exchange(outer_ends, outer_factors)
    )

    keep, send, middle, *ends = call(
        functools.partial(couplings_kernel, ratio),
        "couplings",
        [(steps, half, cells), (steps + 3, half, cells), (2, half, cells), (2, tile, cells), (2, tile, cells)],
        slab,
        velocity,
        cut,
        outer_first,
        outer_turned,
        outer_layer,
        outer_factors,
        inner_first,
        inner_turned,
        inner_layer,
        inner_factors,
    )
    other = partner(send, 1)
    entered = [exchange(mine, table) for mine, table in zip(ends, (outer_factors, inner_factors))]
    factors = (outer_factors, inner_factors)

    def enter(side):
        own_in, send_in = call(
            functools.partial(carry_kernel, side, steps_local),
            ("outer", "inner")[side] + "_entering",
            [(2, tile, cells)] * 2,
            middle,
            factors[side],
            *entered[side],
        )
        return own_in, partner(send_in, 1)

    own_in, other_in = zip(enter(OUTER), enter(INNER))

    def finish(results, *jobs):
        args = []
        for theirs, side in jobs:
            args += [other if theirs else keep, (other_in if theirs else own_in)[side], factors[side]]
        return call(
            functools.partial(finish_kernel, jobs, ratio, chips),
            "finish",
            [(steps_local, depth, cells)] * 2,
            *args,
            *results,
            in_specs=[vmem] * len(args) + [anywhere] * len(results),
            out_specs=[anywhere] * 2,
            scratch_shapes=[
                pltpu.VMEM((len(jobs), 2, steps_local, tile, cells), f32),
                pltpu.SemaphoreType.DMA((len(jobs), 2)),
            ],
            input_output_aliases={len(args) + i: i for i in range(len(results))},
        )

    results = finish((), (False, OUTER), (False, INNER), (True, OUTER))
    return finish(results, (True, INNER))


def solution(mesh):
    placed = (P("tm", "gz", None), P("tm", "gz", None), P("gz", None), P(None, "gz", None))
    return jax.shard_map(
        body,
        mesh=mesh,
        in_specs=placed,
        out_specs=(P("tm", "gz", None), P("tm", "gz", None)),
        check_vma=False,
    )
```

```python
import functools
import math

import jax
import jax.numpy as jnp
from jax import lax
from jax.experimental import pallas as pl
from jax.experimental.pallas import tpu as pltpu
from jax.sharding import PartitionSpec as P

NY = 64
LANES = 128

alpha_wrap = 0.1
beta_couple = 0.5
gamma_couple = 0.5


def this_core():
    return lax.rem(lax.axis_index("tm"), 2)


def this_chip():
    return lax.div(lax.axis_index("tm"), 2)


def lane_block(start, width=LANES):
    return pl.ds(pl.multiple_of(start, LANES), width)


def each_block(cells, width, work):
    def one(index, carry):
        work(lane_block(index * width, width))
        return carry

    lax.fori_loop(0, cells // width, one, 0)
    if cells % width:
        work(slice(cells - cells % width, cells))


def power(value, count):
    result = None
    while count:
        if count & 1:
            result = value if result is None else result * value
        count >>= 1
        if count:
            value = value * value
    return result


def step_scale(ratio, steps, chips, sign):
    chip = this_chip()
    base = jnp.float32(1.0)
    bit = 0
    while 1 << bit < chips:
        factor = ratio ** (sign * steps * (1 << bit))
        base = base * jnp.where(lax.rem(lax.div(chip, 1 << bit), 2) == 1, factor, 1.0)
        bit += 1
    return [base * (ratio ** (sign * step)) for step in range(steps)]


OUTER, INNER = 0, 1
MICROSECONDS = {
    'halves': 2,
    'ends': 1,
    'relay': 0.2,
    'first_sweep': 1,
    'couplings': 3,
    'entering': 0.2,
    'finish': 1,
}
UNROLL_ENDS = 8
UNROLL_COUPLINGS = 4


def tile_rows(side, half, depth):
    core = this_core()
    tile = half // 2
    return core * (depth - tile) if side == OUTER else tile + core * tile


def faces(side, slab, outer, group, half):
    core = this_core()
    depth, cells = slab.shape
    tile = half // 2
    groups = cells // LANES
    own = pl.ds(pl.multiple_of(tile_rows(side, half, depth), 8), tile)
    here = lane_block(group * LANES)
    kappa = slab[own, here]
    left = slab[own, lane_block(jnp.maximum(group - 1, 0) * LANES)]
    right = slab[own, lane_block(jnp.minimum(group + 1, groups - 1) * LANES)]
    mirrored = lambda row: jnp.where(core == 0, slab[row : row + 1, here], slab[depth - 1 - row : depth - row, here])
    outward = outer if side == OUTER else mirrored(tile - 1)
    inward = mirrored(tile if side == OUTER else half)
    first, last = edge_rows(kappa.shape)
    shift, back = z_shifts(tile)
    lane = lax.broadcasted_iota(jnp.int32, kappa.shape, 1)
    column = lax.rem(lane, NY)
    low = lane < NY
    turned = pltpu.roll(kappa, NY, 1)
    outward = jnp.where(first, outward, pltpu.roll(kappa, shift, 0))
    inward = jnp.where(last, inward, pltpu.roll(kappa, back, 0))
    pairs = (
        ((outward, outward > 0.0), (inward, inward > 0.0)),
        (
            (jnp.where(low, turned, pltpu.roll(right, NY, 1)), jnp.logical_or(low, group < groups - 1)),
            (jnp.where(low, pltpu.roll(left, NY, 1), turned), jnp.logical_or(lane >= NY, group > 0)),
        ),
        ((pltpu.roll(kappa, LANES - 1, 1), column < NY - 1), (pltpu.roll(kappa, 1, 1), column > 0)),
    )
    return [[(jnp.where(ok, 0.5 * (kappa + value), kappa), ok) for value, ok in pair] for pair in pairs]


def cut_inside():
    slab = lax.axis_index("gz")
    return jnp.where(this_core() == 0, slab > 0, slab < lax.axis_size("gz") - 1)


def edge_rows(shape):
    core = this_core()
    row = lax.broadcasted_iota(jnp.int32, shape, 0)
    last = shape[0] - 1
    return row == core * last, row == (1 - core) * last


def z_shifts(tile):
    core = this_core()
    return 1 + core * (tile - 2), tile - 1 - core * (tile - 2)


def total_weight(weights):
    total = None
    for pair in weights:
        for weight, _ in pair:
            total = weight if total is None else total + weight
    return total


def layer_diagonal(kappa, ahead, behind):
    rows = kappa.shape[0]
    lane = lax.broadcasted_iota(jnp.int32, kappa.shape, 1)
    row = lax.broadcasted_iota(jnp.int32, kappa.shape, 0)
    column = lax.rem(lane, NY)
    turned = pltpu.roll(kappa, NY, 1)
    x_ahead = jnp.where(lane < NY, turned, pltpu.roll(turned, rows - 1, 0))
    x_behind = jnp.where(lane < NY, pltpu.roll(turned, 1, 0), turned)
    pairs = (
        (ahead, ahead > 0.0),
        (behind, behind > 0.0),
        (x_ahead, jnp.logical_or(lane < NY, row < rows - 1)),
        (x_behind, jnp.logical_or(lane >= NY, row > 0)),
        (pltpu.roll(kappa, LANES - 1, 1), column < NY - 1),
        (pltpu.roll(kappa, 1, 1), column > 0),
    )
    total = None
    for value, ok in pairs:
        weight = jnp.where(ok, 0.5 * (kappa + value), kappa)
        total = weight if total is None else total + weight
    return total


def cell_factors(diagonal, ratio):
    shifted = 1.0 + diagonal
    lifted = shifted * shifted - (ratio * ratio + beta_couple * gamma_couple)
    mix = shifted / (lifted + jnp.sqrt(lifted * lifted + shifted * shifted))
    inverse = 1.0 / (shifted + 0.5 * mix)
    return ratio * inverse, inverse, mix * inverse, 1.0 / shifted


def local_ends(values, decay, inverse, mixed, upright, steps):
    back = None
    last = None
    weight = None
    for step in reversed(range(steps)):
        state, adjoint = values(step)
        drive = inverse * adjoint - mixed * state
        back = drive if back is None else decay * back + drive
        term = state + 0.5 * back
        last = term if last is None else last + weight * term
        weight = decay if weight is None else weight * decay
    return back, last * upright


def solve_steps(values, decay, inverse, mixed, upright, ratio, back_in, state_in, steps, put):
    backs = [None] * steps
    back = back_in
    for step in reversed(range(steps)):
        state, adjoint = values(step)
        drive = inverse * adjoint - mixed * state
        back = drive if back is None else decay * back + drive
        backs[step] = back
    gain = ratio * mixed
    half_up = 0.5 * upright
    previous = state_in
    for step in range(steps):
        state, _ = values(step)
        current = upright * state + half_up * backs[step]
        adjoint = backs[step]
        if previous is not None:
            current = current + decay * previous
            adjoint = adjoint - gain * previous
        put(step, current, adjoint)
        previous = current
    return backs[0], previous


def pack_kernel(state, adjoint, kappa, keep, send, slab, edge, edge_send, layers, sems):
    steps_local, depth, cells = state.shape
    half = depth // 2
    core = this_core()
    mine = pl.ds(pl.multiple_of(core * half, 8), half)
    others = pl.ds(pl.multiple_of((1 - core) * half, 8), half)
    within = pl.ds(0, cells)
    copies = [pltpu.make_async_copy(kappa, slab, sems.at[4])]
    for field, source in enumerate((state, adjoint)):
        copies.append(pltpu.make_async_copy(source.at[:, mine, :], keep.at[field, :, :, within], sems.at[2 * field]))
        copies.append(pltpu.make_async_copy(source.at[:, others, :], send.at[field, :, :, within], sems.at[2 * field + 1]))
    for copy in copies:
        copy.start()

    def lay(source, rows, target):
        for group in range(cells // LANES):
            lanes = slice(group * LANES, (group + 1) * LANES)
            one, other = [source[row : row + 1, lanes] for row in rows]
            target[group : group + 1, :] = jnp.where(core == 0, one, other)

    slab_copy, *tile_copies = copies
    slab_copy.wait()
    last = depth - 1
    lay(slab, (0, last), edge.at[2 * steps_local])
    lay(slab, (1, last - 1), edge.at[2 * steps_local + 1])
    for slot, row in enumerate((0, half - 1, half, half + 1)):
        lay(slab, (row, last - row), layers.at[slot])
    near, far = (0, half - 1), (half - 1, 0)
    beyond = pl.ds(cells, LANES)
    for field in range(2):
        for copy in tile_copies[2 * field : 2 * field + 2]:
            copy.wait()
        for index in range(steps_local):
            slot = 2 * index + field
            lay(keep.at[field, index], near, edge.at[slot])
            lay(send.at[field, index], far, edge_send.at[slot])
            lay(send.at[field, index], near, keep.at[field, index, :, beyond])
            lay(keep.at[field, index], far, send.at[field, index, :, beyond])


def ends_kernel(side, ratio, chips, keep, other, slab, layers, *rest):
    cut, cut_straight = rest[:2] if side == OUTER else (None, None)
    raw_ref, factor_ref, ends_ref = rest[-3:]
    steps_local, half, cells = keep.shape[1:]
    cells = cells - LANES
    steps = 2 * steps_local
    tile = half // 2
    groups = cells // LANES
    core = this_core()
    scales = step_scale(ratio, steps, chips, 1)
    own = pl.ds(pl.multiple_of((core if side == OUTER else 1 - core) * tile, 8), tile)
    places = []
    for position in range(2):
        sub = core if position == 0 else 1 - core
        for index in range(steps_local):
            scale = jnp.where(sub == 0, scales[index], scales[steps_local + index])
            places.append((position, index, sub * steps + 2 * index, scale))

    def work(diagonal, loads, stores):
        factors = cell_factors(diagonal, ratio)
        for slot, value in enumerate(factors):
            stores(factor_ref, slot, value)
        for position, index, slot, scale in places:
            for field in range(2):
                stores(raw_ref, slot + field, loads(position, index, field) * scale)

    def put_ends(here):
        factors = [factor_ref[slot, :, here] for slot in range(4)]
        values = lambda step: (raw_ref[2 * step, :, here], raw_ref[2 * step + 1, :, here])
        for slot, value in enumerate(local_ends(values, *factors, steps)):
            ends_ref[slot, :, here] = value

    def one(group, carry):
        here = lane_block(group * LANES)
        beyond = jnp.where(cut_inside(), cut[steps, pl.ds(group, 1), :], 0.0) if side == OUTER else None
        diagonal = total_weight(faces(side, slab, beyond, group, half))

        def stores(ref, slot, value):
            ref[slot, :, here] = value

        work(diagonal, lambda position, index, field: (keep, other)[position][field, index, own, here], stores)
        put_ends(here)
        return carry

    lax.fori_loop(0, groups, one, 0, unroll=UNROLL_ENDS)

    def stores_cut(ref, slot, value):
        for part in range(2):
            lanes = slice(cells + part * LANES, cells + (part + 1) * LANES)
            ref[slot, :, lanes] = value[part * tile : (part + 1) * tile]

    if side == OUTER:
        diagonal = layer_diagonal(cut[steps], layers[0], cut[steps + 1])
        loads = lambda position, index, field: (cut_straight, cut)[position][2 * index + field]
    else:
        diagonal = layer_diagonal(layers[2], layers[1], layers[3])
        loads = lambda position, index, field: (keep, other)[position][field, index, :, cells:]
    work(diagonal, loads, stores_cut)
    for part in range(2):
        put_ends(slice(cells + part * LANES, cells + (part + 1) * LANES))


def power_sum(value, count):
    total = None
    for _ in range(count):
        total = 1.0 if total is None else 1.0 + value * total
    return total


def response_of(decay, upright, steps):
    return (0.5 * upright) * decay * power_sum(decay * decay, steps)


def ring_factors(factors, steps, chips):
    decay, _, _, upright = factors
    block = power(decay, steps)
    return block, response_of(decay, upright, steps), 1.0 / (1.0 - power(block, chips))


def choose(flag, one, other):
    return tuple(jnp.where(flag, a, b) for a, b in zip(one, other))


def ring_weights(factors, steps):
    block, response, closing = ring_factors(factors, steps, 4)
    square = block * block
    cross = response * closing * closing
    near = cross * block * (1.0 + square) * (1.0 + square)
    once = closing * block
    twice = closing * square
    thrice = once * square
    return (
        (thrice, thrice, cross * (1.0 + square) * (1.0 + square * square)),
        (closing, twice, near),
        (once, once, 2.0 * cross * square * (1.0 + square)),
        (twice, closing, near),
    )


def weighted(weights, ends):
    back, last = ends
    return weights[0] * back, weights[1] * last + weights[2] * back


def relay_kernel(steps, factor_ref, mine, theirs, passed):
    odd = lax.rem(this_chip(), 2) == 1
    along_x = this_core() == 0

    def one(here):
        _, next_, across, before = ring_weights([factor_ref[slot, :, here] for slot in range(4)], steps)
        beside = choose(odd, next_, before)
        a = weighted(choose(along_x, across, beside), (mine[0, :, here], mine[1, :, here]))
        b = weighted(choose(along_x, beside, choose(odd, before, next_)), (theirs[0, :, here], theirs[1, :, here]))
        passed[0, :, here] = a[0] + b[0]
        passed[1, :, here] = a[1] + b[1]

    each_block(mine.shape[2], 4 * LANES, one)


def entering(factors, ends, here, steps):
    if len(ends) == 1:
        return ends[0][0, :, here], ends[0][1, :, here]
    mine, theirs, tail = ends
    own, next_, across, before = ring_weights(factors, steps)
    odd = lax.rem(this_chip(), 2) == 1
    along_x = this_core() == 0
    a = weighted(own, (mine[0, :, here], mine[1, :, here]))
    b = weighted(choose(along_x, choose(odd, before, next_), across), (theirs[0, :, here], theirs[1, :, here]))
    return a[0] + b[0] + tail[0, :, here], a[1] + b[1] + tail[1, :, here]


def sweep_kernel(ratio, raw_ref, factor_ref, *rest):
    *ends, first_ref, turned_ref, layer_ref = rest
    tile = raw_ref.shape[1]
    steps = raw_ref.shape[0] // 2
    cells = first_ref.shape[2]

    def sweep(put, here):
        factors = [factor_ref[slot, :, here] for slot in range(4)]
        values = lambda step: (raw_ref[2 * step, :, here], raw_ref[2 * step + 1, :, here])
        solve_steps(values, *factors, ratio, *entering(factors, ends, here, steps), steps, put)

    def own(here):
        def put(step, state, adjoint):
            for field, value in enumerate((state, adjoint)):
                slot = 2 * step + field
                first_ref[slot, :, here] = value
                turned_ref[slot, :, here] = turned(value)

        sweep(put, here)

    each_block(cells, 4 * LANES, own)

    def put_layer(step, state, adjoint):
        for field, value in enumerate((state, adjoint)):
            for part in range(2):
                layer_ref[2 * step + field, part * tile : (part + 1) * tile, :] = value[:, part * LANES : (part + 1) * LANES]

    sweep(put_layer, slice(cells, cells + 2 * LANES))


def turned(value):
    parts = [pltpu.roll(value[:, i : i + LANES], NY, 1) for i in range(0, value.shape[1], LANES)]
    return parts[0] if len(parts) == 1 else jnp.concatenate(parts, axis=1)


def couplings_kernel(ratio, slab, velocity_ref, cut_ref, *refs):
    *results, outer_ends, inner_ends = refs[-5:]
    outer, inner = refs[:4], refs[4:8]
    work = functools.partial(couple_tile, ratio, slab, velocity_ref, cut_ref)
    work(OUTER, *outer, inner[0], *results, outer_ends)
    work(INNER, *inner, outer[0], *results, inner_ends)


def couple_tile(ratio, slab, velocity_ref, cut_ref, side, first_ref, turned_ref, layer_ref, factor_ref, next_ref, keep, send, middle, ends_ref):
    slots, tile, cells = first_ref.shape
    steps = slots // 2
    steps_local = steps // 2
    depth = slab.shape[0]
    half = 2 * tile
    groups = cells // LANES
    core = this_core()
    own = pl.ds(pl.multiple_of(tile_rows(side, half, depth), 8), tile)
    held = slice(side * tile, (side + 1) * tile)
    out_shift, in_shift = z_shifts(tile)

    def one(group, carry):
        here = lane_block(group * LANES)
        left = lane_block(jnp.maximum(group - 1, 0) * LANES)
        right = lane_block(jnp.minimum(group + 1, groups - 1) * LANES)
        row = pl.ds(group, 1)
        beyond = jnp.where(cut_inside(), cut_ref[steps, row, :], 0.0) if side == OUTER else None
        weights = faces(side, slab, beyond, group, half)
        lane = lax.broadcasted_iota(jnp.int32, (tile, LANES), 1)
        low = lane < NY
        first, last = edge_rows((tile, LANES))
        drifts = [0.5 * velocity_ref[component, own, here] for component in (2, 0, 1)]
        drifts[0] = jnp.where(core == 0, -drifts[0], drifts[0])
        tables = []
        for sign in (1.0, -1.0):
            one_way, other_way = [], []
            for ((ahead, ok_ahead), (behind, ok_behind)), drift in zip(weights, drifts):
                one_way.append(jnp.where(ok_ahead, ahead - sign * drift, 0.0))
                other_way.append(jnp.where(ok_behind, behind + sign * drift, 0.0))
            x_same = jnp.where(low, one_way[1], other_way[1])
            x_next = jnp.where(low, other_way[1], one_way[1])
            tables.append((one_way[0], other_way[0], x_same, x_next, one_way[2], other_way[2]))
        factors = [factor_ref[slot, :, here] for slot in range(4)]

        def coupled(slot):
            c_out, c_in, x_same, x_next, c_ahead, c_behind = tables[slot % 2]
            value = first_ref[slot, :, here]
            following = next_ref[slot, :, here]
            cut = layer_ref[slot, row, :]
            if side == OUTER:
                outward = jnp.where(first, cut, pltpu.roll(value, out_shift, 0))
                inward = pltpu.roll(jnp.where(first, following, value), in_shift, 0)
            else:
                outward = pltpu.roll(jnp.where(last, following, value), out_shift, 0)
                inward = jnp.where(last, cut, pltpu.roll(value, in_shift, 0))
            result = c_out * outward + c_in * inward
            beside = jnp.where(low, turned_ref[slot, :, left], turned_ref[slot, :, right])
            result = result + (x_same * turned_ref[slot, :, here] + x_next * beside)
            return result + (c_ahead * pltpu.roll(value, LANES - 1, 1) + c_behind * pltpu.roll(value, 1, 1))

        results = {}
        ends = []
        for sub in range(2):
            offset = 2 * steps_local * sub
            drives = [coupled(offset + slot) for slot in range(2 * steps_local)]

            def put(step, state, adjoint):
                results[sub, step] = (state, adjoint)

            values = lambda step: (drives[2 * step], drives[2 * step + 1])
            ends.append(solve_steps(values, *factors, ratio, None, None, steps_local, put))
        for step in range(steps_local):
            for field in range(2):
                slot = 2 * step + field
                early, late = [
                    first_ref[2 * steps_local * sub + slot, :, here] + results[sub, step][field] for sub in range(2)
                ]
                keep[slot, held, here] = jnp.where(core == 0, early, late)
                send[slot, held, here] = jnp.where(core == 0, late, early)
        for slot, value in enumerate(finish_factors(ratio, factors)):
            send[2 * steps_local + slot, held, here] = value
        (early_back, early_last), (late_back, late_last) = ends
        decay, _, _, upright = factors
        block = power(decay, steps_local)
        middle[0, held, here] = late_back
        middle[1, held, here] = early_last
        ends_ref[0, :, here] = early_back + block * late_back
        ends_ref[1, :, here] = late_last + block * (early_last + response_of(decay, upright, steps_local) * late_back)
        return carry

    lax.fori_loop(0, groups, one, 0, unroll=UNROLL_COUPLINGS)


def finish_factors(ratio, factors):
    decay, _, mixed, upright = factors
    return decay, ratio * mixed, 0.5 * upright


def carry_kernel(side, steps_local, middle, factor_ref, *rest):
    *ends, keep, send = rest
    tile, cells = keep.shape[1:]
    held = slice(side * tile, (side + 1) * tile)
    core = this_core()

    def one(here):
        factors = [factor_ref[slot, :, here] for slot in range(4)]
        decay, _, _, upright = factors
        back, state = entering(factors, ends, here, 2 * steps_local)
        block = power(decay, steps_local)
        early_back = middle[0, held, here] + block * back
        late_state = middle[1, held, here] + block * state + response_of(decay, upright, steps_local) * early_back
        for slot, (early, late) in enumerate(((early_back, back), (state, late_state))):
            keep[slot, :, here] = jnp.where(core == 0, early, late)
            send[slot, :, here] = jnp.where(core == 0, late, early)

    each_block(cells, 4 * LANES, one)


def finish_kernel(jobs, ratio, chips, *refs):
    state_out, adjoint_out, result, sems = refs[-4:]
    steps_local, depth, cells = state_out.shape
    tile = depth // 4
    core = this_core()
    whole = step_scale(ratio, 2 * steps_local, chips, -1)
    scales = [jnp.where(core == 0, whole[step], whole[steps_local + step]) for step in range(steps_local)]
    copies = []
    for job, (theirs, side) in enumerate(jobs):
        parts, entered, factor_ref = refs[3 * job : 3 * job + 3]
        held = slice(side * tile, (side + 1) * tile)
        start = tile_rows(side, 2 * tile, depth)
        rows = pl.ds(pl.multiple_of(depth - tile - start if theirs else start, 8), tile)

        def one(here):
            if theirs:
                decay, gain, half_up = [parts[2 * steps_local + slot, held, here] for slot in range(3)]
            else:
                decay, gain, half_up = finish_factors(ratio, [factor_ref[slot, :, here] for slot in range(4)])
            backs = [entered[0, :, here]]
            for _ in range(steps_local):
                backs.append(decay * backs[-1])
            backs = backs[:0:-1]
            previous = entered[1, :, here]
            for step in range(steps_local):
                current = decay * previous + half_up * backs[step]
                adjoint = backs[step] - gain * previous
                result[job, 0, step, :, here] = (parts[2 * step, held, here] + current) * scales[step]
                result[job, 1, step, :, here] = (parts[2 * step + 1, held, here] + adjoint) * scales[step]
                previous = current

        each_block(cells, 4 * LANES, one)
        for field, out in enumerate((state_out, adjoint_out)):
            copies.append(pltpu.make_async_copy(result.at[job, field], out.at[:, rows, :], sems.at[job, field]))
            copies[-1].start()
    for copy in copies:
        copy.wait()


def body(state_rhs, adjoint_rhs, diffusivity, velocity):
    steps_local, depth, cells = state_rhs.shape
    ranks = lax.axis_size("tm")
    slabs = lax.axis_size("gz")
    chips = ranks // 2
    total = steps_local * ranks
    steps = 2 * steps_local
    half = depth // 2
    tile = half // 2
    groups = cells // LANES
    wide = cells + 2 * LANES
    ratio = alpha_wrap ** (1.0 / total)
    core = this_core()
    f32 = jnp.float32
    anywhere = pl.BlockSpec(memory_space=pl.ANY)
    vmem = pl.BlockSpec(memory_space=pltpu.VMEM)

    def partner(value, mask):
        return lax.ppermute(value, "tm", [(i, i ^ mask) for i in range(ranks)])

    def outward(value):
        spare = (4, 2) if ranks % 8 == 0 else (0, 0)
        pairs = []
        for t in range(ranks):
            for g in range(slabs):
                to = g - 1 if t % 2 == 0 else g + 1
                other = (t ^ 1) * slabs + to if 0 <= to < slabs else (t ^ spare[t % 2]) * slabs + g
                pairs.append((t * slabs + g, other))
        return lax.ppermute(value, ("tm", "gz"), pairs)

    def onward(value):
        pairs = []
        for t in range(ranks):
            for g in range(slabs):
                to = g + 1 if t % 2 == 0 else g - 1
                other = t * slabs + to if 0 <= to < slabs else (t ^ 1) * slabs + g
                pairs.append((t * slabs + g, other))
        return lax.ppermute(value, ("tm", "gz"), pairs)

    def call(kernel, name, out_shape, *args, **kwargs):
        shapes = [jax.ShapeDtypeStruct(s, f32) for s in out_shape]
        micros = next(value for word, value in MICROSECONDS.items() if word in name)
        return pl.pallas_call(
            kernel,
            out_shape=shapes,
            compiler_params=pltpu.CompilerParams(vmem_limit_bytes=32 * 1024 * 1024),
            cost_estimate=pl.CostEstimate(flops=0, transcendentals=0, bytes_accessed=int(micros * 3.7e6)),
            name=name,
            **kwargs,
        )(*args)

    layer = (groups, LANES)
    halves = (2, steps_local, half, cells + LANES)
    keep, send, slab, edge, edge_send, layers = call(
        pack_kernel,
        "halves_and_layers",
        [halves, halves, (depth, cells), (steps + 2,) + layer, (steps,) + layer, (4,) + layer],
        *[pltpu.with_memory_space_constraint(x, pltpu.HBM) for x in (state_rhs, adjoint_rhs, diffusivity)],
        in_specs=[anywhere] * 3,
        scratch_shapes=[pltpu.SemaphoreType.DMA((5,))],
    )
    other = partner(send, 1)
    cut = outward(edge)
    cut_straight = onward(edge_send)

    def first_ends(side, *args):
        return call(
            functools.partial(ends_kernel, side, ratio, chips),
            ("outer", "inner")[side] + "_ends",
            [(2 * steps, tile, wide), (4, tile, wide), (2, tile, wide)],
            keep,
            other,
            slab,
            layers,
            *args,
        )

    inner_raw, inner_factors, inner_ends = first_ends(INNER)
    outer_raw, outer_factors, outer_ends = first_ends(OUTER, cut, cut_straight, inner_ends)

    def beside(value, masks):
        return lax.ppermute(value, "tm", [(i, i ^ masks[i % 2]) for i in range(ranks)])

    def exchange(mine, factors):
        if chips != 4:
            return [gathered(mine, factors)]
        theirs = beside(mine, (2, 4))
        (passed,) = call(functools.partial(relay_kernel, steps), "relay", [mine.shape], factors, mine, theirs)
        return [mine, theirs, beside(passed, (4, 2))]

    def gathered(mine, factors):
        width = mine.shape[2]
        every = lax.dynamic_index_in_dim(
            lax.all_gather(mine, "tm").reshape((chips, 2) + mine.shape), core, 1, keepdims=False
        )
        block, response, closing = ring_factors([factors[i, :, :width] for i in range(4)], steps, chips)
        at = lambda array, index: lax.dynamic_index_in_dim(array, lax.rem(index + 2 * chips, chips), 0, keepdims=False)
        chip = this_chip()

        def entering_back(where):
            value = jnp.zeros((tile, width), f32)
            for offset in reversed(range(chips)):
                value = block * value + at(every[:, 0], where + 1 + offset)
            return value * closing

        value = jnp.zeros((tile, width), f32)
        for offset in reversed(range(chips)):
            source = chip - 1 - offset
            value = block * value + at(every[:, 1], source) + response * entering_back(source)
        return jnp.stack([entering_back(chip), value * closing])

    def first_sweep(side, raw, factors, ends):
        return call(
            functools.partial(sweep_kernel, ratio),
            ("outer", "inner")[side] + "_first_sweep",
            [(2 * steps, tile, cells)] * 2 + [(2 * steps,) + layer],
            raw,
            factors,
            *ends,
        )

    inner_first, inner_turned, inner_layer = first_sweep(
        INNER, inner_raw, inner_factors, exchange(inner_ends, inner_factors)
    )
    outer_first, outer_turned, outer_layer = first_sweep(
        OUTER, outer_raw, outer_factors, exchange(outer_ends, outer_factors)
    )

    keep, send, middle, *ends = call(
        functools.partial(couplings_kernel, ratio),
        "couplings",
        [(steps, half, cells), (steps + 3, half, cells), (2, half, cells), (2, tile, cells), (2, tile, cells)],
        slab,
        velocity,
        cut,
        outer_first,
        outer_turned,
        outer_layer,
        outer_factors,
        inner_first,
        inner_turned,
        inner_layer,
        inner_factors,
    )
    other = partner(send, 1)
    entered = [exchange(mine, table) for mine, table in zip(ends, (outer_factors, inner_factors))]
    factors = (outer_factors, inner_factors)

    def enter(side):
        own_in, send_in = call(
            functools.partial(carry_kernel, side, steps_local),
            ("outer", "inner")[side] + "_entering",
            [(2, tile, cells)] * 2,
            middle,
            factors[side],
            *entered[side],
        )
        return own_in, partner(send_in, 1)

    own_in, other_in = zip(enter(OUTER), enter(INNER))

    def finish(results, *jobs):
        args = []
        for theirs, side in jobs:
            args += [other if theirs else keep, (other_in if theirs else own_in)[side], factors[side]]
        return call(
            functools.partial(finish_kernel, jobs, ratio, chips),
            "finish",
            [(steps_local, depth, cells)] * 2,
            *args,
            *results,
            in_specs=[vmem] * len(args) + [anywhere] * len(results),
            out_specs=[anywhere] * 2,
            scratch_shapes=[
                pltpu.VMEM((len(jobs), 2, steps_local, tile, cells), f32),
                pltpu.SemaphoreType.DMA((len(jobs), 2)),
            ],
            input_output_aliases={len(args) + i: i for i in range(len(results))},
        )

    results = finish((), (False, OUTER), (False, INNER), (True, OUTER))
    return finish(results, (True, INNER))


def solution(mesh):
    placed = (P("tm", "gz", None), P("tm", "gz", None), P("gz", None), P(None, "gz", None))
    return jax.shard_map(
        body,
        mesh=mesh,
        in_specs=placed,
        out_specs=(P("tm", "gz", None), P("tm", "gz", None)),
        check_vma=False,
    )
```

```python
import functools
import math

import jax
import jax.numpy as jnp
from jax import lax
from jax.experimental import pallas as pl
from jax.experimental.pallas import tpu as pltpu
from jax.sharding import PartitionSpec as P

NY = 64
LANES = 128

alpha_wrap = 0.1
beta_couple = 0.5
gamma_couple = 0.5


def this_core():
    return lax.rem(lax.axis_index("tm"), 2)


def this_chip():
    return lax.div(lax.axis_index("tm"), 2)


def lane_block(start, width=LANES):
    return pl.ds(pl.multiple_of(start, LANES), width)


def each_block(cells, width, work, first=0):
    for start in range(0, cells, width):
        work(slice(first + start, first + min(start + width, cells)))


def power(value, count):
    result = None
    while count:
        if count & 1:
            result = value if result is None else result * value
        count >>= 1
        if count:
            value = value * value
    return result


def step_scale(ratio, steps, chips, sign):
    chip = this_chip()
    base = jnp.float32(1.0)
    bit = 0
    while 1 << bit < chips:
        factor = ratio ** (sign * steps * (1 << bit))
        base = base * jnp.where(lax.rem(lax.div(chip, 1 << bit), 2) == 1, factor, 1.0)
        bit += 1
    return [base * (ratio ** (sign * step)) for step in range(steps)]


OUTER, INNER = 0, 1
PIECES = 2
MICROSECONDS = {
    'halves': 2,
    'ends': 1,
    'relay': 0.2,
    'first_sweep': 1,
    'couplings': 3,
    'entering': 0.2,
    'finish': 1,
}
UNROLL_ENDS = 16
UNROLL_COUPLINGS = 16


def tile_rows(side, half, depth):
    core = this_core()
    tile = half // 2
    return core * (depth - tile) if side == OUTER else tile + core * tile


def faces(side, slab, outer, group, half):
    core = this_core()
    depth, cells = slab.shape
    tile = half // 2
    groups = cells // LANES
    own = pl.ds(pl.multiple_of(tile_rows(side, half, depth), 8), tile)
    here = lane_block(group * LANES)
    kappa = slab[own, here]
    left = slab[own, lane_block(jnp.maximum(group - 1, 0) * LANES)]
    right = slab[own, lane_block(jnp.minimum(group + 1, groups - 1) * LANES)]
    mirrored = lambda row: jnp.where(core == 0, slab[row : row + 1, here], slab[depth - 1 - row : depth - row, here])
    outward = outer if side == OUTER else mirrored(tile - 1)
    inward = mirrored(tile if side == OUTER else half)
    first, last = edge_rows(kappa.shape)
    shift, back = z_shifts(tile)
    lane = lax.broadcasted_iota(jnp.int32, kappa.shape, 1)
    column = lax.rem(lane, NY)
    low = lane < NY
    turned = pltpu.roll(kappa, NY, 1)
    outward = jnp.where(first, outward, pltpu.roll(kappa, shift, 0))
    inward = jnp.where(last, inward, pltpu.roll(kappa, back, 0))
    pairs = (
        ((outward, outward > 0.0), (inward, inward > 0.0)),
        (
            (jnp.where(low, turned, pltpu.roll(right, NY, 1)), jnp.logical_or(low, group < groups - 1)),
            (jnp.where(low, pltpu.roll(left, NY, 1), turned), jnp.logical_or(lane >= NY, group > 0)),
        ),
        ((pltpu.roll(kappa, LANES - 1, 1), column < NY - 1), (pltpu.roll(kappa, 1, 1), column > 0)),
    )
    return [[(jnp.where(ok, 0.5 * (kappa + value), kappa), ok) for value, ok in pair] for pair in pairs]


def cut_inside():
    slab = lax.axis_index("gz")
    return jnp.where(this_core() == 0, slab > 0, slab < lax.axis_size("gz") - 1)


def edge_rows(shape):
    core = this_core()
    row = lax.broadcasted_iota(jnp.int32, shape, 0)
    last = shape[0] - 1
    return row == core * last, row == (1 - core) * last


def z_shifts(tile):
    core = this_core()
    return 1 + core * (tile - 2), tile - 1 - core * (tile - 2)


def total_weight(weights):
    total = None
    for pair in weights:
        for weight, _ in pair:
            total = weight if total is None else total + weight
    return total


def layer_diagonal(kappa, ahead, behind):
    rows = kappa.shape[0]
    lane = lax.broadcasted_iota(jnp.int32, kappa.shape, 1)
    row = lax.broadcasted_iota(jnp.int32, kappa.shape, 0)
    column = lax.rem(lane, NY)
    turned = pltpu.roll(kappa, NY, 1)
    x_ahead = jnp.where(lane < NY, turned, pltpu.roll(turned, rows - 1, 0))
    x_behind = jnp.where(lane < NY, pltpu.roll(turned, 1, 0), turned)
    pairs = (
        (ahead, ahead > 0.0),
        (behind, behind > 0.0),
        (x_ahead, jnp.logical_or(lane < NY, row < rows - 1)),
        (x_behind, jnp.logical_or(lane >= NY, row > 0)),
        (pltpu.roll(kappa, LANES - 1, 1), column < NY - 1),
        (pltpu.roll(kappa, 1, 1), column > 0),
    )
    total = None
    for value, ok in pairs:
        weight = jnp.where(ok, 0.5 * (kappa + value), kappa)
        total = weight if total is None else total + weight
    return total


def cell_factors(diagonal, ratio):
    shifted = 1.0 + diagonal
    lifted = shifted * shifted - (ratio * ratio + beta_couple * gamma_couple)
    mix = shifted / (lifted + jnp.sqrt(lifted * lifted + shifted * shifted))
    inverse = 1.0 / (shifted + 0.5 * mix)
    return ratio * inverse, inverse, mix * inverse, 1.0 / shifted


def local_ends(values, decay, inverse, mixed, upright, steps):
    back = None
    last = None
    weight = None
    for step in reversed(range(steps)):
        state, adjoint = values(step)
        drive = inverse * adjoint - mixed * state
        back = drive if back is None else decay * back + drive
        term = state + 0.5 * back
        last = term if last is None else last + weight * term
        weight = decay if weight is None else weight * decay
    return back, last * upright


def solve_steps(values, decay, inverse, mixed, upright, ratio, back_in, state_in, steps, put):
    backs = [None] * steps
    back = back_in
    for step in reversed(range(steps)):
        state, adjoint = values(step)
        drive = inverse * adjoint - mixed * state
        back = drive if back is None else decay * back + drive
        backs[step] = back
    gain = ratio * mixed
    half_up = 0.5 * upright
    previous = state_in
    for step in range(steps):
        state, _ = values(step)
        current = upright * state + half_up * backs[step]
        adjoint = backs[step]
        if previous is not None:
            current = current + decay * previous
            adjoint = adjoint - gain * previous
        put(step, current, adjoint)
        previous = current
    return backs[0], previous


def pack_kernel(state, adjoint, kappa, keep, send, slab, edge, edge_send, layers, sems):
    steps_local, depth, cells = state.shape
    half = depth // 2
    core = this_core()
    mine = pl.ds(pl.multiple_of(core * half, 8), half)
    others = pl.ds(pl.multiple_of((1 - core) * half, 8), half)
    within = pl.ds(0, cells)
    copies = [pltpu.make_async_copy(kappa, slab, sems.at[4])]
    for field, source in enumerate((state, adjoint)):
        copies.append(pltpu.make_async_copy(source.at[:, mine, :], keep.at[field, :, :, within], sems.at[2 * field]))
        copies.append(pltpu.make_async_copy(source.at[:, others, :], send.at[field, :, :, within], sems.at[2 * field + 1]))
    for copy in copies:
        copy.start()

    def lay(source, rows, target):
        for group in range(cells // LANES):
            lanes = slice(group * LANES, (group + 1) * LANES)
            one, other = [source[row : row + 1, lanes] for row in rows]
            target[group : group + 1, :] = jnp.where(core == 0, one, other)

    slab_copy, *tile_copies = copies
    slab_copy.wait()
    last = depth - 1
    lay(slab, (0, last), edge.at[2 * steps_local])
    lay(slab, (1, last - 1), edge.at[2 * steps_local + 1])
    for slot, row in enumerate((0, half - 1, half, half + 1)):
        lay(slab, (row, last - row), layers.at[slot])
    near, far = (0, half - 1), (half - 1, 0)
    beyond = pl.ds(cells, LANES)
    for field in range(2):
        for copy in tile_copies[2 * field : 2 * field + 2]:
            copy.wait()
        for index in range(steps_local):
            slot = 2 * index + field
            lay(keep.at[field, index], near, edge.at[slot])
            lay(send.at[field, index], far, edge_send.at[slot])
            lay(send.at[field, index], near, keep.at[field, index, :, beyond])
            lay(keep.at[field, index], far, send.at[field, index, :, beyond])


def ends_kernel(side, ratio, chips, keep, other, slab, layers, *rest):
    cut, cut_straight = rest[:2] if side == OUTER else (None, None)
    raw_ref, factor_ref, ends_ref = rest[-3:]
    steps_local, half, cells = keep.shape[1:]
    cells = cells - LANES
    steps = 2 * steps_local
    tile = half // 2
    groups = cells // LANES
    core = this_core()
    scales = step_scale(ratio, steps, chips, 1)
    own = pl.ds(pl.multiple_of((core if side == OUTER else 1 - core) * tile, 8), tile)
    places = []
    for position in range(2):
        sub = core if position == 0 else 1 - core
        for index in range(steps_local):
            scale = jnp.where(sub == 0, scales[index], scales[steps_local + index])
            places.append((position, index, sub * steps + 2 * index, scale))

    def work(diagonal, loads, stores):
        factors = cell_factors(diagonal, ratio)
        for slot, value in enumerate(factors):
            stores(factor_ref, slot, value)
        for position, index, slot, scale in places:
            for field in range(2):
                stores(raw_ref, slot + field, loads(position, index, field) * scale)

    def put_ends(here):
        factors = [factor_ref[slot, :, here] for slot in range(4)]
        values = lambda step: (raw_ref[2 * step, :, here], raw_ref[2 * step + 1, :, here])
        for slot, value in enumerate(local_ends(values, *factors, steps)):
            ends_ref[slot, :, here] = value

    def one(group, carry):
        here = lane_block(group * LANES)
        beyond = jnp.where(cut_inside(), cut[steps, pl.ds(group, 1), :], 0.0) if side == OUTER else None
        diagonal = total_weight(faces(side, slab, beyond, group, half))

        def stores(ref, slot, value):
            ref[slot, :, here] = value

        work(diagonal, lambda position, index, field: (keep, other)[position][field, index, own, here], stores)
        put_ends(here)
        return carry

    lax.fori_loop(0, groups, one, 0, unroll=UNROLL_ENDS)

    def stores_cut(ref, slot, value):
        for part in range(2):
            lanes = slice(cells + part * LANES, cells + (part + 1) * LANES)
            ref[slot, :, lanes] = value[part * tile : (part + 1) * tile]

    if side == OUTER:
        diagonal = layer_diagonal(cut[steps], layers[0], cut[steps + 1])
        loads = lambda position, index, field: (cut_straight, cut)[position][2 * index + field]
    else:
        diagonal = layer_diagonal(layers[2], layers[1], layers[3])
        loads = lambda position, index, field: (keep, other)[position][field, index, :, cells:]
    work(diagonal, loads, stores_cut)
    for part in range(2):
        put_ends(slice(cells + part * LANES, cells + (part + 1) * LANES))


def power_sum(value, count):
    total = None
    for _ in range(count):
        total = 1.0 if total is None else 1.0 + value * total
    return total


def response_of(decay, upright, steps):
    return (0.5 * upright) * decay * power_sum(decay * decay, steps)


def ring_factors(factors, steps, chips):
    decay, _, _, upright = factors
    block = power(decay, steps)
    return block, response_of(decay, upright, steps), 1.0 / (1.0 - power(block, chips))


def choose(flag, one, other):
    return tuple(jnp.where(flag, a, b) for a, b in zip(one, other))


def ring_weights(factors, steps):
    block, response, closing = ring_factors(factors, steps, 4)
    square = block * block
    cross = response * closing * closing
    near = cross * block * (1.0 + square) * (1.0 + square)
    once = closing * block
    twice = closing * square
    thrice = once * square
    return (
        (thrice, thrice, cross * (1.0 + square) * (1.0 + square * square)),
        (closing, twice, near),
        (once, once, 2.0 * cross * square * (1.0 + square)),
        (twice, closing, near),
    )


def weighted(weights, ends):
    back, last = ends
    return weights[0] * back, weights[1] * last + weights[2] * back


def relay_kernel(steps, factor_ref, mine, theirs, passed):
    odd = lax.rem(this_chip(), 2) == 1
    along_x = this_core() == 0

    def one(here):
        _, next_, across, before = ring_weights([factor_ref[slot, :, here] for slot in range(4)], steps)
        beside = choose(odd, next_, before)
        a = weighted(choose(along_x, across, beside), (mine[0, :, here], mine[1, :, here]))
        b = weighted(choose(along_x, beside, choose(odd, before, next_)), (theirs[0, :, here], theirs[1, :, here]))
        passed[0, :, here] = a[0] + b[0]
        passed[1, :, here] = a[1] + b[1]

    each_block(mine.shape[2], 3 * LANES, one)


def entering(factors, ends, here, steps):
    if len(ends) == 1:
        return ends[0][0, :, here], ends[0][1, :, here]
    mine, theirs, tail = ends
    own, next_, across, before = ring_weights(factors, steps)
    odd = lax.rem(this_chip(), 2) == 1
    along_x = this_core() == 0
    a = weighted(own, (mine[0, :, here], mine[1, :, here]))
    b = weighted(choose(along_x, choose(odd, before, next_), across), (theirs[0, :, here], theirs[1, :, here]))
    return a[0] + b[0] + tail[0, :, here], a[1] + b[1] + tail[1, :, here]


def sweep_kernel(ratio, raw_ref, factor_ref, *rest):
    *ends, first_ref, turned_ref, layer_ref = rest
    tile = raw_ref.shape[1]
    steps = raw_ref.shape[0] // 2
    cells = first_ref.shape[2]

    def sweep(put, here):
        factors = [factor_ref[slot, :, here] for slot in range(4)]
        values = lambda step: (raw_ref[2 * step, :, here], raw_ref[2 * step + 1, :, here])
        solve_steps(values, *factors, ratio, *entering(factors, ends, here, steps), steps, put)

    def own(here):
        def put(step, state, adjoint):
            for field, value in enumerate((state, adjoint)):
                slot = 2 * step + field
                first_ref[slot, :, here] = value
                turned_ref[slot, :, here] = turned(value)

        sweep(put, here)

    each_block(cells, 4 * LANES, own)

    def put_layer(step, state, adjoint):
        for field, value in enumerate((state, adjoint)):
            for part in range(2):
                layer_ref[2 * step + field, part * tile : (part + 1) * tile, :] = value[:, part * LANES : (part + 1) * LANES]

    sweep(put_layer, slice(cells, cells + 2 * LANES))


def turned(value):
    parts = [pltpu.roll(value[:, i : i + LANES], NY, 1) for i in range(0, value.shape[1], LANES)]
    return parts[0] if len(parts) == 1 else jnp.concatenate(parts, axis=1)


def couplings_kernel(ratio, slab, velocity_ref, cut_ref, *refs):
    *results, outer_ends, inner_ends = refs[-5:]
    outer, inner = refs[:4], refs[4:8]
    work = functools.partial(couple_tile, ratio, slab, velocity_ref, cut_ref)
    work(OUTER, *outer, inner[0], *results, outer_ends)
    work(INNER, *inner, outer[0], *results, inner_ends)


def couple_tile(ratio, slab, velocity_ref, cut_ref, side, first_ref, turned_ref, layer_ref, factor_ref, next_ref, keep, send, middle, ends_ref):
    slots, tile, cells = first_ref.shape
    steps = slots // 2
    steps_local = steps // 2
    depth = slab.shape[0]
    half = 2 * tile
    groups = cells // LANES
    core = this_core()
    own = pl.ds(pl.multiple_of(tile_rows(side, half, depth), 8), tile)
    held = slice(side * tile, (side + 1) * tile)
    out_shift, in_shift = z_shifts(tile)

    def one(group, carry):
        here = lane_block(group * LANES)
        left = lane_block(jnp.maximum(group - 1, 0) * LANES)
        right = lane_block(jnp.minimum(group + 1, groups - 1) * LANES)
        row = pl.ds(group, 1)
        beyond = jnp.where(cut_inside(), cut_ref[steps, row, :], 0.0) if side == OUTER else None
        weights = faces(side, slab, beyond, group, half)
        lane = lax.broadcasted_iota(jnp.int32, (tile, LANES), 1)
        low = lane < NY
        first, last = edge_rows((tile, LANES))
        drifts = [0.5 * velocity_ref[component, own, here] for component in (2, 0, 1)]
        drifts[0] = jnp.where(core == 0, -drifts[0], drifts[0])
        tables = []
        for sign in (1.0, -1.0):
            one_way, other_way = [], []
            for ((ahead, ok_ahead), (behind, ok_behind)), drift in zip(weights, drifts):
                one_way.append(jnp.where(ok_ahead, ahead - sign * drift, 0.0))
                other_way.append(jnp.where(ok_behind, behind + sign * drift, 0.0))
            x_same = jnp.where(low, one_way[1], other_way[1])
            x_next = jnp.where(low, other_way[1], one_way[1])
            tables.append((one_way[0], other_way[0], x_same, x_next, one_way[2], other_way[2]))
        factors = [factor_ref[slot, :, here] for slot in range(4)]

        def coupled(slot):
            c_out, c_in, x_same, x_next, c_ahead, c_behind = tables[slot % 2]
            value = first_ref[slot, :, here]
            following = next_ref[slot, :, here]
            cut = layer_ref[slot, row, :]
            if side == OUTER:
                outward = jnp.where(first, cut, pltpu.roll(value, out_shift, 0))
                inward = pltpu.roll(jnp.where(first, following, value), in_shift, 0)
            else:
                outward = pltpu.roll(jnp.where(last, following, value), out_shift, 0)
                inward = jnp.where(last, cut, pltpu.roll(value, in_shift, 0))
            result = c_out * outward + c_in * inward
            beside = jnp.where(low, turned_ref[slot, :, left], turned_ref[slot, :, right])
            result = result + (x_same * turned_ref[slot, :, here] + x_next * beside)
            return result + (c_ahead * pltpu.roll(value, LANES - 1, 1) + c_behind * pltpu.roll(value, 1, 1))

        results = {}
        ends = []
        for sub in range(2):
            offset = 2 * steps_local * sub
            drives = [coupled(offset + slot) for slot in range(2 * steps_local)]

            def put(step, state, adjoint):
                results[sub, step] = (state, adjoint)

            values = lambda step: (drives[2 * step], drives[2 * step + 1])
            ends.append(solve_steps(values, *factors, ratio, None, None, steps_local, put))
        for step in range(steps_local):
            for field in range(2):
                slot = 2 * step + field
                early, late = [
                    first_ref[2 * steps_local * sub + slot, :, here] + results[sub, step][field] for sub in range(2)
                ]
                keep[slot, held, here] = jnp.where(core == 0, early, late)
                send[slot, held, here] = jnp.where(core == 0, late, early)
        for slot, value in enumerate(finish_factors(ratio, factors)):
            send[2 * steps_local + slot, held, here] = value
        (early_back, early_last), (late_back, late_last) = ends
        decay, _, _, upright = factors
        block = power(decay, steps_local)
        middle[0, held, here] = late_back
        middle[1, held, here] = early_last
        ends_ref[0, :, here] = early_back + block * late_back
        ends_ref[1, :, here] = late_last + block * (early_last + response_of(decay, upright, steps_local) * late_back)
        return carry

    lax.fori_loop(0, groups, one, 0, unroll=UNROLL_COUPLINGS)


def finish_factors(ratio, factors):
    decay, _, mixed, upright = factors
    return decay, ratio * mixed, 0.5 * upright


def carry_kernel(side, steps_local, middle, factor_ref, *rest):
    *ends, keep, send = rest
    tile, cells = keep.shape[1:]
    held = slice(side * tile, (side + 1) * tile)
    core = this_core()

    def one(here):
        factors = [factor_ref[slot, :, here] for slot in range(4)]
        decay, _, _, upright = factors
        back, state = entering(factors, ends, here, 2 * steps_local)
        block = power(decay, steps_local)
        early_back = middle[0, held, here] + block * back
        late_state = middle[1, held, here] + block * state + response_of(decay, upright, steps_local) * early_back
        for slot, (early, late) in enumerate(((early_back, back), (state, late_state))):
            keep[slot, :, here] = jnp.where(core == 0, early, late)
            send[slot, :, here] = jnp.where(core == 0, late, early)

    each_block(cells, 4 * LANES, one)


def finish_kernel(jobs, ratio, chips, *refs):
    state_out, adjoint_out, result, sems = refs[-4:]
    steps_local, depth, cells = state_out.shape
    tile = depth // 4
    core = this_core()
    whole = step_scale(ratio, 2 * steps_local, chips, -1)
    scales = [jnp.where(core == 0, whole[step], whole[steps_local + step]) for step in range(steps_local)]
    copies = []
    for job, (theirs, side) in enumerate(jobs):
        parts, entered, factor_ref = refs[3 * job : 3 * job + 3]
        held = slice(side * tile, (side + 1) * tile)
        start = tile_rows(side, 2 * tile, depth)
        rows = pl.ds(pl.multiple_of(depth - tile - start if theirs else start, 8), tile)

        def one(here):
            if theirs:
                decay, gain, half_up = [parts[2 * steps_local + slot, held, here] for slot in range(3)]
            else:
                decay, gain, half_up = finish_factors(ratio, [factor_ref[slot, :, here] for slot in range(4)])
            backs = [entered[0, :, here]]
            for _ in range(steps_local):
                backs.append(decay * backs[-1])
            backs = backs[:0:-1]
            previous = entered[1, :, here]
            for step in range(steps_local):
                current = decay * previous + half_up * backs[step]
                adjoint = backs[step] - gain * previous
                result[job, 0, step, :, here] = (parts[2 * step, held, here] + current) * scales[step]
                result[job, 1, step, :, here] = (parts[2 * step + 1, held, here] + adjoint) * scales[step]
                previous = current

        for piece in range(PIECES):
            first = piece * (cells // PIECES)
            each_block(cells // PIECES, 4 * LANES, one, first)
            lanes = pl.ds(first, cells // PIECES)
            for field, out in enumerate((state_out, adjoint_out)):
                copies.append(
                    pltpu.make_async_copy(
                        result.at[job, field, :, :, lanes], out.at[:, rows, lanes], sems.at[job, field, piece]
                    )
                )
                copies[-1].start()
    for copy in copies:
        copy.wait()


def body(state_rhs, adjoint_rhs, diffusivity, velocity):
    steps_local, depth, cells = state_rhs.shape
    ranks = lax.axis_size("tm")
    slabs = lax.axis_size("gz")
    chips = ranks // 2
    total = steps_local * ranks
    steps = 2 * steps_local
    half = depth // 2
    tile = half // 2
    groups = cells // LANES
    wide = cells + 2 * LANES
    ratio = alpha_wrap ** (1.0 / total)
    core = this_core()
    f32 = jnp.float32
    anywhere = pl.BlockSpec(memory_space=pl.ANY)
    vmem = pl.BlockSpec(memory_space=pltpu.VMEM)

    def partner(value, mask):
        return lax.ppermute(value, "tm", [(i, i ^ mask) for i in range(ranks)])

    def outward(value):
        spare = (4, 2) if ranks % 8 == 0 else (0, 0)
        pairs = []
        for t in range(ranks):
            for g in range(slabs):
                to = g - 1 if t % 2 == 0 else g + 1
                other = (t ^ 1) * slabs + to if 0 <= to < slabs else (t ^ spare[t % 2]) * slabs + g
                pairs.append((t * slabs + g, other))
        return lax.ppermute(value, ("tm", "gz"), pairs)

    def onward(value):
        pairs = []
        for t in range(ranks):
            for g in range(slabs):
                to = g + 1 if t % 2 == 0 else g - 1
                other = t * slabs + to if 0 <= to < slabs else (t ^ 1) * slabs + g
                pairs.append((t * slabs + g, other))
        return lax.ppermute(value, ("tm", "gz"), pairs)

    def call(kernel, name, out_shape, *args, **kwargs):
        shapes = [jax.ShapeDtypeStruct(s, f32) for s in out_shape]
        micros = next(value for word, value in MICROSECONDS.items() if word in name)
        return pl.pallas_call(
            kernel,
            out_shape=shapes,
            compiler_params=pltpu.CompilerParams(vmem_limit_bytes=32 * 1024 * 1024),
            cost_estimate=pl.CostEstimate(flops=0, transcendentals=0, bytes_accessed=int(micros * 3.7e6)),
            name=name,
            **kwargs,
        )(*args)

    layer = (groups, LANES)
    halves = (2, steps_local, half, cells + LANES)
    keep, send, slab, edge, edge_send, layers = call(
        pack_kernel,
        "halves_and_layers",
        [halves, halves, (depth, cells), (steps + 2,) + layer, (steps,) + layer, (4,) + layer],
        *[pltpu.with_memory_space_constraint(x, pltpu.HBM) for x in (state_rhs, adjoint_rhs, diffusivity)],
        in_specs=[anywhere] * 3,
        scratch_shapes=[pltpu.SemaphoreType.DMA((5,))],
    )
    other = partner(send, 1)
    cut = outward(edge)
    cut_straight = onward(edge_send)

    def first_ends(side, *args):
        return call(
            functools.partial(ends_kernel, side, ratio, chips),
            ("outer", "inner")[side] + "_ends",
            [(2 * steps, tile, wide), (4, tile, wide), (2, tile, wide)],
            keep,
            other,
            slab,
            layers,
            *args,
        )

    inner_raw, inner_factors, inner_ends = first_ends(INNER)
    outer_raw, outer_factors, outer_ends = first_ends(OUTER, cut, cut_straight, inner_ends)

    def beside(value, masks):
        return lax.ppermute(value, "tm", [(i, i ^ masks[i % 2]) for i in range(ranks)])

    def exchange(mine, factors):
        if chips != 4:
            return [gathered(mine, factors)]
        theirs = beside(mine, (2, 4))
        (passed,) = call(functools.partial(relay_kernel, steps), "relay", [mine.shape], factors, mine, theirs)
        return [mine, theirs, beside(passed, (4, 2))]

    def gathered(mine, factors):
        width = mine.shape[2]
        every = lax.dynamic_index_in_dim(
            lax.all_gather(mine, "tm").reshape((chips, 2) + mine.shape), core, 1, keepdims=False
        )
        block, response, closing = ring_factors([factors[i, :, :width] for i in range(4)], steps, chips)
        at = lambda array, index: lax.dynamic_index_in_dim(array, lax.rem(index + 2 * chips, chips), 0, keepdims=False)
        chip = this_chip()

        def entering_back(where):
            value = jnp.zeros((tile, width), f32)
            for offset in reversed(range(chips)):
                value = block * value + at(every[:, 0], where + 1 + offset)
            return value * closing

        value = jnp.zeros((tile, width), f32)
        for offset in reversed(range(chips)):
            source = chip - 1 - offset
            value = block * value + at(every[:, 1], source) + response * entering_back(source)
        return jnp.stack([entering_back(chip), value * closing])

    def first_sweep(side, raw, factors, ends):
        return call(
            functools.partial(sweep_kernel, ratio),
            ("outer", "inner")[side] + "_first_sweep",
            [(2 * steps, tile, cells)] * 2 + [(2 * steps,) + layer],
            raw,
            factors,
            *ends,
        )

    inner_first, inner_turned, inner_layer = first_sweep(
        INNER, inner_raw, inner_factors, exchange(inner_ends, inner_factors)
    )
    outer_first, outer_turned, outer_layer = first_sweep(
        OUTER, outer_raw, outer_factors, exchange(outer_ends, outer_factors)
    )

    keep, send, middle, *ends = call(
        functools.partial(couplings_kernel, ratio),
        "couplings",
        [(steps, half, cells), (steps + 3, half, cells), (2, half, cells), (2, tile, cells), (2, tile, cells)],
        slab,
        velocity,
        cut,
        outer_first,
        outer_turned,
        outer_layer,
        outer_factors,
        inner_first,
        inner_turned,
        inner_layer,
        inner_factors,
    )
    other = partner(send, 1)
    entered = [exchange(mine, table) for mine, table in zip(ends, (outer_factors, inner_factors))]
    factors = (outer_factors, inner_factors)

    def enter(side):
        own_in, send_in = call(
            functools.partial(carry_kernel, side, steps_local),
            ("outer", "inner")[side] + "_entering",
            [(2, tile, cells)] * 2,
            middle,
            factors[side],
            *entered[side],
        )
        return own_in, partner(send_in, 1)

    own_in, other_in = zip(enter(OUTER), enter(INNER))

    def finish(results, *jobs):
        args = []
        for theirs, side in jobs:
            args += [other if theirs else keep, (other_in if theirs else own_in)[side], factors[side]]
        return call(
            functools.partial(finish_kernel, jobs, ratio, chips),
            "finish",
            [(steps_local, depth, cells)] * 2,
            *args,
            *results,
            in_specs=[vmem] * len(args) + [anywhere] * len(results),
            out_specs=[anywhere] * 2,
            scratch_shapes=[
                pltpu.VMEM((len(jobs), 2, steps_local, tile, cells), f32),
                pltpu.SemaphoreType.DMA((len(jobs), 2, PIECES)),
            ],
            input_output_aliases={len(args) + i: i for i in range(len(results))},
        )

    results = finish((), (False, OUTER), (False, INNER), (True, OUTER))
    return finish(results, (True, INNER))


def solution(mesh):
    placed = (P("tm", "gz", None), P("tm", "gz", None), P("gz", None), P(None, "gz", None))
    return jax.shard_map(
        body,
        mesh=mesh,
        in_specs=placed,
        out_specs=(P("tm", "gz", None), P("tm", "gz", None)),
        check_vma=False,
    )
```

```python
import functools
import math

import jax
import jax.numpy as jnp
from jax import lax
from jax.experimental import pallas as pl
from jax.experimental.pallas import tpu as pltpu
from jax.sharding import PartitionSpec as P

NY = 64
LANES = 128

alpha_wrap = 0.1
beta_couple = 0.5
gamma_couple = 0.5


FIXED = []


def this_core():
    return FIXED[-1] if FIXED else lax.rem(lax.axis_index("tm"), 2)


def pick(flag, one, other):
    if isinstance(flag, bool):
        return one if flag else other
    return jnp.where(flag, one, other)


def aligned(start, size):
    return slice(start, start + size) if isinstance(start, int) else pl.ds(pl.multiple_of(start, 8), size)


def this_chip():
    return lax.div(lax.axis_index("tm"), 2)


def lane_block(start, width=LANES):
    return pl.ds(pl.multiple_of(start, LANES), width)


def each_block(cells, width, work, first=0):
    for start in range(0, cells, width):
        work(slice(first + start, first + min(start + width, cells)))


def power(value, count):
    result = None
    while count:
        if count & 1:
            result = value if result is None else result * value
        count >>= 1
        if count:
            value = value * value
    return result


def step_scale(ratio, steps, chips, sign):
    chip = this_chip()
    base = jnp.float32(1.0)
    bit = 0
    while 1 << bit < chips:
        factor = ratio ** (sign * steps * (1 << bit))
        base = base * jnp.where(lax.rem(lax.div(chip, 1 << bit), 2) == 1, factor, 1.0)
        bit += 1
    return [base * (ratio ** (sign * step)) for step in range(steps)]


OUTER, INNER = 0, 1
PIECES = 2
MICROSECONDS = {
    'halves': 2,
    'ends': 1,
    'relay': 0.2,
    'first_sweep': 1,
    'couplings': 3,
    'entering': 0.2,
    'finish': 1,
}
UNROLL_ENDS = 16
UNROLL_COUPLINGS = 16


def tile_rows(side, half, depth):
    core = this_core()
    tile = half // 2
    return core * (depth - tile) if side == OUTER else tile + core * tile


def faces(side, slab, outer, group, half):
    core = this_core()
    depth, cells = slab.shape
    tile = half // 2
    groups = cells // LANES
    own = aligned(tile_rows(side, half, depth), tile)
    here = lane_block(group * LANES)
    kappa = slab[own, here]
    left = slab[own, lane_block(jnp.maximum(group - 1, 0) * LANES)]
    right = slab[own, lane_block(jnp.minimum(group + 1, groups - 1) * LANES)]
    mirrored = lambda row: pick(core == 0, slab[row : row + 1, here], slab[depth - 1 - row : depth - row, here])
    outward = outer if side == OUTER else mirrored(tile - 1)
    inward = mirrored(tile if side == OUTER else half)
    first, last = edge_rows(kappa.shape)
    shift, back = z_shifts(tile)
    lane = lax.broadcasted_iota(jnp.int32, kappa.shape, 1)
    column = lax.rem(lane, NY)
    low = lane < NY
    turned = pltpu.roll(kappa, NY, 1)
    outward = jnp.where(first, outward, pltpu.roll(kappa, shift, 0))
    inward = jnp.where(last, inward, pltpu.roll(kappa, back, 0))
    pairs = (
        ((outward, outward > 0.0), (inward, inward > 0.0)),
        (
            (jnp.where(low, turned, pltpu.roll(right, NY, 1)), jnp.logical_or(low, group < groups - 1)),
            (jnp.where(low, pltpu.roll(left, NY, 1), turned), jnp.logical_or(lane >= NY, group > 0)),
        ),
        ((pltpu.roll(kappa, LANES - 1, 1), column < NY - 1), (pltpu.roll(kappa, 1, 1), column > 0)),
    )
    return [[(jnp.where(ok, 0.5 * (kappa + value), kappa), ok) for value, ok in pair] for pair in pairs]


def cut_inside():
    slab = lax.axis_index("gz")
    return pick(this_core() == 0, slab > 0, slab < lax.axis_size("gz") - 1)


def edge_rows(shape):
    core = this_core()
    row = lax.broadcasted_iota(jnp.int32, shape, 0)
    last = shape[0] - 1
    return row == core * last, row == (1 - core) * last


def z_shifts(tile):
    core = this_core()
    return 1 + core * (tile - 2), tile - 1 - core * (tile - 2)


def total_weight(weights):
    total = None
    for pair in weights:
        for weight, _ in pair:
            total = weight if total is None else total + weight
    return total


def layer_diagonal(kappa, ahead, behind):
    rows = kappa.shape[0]
    lane = lax.broadcasted_iota(jnp.int32, kappa.shape, 1)
    row = lax.broadcasted_iota(jnp.int32, kappa.shape, 0)
    column = lax.rem(lane, NY)
    turned = pltpu.roll(kappa, NY, 1)
    x_ahead = jnp.where(lane < NY, turned, pltpu.roll(turned, rows - 1, 0))
    x_behind = jnp.where(lane < NY, pltpu.roll(turned, 1, 0), turned)
    pairs = (
        (ahead, ahead > 0.0),
        (behind, behind > 0.0),
        (x_ahead, jnp.logical_or(lane < NY, row < rows - 1)),
        (x_behind, jnp.logical_or(lane >= NY, row > 0)),
        (pltpu.roll(kappa, LANES - 1, 1), column < NY - 1),
        (pltpu.roll(kappa, 1, 1), column > 0),
    )
    total = None
    for value, ok in pairs:
        weight = jnp.where(ok, 0.5 * (kappa + value), kappa)
        total = weight if total is None else total + weight
    return total


def cell_factors(diagonal, ratio):
    shifted = 1.0 + diagonal
    lifted = shifted * shifted - (ratio * ratio + beta_couple * gamma_couple)
    mix = shifted / (lifted + jnp.sqrt(lifted * lifted + shifted * shifted))
    inverse = 1.0 / (shifted + 0.5 * mix)
    return ratio * inverse, inverse, mix * inverse, 1.0 / shifted


def local_ends(values, decay, inverse, mixed, upright, steps):
    back = None
    last = None
    weight = None
    for step in reversed(range(steps)):
        state, adjoint = values(step)
        drive = inverse * adjoint - mixed * state
        back = drive if back is None else decay * back + drive
        term = state + 0.5 * back
        last = term if last is None else last + weight * term
        weight = decay if weight is None else weight * decay
    return back, last * upright


def solve_steps(values, decay, inverse, mixed, upright, ratio, back_in, state_in, steps, put):
    backs = [None] * steps
    back = back_in
    for step in reversed(range(steps)):
        state, adjoint = values(step)
        drive = inverse * adjoint - mixed * state
        back = drive if back is None else decay * back + drive
        backs[step] = back
    gain = ratio * mixed
    half_up = 0.5 * upright
    previous = state_in
    for step in range(steps):
        state, _ = values(step)
        current = upright * state + half_up * backs[step]
        adjoint = backs[step]
        if previous is not None:
            current = current + decay * previous
            adjoint = adjoint - gain * previous
        put(step, current, adjoint)
        previous = current
    return backs[0], previous


def pack_kernel(state, adjoint, kappa, keep, send, slab, edge, edge_send, layers, sems):
    steps_local, depth, cells = state.shape
    half = depth // 2
    core = this_core()
    mine = pl.ds(pl.multiple_of(core * half, 8), half)
    others = pl.ds(pl.multiple_of((1 - core) * half, 8), half)
    within = pl.ds(0, cells)
    copies = [pltpu.make_async_copy(kappa, slab, sems.at[4])]
    for field, source in enumerate((state, adjoint)):
        copies.append(pltpu.make_async_copy(source.at[:, mine, :], keep.at[field, :, :, within], sems.at[2 * field]))
        copies.append(pltpu.make_async_copy(source.at[:, others, :], send.at[field, :, :, within], sems.at[2 * field + 1]))
    for copy in copies:
        copy.start()

    def lay(source, rows, target):
        for group in range(cells // LANES):
            lanes = slice(group * LANES, (group + 1) * LANES)
            one, other = [source[row : row + 1, lanes] for row in rows]
            target[group : group + 1, :] = pick(core == 0, one, other)

    slab_copy, *tile_copies = copies
    slab_copy.wait()
    last = depth - 1
    lay(slab, (0, last), edge.at[2 * steps_local])
    lay(slab, (1, last - 1), edge.at[2 * steps_local + 1])
    for slot, row in enumerate((0, half - 1, half, half + 1)):
        lay(slab, (row, last - row), layers.at[slot])
    near, far = (0, half - 1), (half - 1, 0)
    beyond = pl.ds(cells, LANES)
    for field in range(2):
        for copy in tile_copies[2 * field : 2 * field + 2]:
            copy.wait()
        for index in range(steps_local):
            slot = 2 * index + field
            lay(keep.at[field, index], near, edge.at[slot])
            lay(send.at[field, index], far, edge_send.at[slot])
            lay(send.at[field, index], near, keep.at[field, index, :, beyond])
            lay(keep.at[field, index], far, send.at[field, index, :, beyond])


def ends_kernel(side, ratio, chips, keep, other, slab, layers, *rest):
    cut, cut_straight = rest[:2] if side == OUTER else (None, None)
    raw_ref, factor_ref, ends_ref = rest[-3:]
    steps_local, half, cells = keep.shape[1:]
    cells = cells - LANES
    steps = 2 * steps_local
    tile = half // 2
    groups = cells // LANES
    core = this_core()
    scales = step_scale(ratio, steps, chips, 1)
    own = pl.ds(pl.multiple_of((core if side == OUTER else 1 - core) * tile, 8), tile)
    places = []
    for position in range(2):
        sub = core if position == 0 else 1 - core
        for index in range(steps_local):
            scale = jnp.where(sub == 0, scales[index], scales[steps_local + index])
            places.append((position, index, sub * steps + 2 * index, scale))

    def work(diagonal, loads, stores):
        factors = cell_factors(diagonal, ratio)
        for slot, value in enumerate(factors):
            stores(factor_ref, slot, value)
        for position, index, slot, scale in places:
            for field in range(2):
                stores(raw_ref, slot + field, loads(position, index, field) * scale)

    def put_ends(here):
        factors = [factor_ref[slot, :, here] for slot in range(4)]
        values = lambda step: (raw_ref[2 * step, :, here], raw_ref[2 * step + 1, :, here])
        for slot, value in enumerate(local_ends(values, *factors, steps)):
            ends_ref[slot, :, here] = value

    def one(group, carry):
        here = lane_block(group * LANES)
        beyond = jnp.where(cut_inside(), cut[steps, pl.ds(group, 1), :], 0.0) if side == OUTER else None
        diagonal = total_weight(faces(side, slab, beyond, group, half))

        def stores(ref, slot, value):
            ref[slot, :, here] = value

        work(diagonal, lambda position, index, field: (keep, other)[position][field, index, own, here], stores)
        put_ends(here)
        return carry

    lax.fori_loop(0, groups, one, 0, unroll=UNROLL_ENDS)

    def stores_cut(ref, slot, value):
        for part in range(2):
            lanes = slice(cells + part * LANES, cells + (part + 1) * LANES)
            ref[slot, :, lanes] = value[part * tile : (part + 1) * tile]

    if side == OUTER:
        diagonal = layer_diagonal(cut[steps], layers[0], cut[steps + 1])
        loads = lambda position, index, field: (cut_straight, cut)[position][2 * index + field]
    else:
        diagonal = layer_diagonal(layers[2], layers[1], layers[3])
        loads = lambda position, index, field: (keep, other)[position][field, index, :, cells:]
    work(diagonal, loads, stores_cut)
    for part in range(2):
        put_ends(slice(cells + part * LANES, cells + (part + 1) * LANES))


def power_sum(value, count):
    total = None
    for _ in range(count):
        total = 1.0 if total is None else 1.0 + value * total
    return total


def response_of(decay, upright, steps):
    return (0.5 * upright) * decay * power_sum(decay * decay, steps)


def ring_factors(factors, steps, chips):
    decay, _, _, upright = factors
    block = power(decay, steps)
    return block, response_of(decay, upright, steps), 1.0 / (1.0 - power(block, chips))


def choose(flag, one, other):
    return tuple(jnp.where(flag, a, b) for a, b in zip(one, other))


def ring_weights(factors, steps):
    block, response, closing = ring_factors(factors, steps, 4)
    square = block * block
    cross = response * closing * closing
    near = cross * block * (1.0 + square) * (1.0 + square)
    once = closing * block
    twice = closing * square
    thrice = once * square
    return (
        (thrice, thrice, cross * (1.0 + square) * (1.0 + square * square)),
        (closing, twice, near),
        (once, once, 2.0 * cross * square * (1.0 + square)),
        (twice, closing, near),
    )


def weighted(weights, ends):
    back, last = ends
    return weights[0] * back, weights[1] * last + weights[2] * back


def relay_kernel(steps, factor_ref, mine, theirs, passed):
    odd = lax.rem(this_chip(), 2) == 1
    along_x = this_core() == 0

    def one(here):
        _, next_, across, before = ring_weights([factor_ref[slot, :, here] for slot in range(4)], steps)
        beside = choose(odd, next_, before)
        a = weighted(choose(along_x, across, beside), (mine[0, :, here], mine[1, :, here]))
        b = weighted(choose(along_x, beside, choose(odd, before, next_)), (theirs[0, :, here], theirs[1, :, here]))
        passed[0, :, here] = a[0] + b[0]
        passed[1, :, here] = a[1] + b[1]

    each_block(mine.shape[2], 3 * LANES, one)


def entering(factors, ends, here, steps):
    if len(ends) == 1:
        return ends[0][0, :, here], ends[0][1, :, here]
    mine, theirs, tail = ends
    own, next_, across, before = ring_weights(factors, steps)
    odd = lax.rem(this_chip(), 2) == 1
    along_x = this_core() == 0
    a = weighted(own, (mine[0, :, here], mine[1, :, here]))
    b = weighted(choose(along_x, choose(odd, before, next_), across), (theirs[0, :, here], theirs[1, :, here]))
    return a[0] + b[0] + tail[0, :, here], a[1] + b[1] + tail[1, :, here]


def sweep_kernel(ratio, raw_ref, factor_ref, *rest):
    *ends, first_ref, turned_ref, layer_ref = rest
    tile = raw_ref.shape[1]
    steps = raw_ref.shape[0] // 2
    cells = first_ref.shape[2]

    def sweep(put, here):
        factors = [factor_ref[slot, :, here] for slot in range(4)]
        values = lambda step: (raw_ref[2 * step, :, here], raw_ref[2 * step + 1, :, here])
        solve_steps(values, *factors, ratio, *entering(factors, ends, here, steps), steps, put)

    def own(here):
        def put(step, state, adjoint):
            for field, value in enumerate((state, adjoint)):
                slot = 2 * step + field
                first_ref[slot, :, here] = value
                turned_ref[slot, :, here] = turned(value)

        sweep(put, here)

    each_block(cells, 4 * LANES, own)

    def put_layer(step, state, adjoint):
        for field, value in enumerate((state, adjoint)):
            for part in range(2):
                layer_ref[2 * step + field, part * tile : (part + 1) * tile, :] = value[:, part * LANES : (part + 1) * LANES]

    sweep(put_layer, slice(cells, cells + 2 * LANES))


def turned(value):
    parts = [pltpu.roll(value[:, i : i + LANES], NY, 1) for i in range(0, value.shape[1], LANES)]
    return parts[0] if len(parts) == 1 else jnp.concatenate(parts, axis=1)


def couplings_kernel(ratio, *refs):
    core = this_core()

    def work(which):
        FIXED.append(which)
        couple_tiles(ratio, *refs)
        FIXED.pop()

    for which in range(2):
        pl.when(core == which)(functools.partial(work, which))


def couple_tiles(ratio, slab, velocity_ref, cut_ref, *refs):
    *results, outer_ends, inner_ends = refs[-5:]
    outer, inner = refs[:4], refs[4:8]
    work = functools.partial(couple_tile, ratio, slab, velocity_ref, cut_ref)
    work(OUTER, *outer, inner[0], *results, outer_ends)
    work(INNER, *inner, outer[0], *results, inner_ends)


def couple_tile(ratio, slab, velocity_ref, cut_ref, side, first_ref, turned_ref, layer_ref, factor_ref, next_ref, keep, send, middle, ends_ref):
    slots, tile, cells = first_ref.shape
    steps = slots // 2
    steps_local = steps // 2
    depth = slab.shape[0]
    half = 2 * tile
    groups = cells // LANES
    core = this_core()
    own = aligned(tile_rows(side, half, depth), tile)
    held = slice(side * tile, (side + 1) * tile)
    out_shift, in_shift = z_shifts(tile)

    def one(group, carry):
        here = lane_block(group * LANES)
        left = lane_block(jnp.maximum(group - 1, 0) * LANES)
        right = lane_block(jnp.minimum(group + 1, groups - 1) * LANES)
        row = pl.ds(group, 1)
        beyond = jnp.where(cut_inside(), cut_ref[steps, row, :], 0.0) if side == OUTER else None
        weights = faces(side, slab, beyond, group, half)
        lane = lax.broadcasted_iota(jnp.int32, (tile, LANES), 1)
        low = lane < NY
        first, last = edge_rows((tile, LANES))
        drifts = [0.5 * velocity_ref[component, own, here] for component in (2, 0, 1)]
        drifts[0] = pick(core == 0, -drifts[0], drifts[0])
        tables = []
        for sign in (1.0, -1.0):
            one_way, other_way = [], []
            for ((ahead, ok_ahead), (behind, ok_behind)), drift in zip(weights, drifts):
                one_way.append(jnp.where(ok_ahead, ahead - sign * drift, 0.0))
                other_way.append(jnp.where(ok_behind, behind + sign * drift, 0.0))
            x_same = jnp.where(low, one_way[1], other_way[1])
            x_next = jnp.where(low, other_way[1], one_way[1])
            tables.append((one_way[0], other_way[0], x_same, x_next, one_way[2], other_way[2]))
        factors = [factor_ref[slot, :, here] for slot in range(4)]

        def coupled(slot):
            c_out, c_in, x_same, x_next, c_ahead, c_behind = tables[slot % 2]
            value = first_ref[slot, :, here]
            following = next_ref[slot, :, here]
            cut = layer_ref[slot, row, :]
            if side == OUTER:
                outward = jnp.where(first, cut, pltpu.roll(value, out_shift, 0))
                inward = pltpu.roll(jnp.where(first, following, value), in_shift, 0)
            else:
                outward = pltpu.roll(jnp.where(last, following, value), out_shift, 0)
                inward = jnp.where(last, cut, pltpu.roll(value, in_shift, 0))
            result = c_out * outward + c_in * inward
            beside = jnp.where(low, turned_ref[slot, :, left], turned_ref[slot, :, right])
            result = result + (x_same * turned_ref[slot, :, here] + x_next * beside)
            return result + (c_ahead * pltpu.roll(value, LANES - 1, 1) + c_behind * pltpu.roll(value, 1, 1))

        results = {}
        ends = []
        for sub in range(2):
            offset = 2 * steps_local * sub
            drives = [coupled(offset + slot) for slot in range(2 * steps_local)]

            def put(step, state, adjoint):
                results[sub, step] = (state, adjoint)

            values = lambda step: (drives[2 * step], drives[2 * step + 1])
            ends.append(solve_steps(values, *factors, ratio, None, None, steps_local, put))
        for step in range(steps_local):
            for field in range(2):
                slot = 2 * step + field
                early, late = [
                    first_ref[2 * steps_local * sub + slot, :, here] + results[sub, step][field] for sub in range(2)
                ]
                keep[slot, held, here] = pick(core == 0, early, late)
                send[slot, held, here] = pick(core == 0, late, early)
        for slot, value in enumerate(finish_factors(ratio, factors)):
            send[2 * steps_local + slot, held, here] = value
        (early_back, early_last), (late_back, late_last) = ends
        decay, _, _, upright = factors
        block = power(decay, steps_local)
        middle[0, held, here] = late_back
        middle[1, held, here] = early_last
        ends_ref[0, :, here] = early_back + block * late_back
        ends_ref[1, :, here] = late_last + block * (early_last + response_of(decay, upright, steps_local) * late_back)
        return carry

    lax.fori_loop(0, groups, one, 0, unroll=UNROLL_COUPLINGS)


def finish_factors(ratio, factors):
    decay, _, mixed, upright = factors
    return decay, ratio * mixed, 0.5 * upright


def carry_kernel(side, steps_local, middle, factor_ref, *rest):
    *ends, keep, send = rest
    tile, cells = keep.shape[1:]
    held = slice(side * tile, (side + 1) * tile)
    core = this_core()

    def one(here):
        factors = [factor_ref[slot, :, here] for slot in range(4)]
        decay, _, _, upright = factors
        back, state = entering(factors, ends, here, 2 * steps_local)
        block = power(decay, steps_local)
        early_back = middle[0, held, here] + block * back
        late_state = middle[1, held, here] + block * state + response_of(decay, upright, steps_local) * early_back
        for slot, (early, late) in enumerate(((early_back, back), (state, late_state))):
            keep[slot, :, here] = pick(core == 0, early, late)
            send[slot, :, here] = pick(core == 0, late, early)

    each_block(cells, 4 * LANES, one)


def finish_kernel(jobs, ratio, chips, *refs):
    state_out, adjoint_out, result, sems = refs[-4:]
    steps_local, depth, cells = state_out.shape
    tile = depth // 4
    core = this_core()
    whole = step_scale(ratio, 2 * steps_local, chips, -1)
    scales = [pick(core == 0, whole[step], whole[steps_local + step]) for step in range(steps_local)]
    copies = []
    for job, (theirs, side) in enumerate(jobs):
        parts, entered, factor_ref = refs[3 * job : 3 * job + 3]
        held = slice(side * tile, (side + 1) * tile)
        start = tile_rows(side, 2 * tile, depth)
        rows = pl.ds(pl.multiple_of(depth - tile - start if theirs else start, 8), tile)

        def one(here):
            if theirs:
                decay, gain, half_up = [parts[2 * steps_local + slot, held, here] for slot in range(3)]
            else:
                decay, gain, half_up = finish_factors(ratio, [factor_ref[slot, :, here] for slot in range(4)])
            backs = [entered[0, :, here]]
            for _ in range(steps_local):
                backs.append(decay * backs[-1])
            backs = backs[:0:-1]
            previous = entered[1, :, here]
            for step in range(steps_local):
                current = decay * previous + half_up * backs[step]
                adjoint = backs[step] - gain * previous
                result[job, 0, step, :, here] = (parts[2 * step, held, here] + current) * scales[step]
                result[job, 1, step, :, here] = (parts[2 * step + 1, held, here] + adjoint) * scales[step]
                previous = current

        for piece in range(PIECES):
            first = piece * (cells // PIECES)
            each_block(cells // PIECES, 4 * LANES, one, first)
            lanes = pl.ds(first, cells // PIECES)
            for field, out in enumerate((state_out, adjoint_out)):
                copies.append(
                    pltpu.make_async_copy(
                        result.at[job, field, :, :, lanes], out.at[:, rows, lanes], sems.at[job, field, piece]
                    )
                )
                copies[-1].start()
    for copy in copies:
        copy.wait()


def body(state_rhs, adjoint_rhs, diffusivity, velocity):
    steps_local, depth, cells = state_rhs.shape
    ranks = lax.axis_size("tm")
    slabs = lax.axis_size("gz")
    chips = ranks // 2
    total = steps_local * ranks
    steps = 2 * steps_local
    half = depth // 2
    tile = half // 2
    groups = cells // LANES
    wide = cells + 2 * LANES
    ratio = alpha_wrap ** (1.0 / total)
    core = this_core()
    f32 = jnp.float32
    anywhere = pl.BlockSpec(memory_space=pl.ANY)
    vmem = pl.BlockSpec(memory_space=pltpu.VMEM)

    def partner(value, mask):
        return lax.ppermute(value, "tm", [(i, i ^ mask) for i in range(ranks)])

    def outward(value):
        spare = (4, 2) if ranks % 8 == 0 else (0, 0)
        pairs = []
        for t in range(ranks):
            for g in range(slabs):
                to = g - 1 if t % 2 == 0 else g + 1
                other = (t ^ 1) * slabs + to if 0 <= to < slabs else (t ^ spare[t % 2]) * slabs + g
                pairs.append((t * slabs + g, other))
        return lax.ppermute(value, ("tm", "gz"), pairs)

    def onward(value):
        pairs = []
        for t in range(ranks):
            for g in range(slabs):
                to = g + 1 if t % 2 == 0 else g - 1
                other = t * slabs + to if 0 <= to < slabs else (t ^ 1) * slabs + g
                pairs.append((t * slabs + g, other))
        return lax.ppermute(value, ("tm", "gz"), pairs)

    def call(kernel, name, out_shape, *args, **kwargs):
        shapes = [jax.ShapeDtypeStruct(s, f32) for s in out_shape]
        micros = next(value for word, value in MICROSECONDS.items() if word in name)
        return pl.pallas_call(
            kernel,
            out_shape=shapes,
            compiler_params=pltpu.CompilerParams(vmem_limit_bytes=32 * 1024 * 1024),
            cost_estimate=pl.CostEstimate(flops=0, transcendentals=0, bytes_accessed=int(micros * 3.7e6)),
            name=name,
            **kwargs,
        )(*args)

    layer = (groups, LANES)
    halves = (2, steps_local, half, cells + LANES)
    keep, send, slab, edge, edge_send, layers = call(
        pack_kernel,
        "halves_and_layers",
        [halves, halves, (depth, cells), (steps + 2,) + layer, (steps,) + layer, (4,) + layer],
        *[pltpu.with_memory_space_constraint(x, pltpu.HBM) for x in (state_rhs, adjoint_rhs, diffusivity)],
        in_specs=[anywhere] * 3,
        scratch_shapes=[pltpu.SemaphoreType.DMA((5,))],
    )
    other = partner(send, 1)
    cut = outward(edge)
    cut_straight = onward(edge_send)

    def first_ends(side, *args):
        return call(
            functools.partial(ends_kernel, side, ratio, chips),
            ("outer", "inner")[side] + "_ends",
            [(2 * steps, tile, wide), (4, tile, wide), (2, tile, wide)],
            keep,
            other,
            slab,
            layers,
            *args,
        )

    inner_raw, inner_factors, inner_ends = first_ends(INNER)
    outer_raw, outer_factors, outer_ends = first_ends(OUTER, cut, cut_straight, inner_ends)

    def beside(value, masks):
        return lax.ppermute(value, "tm", [(i, i ^ masks[i % 2]) for i in range(ranks)])

    def exchange(mine, factors):
        if chips != 4:
            return [gathered(mine, factors)]
        theirs = beside(mine, (2, 4))
        (passed,) = call(functools.partial(relay_kernel, steps), "relay", [mine.shape], factors, mine, theirs)
        return [mine, theirs, beside(passed, (4, 2))]

    def gathered(mine, factors):
        width = mine.shape[2]
        every = lax.dynamic_index_in_dim(
            lax.all_gather(mine, "tm").reshape((chips, 2) + mine.shape), core, 1, keepdims=False
        )
        block, response, closing = ring_factors([factors[i, :, :width] for i in range(4)], steps, chips)
        at = lambda array, index: lax.dynamic_index_in_dim(array, lax.rem(index + 2 * chips, chips), 0, keepdims=False)
        chip = this_chip()

        def entering_back(where):
            value = jnp.zeros((tile, width), f32)
            for offset in reversed(range(chips)):
                value = block * value + at(every[:, 0], where + 1 + offset)
            return value * closing

        value = jnp.zeros((tile, width), f32)
        for offset in reversed(range(chips)):
            source = chip - 1 - offset
            value = block * value + at(every[:, 1], source) + response * entering_back(source)
        return jnp.stack([entering_back(chip), value * closing])

    def first_sweep(side, raw, factors, ends):
        return call(
            functools.partial(sweep_kernel, ratio),
            ("outer", "inner")[side] + "_first_sweep",
            [(2 * steps, tile, cells)] * 2 + [(2 * steps,) + layer],
            raw,
            factors,
            *ends,
        )

    inner_first, inner_turned, inner_layer = first_sweep(
        INNER, inner_raw, inner_factors, exchange(inner_ends, inner_factors)
    )
    outer_first, outer_turned, outer_layer = first_sweep(
        OUTER, outer_raw, outer_factors, exchange(outer_ends, outer_factors)
    )

    keep, send, middle, *ends = call(
        functools.partial(couplings_kernel, ratio),
        "couplings",
        [(steps, half, cells), (steps + 3, half, cells), (2, half, cells), (2, tile, cells), (2, tile, cells)],
        slab,
        velocity,
        cut,
        outer_first,
        outer_turned,
        outer_layer,
        outer_factors,
        inner_first,
        inner_turned,
        inner_layer,
        inner_factors,
    )
    other = partner(send, 1)
    entered = [exchange(mine, table) for mine, table in zip(ends, (outer_factors, inner_factors))]
    factors = (outer_factors, inner_factors)

    def enter(side):
        own_in, send_in = call(
            functools.partial(carry_kernel, side, steps_local),
            ("outer", "inner")[side] + "_entering",
            [(2, tile, cells)] * 2,
            middle,
            factors[side],
            *entered[side],
        )
        return own_in, partner(send_in, 1)

    own_in, other_in = zip(enter(OUTER), enter(INNER))

    def finish(results, *jobs):
        args = []
        for theirs, side in jobs:
            args += [other if theirs else keep, (other_in if theirs else own_in)[side], factors[side]]
        return call(
            functools.partial(finish_kernel, jobs, ratio, chips),
            "finish",
            [(steps_local, depth, cells)] * 2,
            *args,
            *results,
            in_specs=[vmem] * len(args) + [anywhere] * len(results),
            out_specs=[anywhere] * 2,
            scratch_shapes=[
                pltpu.VMEM((len(jobs), 2, steps_local, tile, cells), f32),
                pltpu.SemaphoreType.DMA((len(jobs), 2, PIECES)),
            ],
            input_output_aliases={len(args) + i: i for i in range(len(results))},
        )

    results = finish((), (False, OUTER), (False, INNER), (True, OUTER))
    return finish(results, (True, INNER))


def solution(mesh):
    placed = (P("tm", "gz", None), P("tm", "gz", None), P("gz", None), P(None, "gz", None))
    return jax.shard_map(
        body,
        mesh=mesh,
        in_specs=placed,
        out_specs=(P("tm", "gz", None), P("tm", "gz", None)),
        check_vma=False,
    )
```
